256 devices in a mesh: seq: 64 (over z, y, core), view: 4 (over x).
Axes of the slice: x: 4, y: 4, z: 8, core: 2. Of those that a mesh axis runs over, the one named last changes fastest.
Arguments:
- ssd_input: bfloat16 [64, 4, 512, 2048], P('seq', 'view'), may hold values from -21 to 21
- gate_input: bfloat16 [64, 4, 512, 2048], P('seq', 'view'), may hold values from -6 to 6
- b_matrix: bfloat16 [64, 4, 512, 128], P('seq', 'view'), may hold values from -6 to 6
- c_matrix: bfloat16 [64, 4, 512, 128], P('seq', 'view'), may hold values from -0.52734375 to 0.52734375
- log_decay: float32 [64, 4, 32, 512], P('seq', 'view'), may hold values from -1 to 0, as said below
- d_skip: float32 [32], replicated, may hold values from 1 to 4
- norm_gain: float32 [2048], replicated, may hold values from 0.1 to 1.9
- out_weight: bfloat16 [2048, 1536], replicated, may hold values from -0.125 to 0.125
- view_order: int32 [64, 4], P('seq'), may hold values from 0 to 3, each once within a row
- tile_order: int32 [64, 4], P('seq'), may hold values from 0 to 3, each once within a row
Outputs:
- next_tokens: bfloat16 [64, 4, 512, 1536], P('seq', 'view')
The draws below stay inside these ranges and needn't reach their ends.
Inputs may be any that keep to these rules, and one draw needn't show every extreme that they name: `log_decay`: negative everywhere. `view_order`: each row is a permutation of the views. `tile_order`: each row is a permutation of the tiles of a block.
All inputs are finite; a program needn't handle non-finite values.
Results may differ from the reference program's by a relative error of at most 0.0059.
Values may be sent and summed in bfloat16 or wider, within the bound.
No kernel may reach another device: no remote copies, remote signals or barrier semaphores. Data moves between devices by JAX's collectives and lax.ppermute only.
A program may use at most 128 MiB of HBM per device.

```python
import jax
import jax.numpy as jnp
from jax import lax

H = 32
HEAD = 64
N = 128
D_OUT = 1536
GROUP = 256
TILE = 128
TOKENS_PER_BLOCK = 512
DI = 2048
BAND_TOTAL = 64
VIEW_TOTAL = 4
PIECE = 8
TILES_DEV = 4


def draw_ssd_input(key, part):
    random_subkeys = jax.random.split(key, 3)
    channel_scale = jnp.exp(jax.random.uniform(random_subkeys[0], (H * HEAD,), jnp.float32, jnp.log(0.3), jnp.log(3.0)))
    token_scale = jnp.exp(jax.random.uniform(random_subkeys[1], (BAND_TOTAL, VIEW_TOTAL, TOKENS_PER_BLOCK, 1), jnp.float32, jnp.log(0.6), jnp.log(1.7)))
    values = jnp.clip(jax.random.normal(random_subkeys[2], (BAND_TOTAL, VIEW_TOTAL, TOKENS_PER_BLOCK, H * HEAD), jnp.float32), -4.0, 4.0)
    return (values * token_scale * channel_scale).astype(jnp.bfloat16)


def draw_log_decay(key, part):
    random_subkeys = jax.random.split(key, 7)
    sequence_length = BAND_TOTAL * VIEW_TOTAL * TOKENS_PER_BLOCK
    fast_share = 0.5
    fast_heads = jax.random.uniform(random_subkeys[0], (H,), jnp.float32) < fast_share
    slow_rate = jnp.exp(jax.random.uniform(random_subkeys[1], (H,), jnp.float32, jnp.log(0.1), jnp.log(0.5))) / sequence_length
    fast_rate = jnp.exp(jax.random.uniform(random_subkeys[2], (H,), jnp.float32, jnp.log(1.0 / 60.0), jnp.log(1.0 / 25.0)))
    head_decay_rate = jnp.where(fast_heads, fast_rate, slow_rate)
    block_multiplier = jnp.exp(jax.random.uniform(random_subkeys[3], (BAND_TOTAL, VIEW_TOTAL, 1, 1), jnp.float32, jnp.log(0.5), jnp.log(2.0)))
    token_multiplier = jnp.exp(jax.random.uniform(random_subkeys[4], (BAND_TOTAL, VIEW_TOTAL, H, TOKENS_PER_BLOCK), jnp.float32, jnp.log(0.5), jnp.log(2.0)))
    spike_positions = jax.random.randint(random_subkeys[5], (3,), 0, sequence_length)
    spike_keep_mask = jnp.log(jax.random.uniform(random_subkeys[6], (3,), jnp.float32, 0.6, 0.8))
    token_positions = jnp.arange(sequence_length, dtype=jnp.int32).reshape(BAND_TOTAL, VIEW_TOTAL, 1, TOKENS_PER_BLOCK)
    spike_log_decay = jnp.zeros((BAND_TOTAL, VIEW_TOTAL, 1, TOKENS_PER_BLOCK), jnp.float32)
    for lookup_index in range(3):
        spike_log_decay = spike_log_decay + jnp.where(token_positions == spike_positions[lookup_index], spike_keep_mask[lookup_index], 0.0)
    return -head_decay_rate[None, None, :, None] * block_multiplier * token_multiplier + spike_log_decay


def block_scale(rng, shape, shards, smallest, top_value):
    def one(axis_at, shards_of):
        steps = jax.random.uniform(jax.random.fold_in(jax.random.fold_in(rng, 6), axis_at), (shards_of,), jnp.float32, smallest / len(shards), top_value / len(shards))
        return jnp.repeat(jnp.exp(steps), shape[axis_at] // shards_of).reshape((-1,) + (1,) * (len(shape) - axis_at - 1))

    gain = one(*shards[0])
    for cut in shards[1:]:
        gain = gain * one(*cut)
    return gain


def normal_values(stream_key, dims, deviation, bound, shards=(), held_as=jnp.bfloat16):
    drawn = deviation * jax.random.normal(stream_key, dims, jnp.float32)
    if shards:
        drawn = drawn * block_scale(stream_key, dims, shards, -0.22, 0.18)
    return jnp.clip(drawn, -bound, bound).astype(held_as)


def setup_inputs(seed: int = 0) -> dict:
    key_list = jax.random.split(jax.random.key(seed), 11)
    return {
        "ssd_input": draw_ssd_input(jax.random.fold_in(key_list[10], 71), 0),
        "gate_input": normal_values(key_list[1], (BAND_TOTAL, VIEW_TOTAL, TOKENS_PER_BLOCK, DI), 1.0, 6.0, ((0, 64), (1, 4))),
        "b_matrix": normal_values(key_list[2], (BAND_TOTAL, VIEW_TOTAL, TOKENS_PER_BLOCK, N), 1.0, 6.0, ((0, 64), (1, 4))),
        "c_matrix": normal_values(key_list[3], (BAND_TOTAL, VIEW_TOTAL, TOKENS_PER_BLOCK, N), 0.088, 0.52734375, ((0, 64), (1, 4))),
        "log_decay": draw_log_decay(jax.random.fold_in(key_list[10], 71), 0),
        "d_skip": jnp.clip(jax.random.uniform(key_list[5], (H,), jnp.float32, 1.0, 4.0), 1.0, 4.0),
        "norm_gain": jnp.clip(1.0 + 0.18 * jax.random.normal(key_list[6], (DI,), jnp.float32), 0.1, 1.9),
        "out_weight": normal_values(key_list[7], (DI, D_OUT), DI ** -0.5, 0.125),
        "view_order": jax.vmap(lambda own: jax.random.permutation(own, VIEW_TOTAL))(jax.random.split(key_list[8], BAND_TOTAL)).reshape((BAND_TOTAL, VIEW_TOTAL)).astype(jnp.int32),
        "tile_order": jax.vmap(lambda own: jax.random.permutation(own, TILES_DEV))(jax.random.split(key_list[9], BAND_TOTAL)).reshape((BAND_TOTAL, TILES_DEV)).astype(jnp.int32),
    }


EPS = 1e-05

def group_parts(x_block, b_block, c_block, g_block):
    group_count = TOKENS_PER_BLOCK // GROUP
    cum_log = jnp.cumsum(g_block.reshape(H, group_count, GROUP), axis=2)
    group_end = cum_log[:, :, GROUP - 1]
    x_groups = x_block.reshape(group_count, GROUP, H, HEAD).astype(jnp.float32)
    b_groups = b_block.reshape(group_count, GROUP, N).astype(jnp.float32)
    c_groups = c_block.reshape(group_count, GROUP, N).astype(jnp.float32)
    return (cum_log, group_end, x_groups, b_groups, c_groups)

def group_states(cum_log, group_end, x_groups, b_groups):
    scaled = jnp.exp(group_end[:, :, None] - cum_log)[..., None] * b_groups[None]
    scaled = lax.optimization_barrier(scaled.astype(jnp.bfloat16)).astype(jnp.float32)
    return jnp.einsum('hckn,ckhp->hcpn', scaled, x_groups)

def summary(block):
    x_block, b_block, c_block, g_block = block
    cum_log, group_end, x_groups, b_groups, c_groups = group_parts(x_block, b_block, c_block, g_block)
    states = group_states(cum_log, group_end, x_groups, b_groups)
    group_decay = jnp.exp(group_end)
    total = jnp.ones((H,), jnp.float32)
    running = jnp.zeros((H, HEAD, N), jnp.float32)
    for lookup_index in range(TOKENS_PER_BLOCK // GROUP):
        running = group_decay[:, lookup_index, None, None] * running + states[:, lookup_index]
        total = total * group_decay[:, lookup_index]
    return (total, running)

def reference(ssd_input, gate_input, b_matrix, c_matrix, log_decay, d_skip, norm_gain, out_weight, view_order, tile_order):
    group_count = TOKENS_PER_BLOCK // GROUP
    blocks = BAND_TOTAL * VIEW_TOTAL
    x_all = ssd_input.reshape(blocks, TOKENS_PER_BLOCK, H * HEAD)
    z_all = gate_input.reshape(blocks, TOKENS_PER_BLOCK, H * HEAD)
    b_all = b_matrix.reshape(blocks, TOKENS_PER_BLOCK, N)
    c_all = c_matrix.reshape(blocks, TOKENS_PER_BLOCK, N)
    g_all = log_decay.reshape(blocks, H, TOKENS_PER_BLOCK)
    totals, states = lax.map(summary, (x_all, b_all, c_all, g_all))
    totals = totals.reshape(BAND_TOTAL, VIEW_TOTAL, H)
    states = states.reshape(BAND_TOTAL, VIEW_TOTAL, H, HEAD, N)

    def row_step(carry, row):
        row_totals, row_states, row_order = row
        entering = jnp.zeros((VIEW_TOTAL, H, HEAD, N), jnp.float32)
        for rank_pos in range(VIEW_TOTAL):
            view_now = row_order[rank_pos]
            entering = entering.at[view_now].set(carry)
            carry = jnp.take(row_totals, view_now, axis=0)[:, None, None] * carry + jnp.take(row_states, view_now, axis=0)
        return (carry, entering)
    _, entering = lax.scan(row_step, jnp.zeros((H, HEAD, N), jnp.float32), (totals, states, view_order))
    entering = entering.reshape(blocks, H, HEAD, N)
    causal = jnp.tril(jnp.ones((GROUP, GROUP), dtype=bool))

    def block_out(block):
        x_block, z_block, b_block, c_block, g_block, start = block
        cum_log, group_end, x_groups, b_groups, c_groups = group_parts(x_block, b_block, c_block, g_block)
        states_here = group_states(cum_log, group_end, x_groups, b_groups)
        group_decay = jnp.exp(group_end)
        scores = jnp.einsum('cqn,ckn->cqk', c_groups, b_groups)
        log_gaps = cum_log[:, :, :, None] - cum_log[:, :, None, :]
        weights = jnp.exp(jnp.where(causal, log_gaps, -jnp.inf)) * scores[None]
        weights = lax.optimization_barrier(weights.astype(jnp.bfloat16)).astype(jnp.float32)
        inside = jnp.einsum('hcqk,ckhp->cqhp', weights, x_groups)
        running = start
        collected = []
        for lookup_index in range(group_count):
            collected.append(running)
            running = group_decay[:, lookup_index, None, None] * running + states_here[:, lookup_index]
        entry = jnp.stack(collected, axis=1)
        entry = lax.optimization_barrier(entry.astype(jnp.bfloat16)).astype(jnp.float32)
        carried = jnp.einsum('cqn,hcpn->cqhp', c_groups, entry) * jnp.transpose(jnp.exp(cum_log), (1, 2, 0))[..., None]
        mixed = inside + carried + d_skip[None, None, :, None] * x_groups
        gate_vals = z_block.reshape(group_count, GROUP, H, HEAD).astype(jnp.float32)
        gated = mixed * jax.nn.silu(gate_vals)
        inv_rms = lax.rsqrt(lax.optimization_barrier(jnp.mean(gated * gated, axis=-1, keepdims=True)) + EPS)
        normed = (gated * inv_rms * norm_gain.reshape(H, HEAD)).astype(jnp.bfloat16).reshape(TOKENS_PER_BLOCK, H * HEAD)
        return jnp.dot(normed, out_weight, preferred_element_type=jnp.float32).astype(jnp.bfloat16)
    projected = lax.map(block_out, (x_all, z_all, b_all, c_all, g_all, entering))
    projected = projected.reshape(BAND_TOTAL, VIEW_TOTAL, BAND_TOTAL, PIECE, D_OUT)
    reordered = jnp.transpose(projected, (2, 1, 0, 3, 4)).reshape(BAND_TOTAL, VIEW_TOTAL, TILES_DEV, TILE, D_OUT)
    picked = jax.vmap(lambda band_rows, order_row: jnp.take(band_rows, order_row, axis=1))(reordered, tile_order)
    return picked.reshape(BAND_TOTAL, VIEW_TOTAL, TOKENS_PER_BLOCK, D_OUT)
```

```python
import functools

import jax
import jax.numpy as jnp
from jax import lax
from jax.experimental import pallas as pl
from jax.experimental.pallas import tpu as pltpu
from jax.sharding import Mesh
from jax.sharding import PartitionSpec as P

H = 32
HEAD = 64
N = 128
TILE = 128
TOKENS_PER_BLOCK = 512
DI = H * HEAD
CHUNK = 128
CHUNKS = TOKENS_PER_BLOCK // CHUNK
COLS = 512
EPS = 1e-05
SEQ = ("z", "y", "core")
PLANE = ("y", "core", "view")
TAIL = 16
ROWS = HEAD + TAIL
BF = jnp.bfloat16
F32 = jnp.float32
MIB = 2**20


def dot(a, b, contract=(1, 0)):
    return lax.dot_general(
        a, b, (((contract[0],), (contract[1],)), ((), ())), preferred_element_type=F32
    )


def three_terms(x):
    hi = x.astype(BF).astype(F32)
    rest = x - hi
    mid = rest.astype(BF).astype(F32)
    return hi, mid, rest - mid


def sums_over(mask, logs):
    return sum(dot(mask, part.astype(BF), (1, 1)) for part in three_terms(logs))


def halves(x):
    hi = x.astype(BF).astype(F32)
    lane = lax.broadcasted_iota(jnp.int32, x.shape, x.ndim - 1)
    return jnp.where(lane < H, hi, x - hi).astype(BF)


def spread(first_head, heads_twice=True):
    shape = (2 * H if heads_twice else H, COLS)
    head = lax.broadcasted_iota(jnp.int32, shape, 0) % H
    column = lax.broadcasted_iota(jnp.int32, shape, 1) // HEAD + first_head
    return jnp.where(head == column, 1.0, 0.0).astype(BF)


def state_kernel(order_ref, log_ref, b_ref, x_ref, out_ref, w_scr, decay_scr, bt_scr):
    step = pl.program_id(0)

    @pl.when(step == 0)
    def _():
        logs = log_ref[...]
        row = lax.broadcasted_iota(jnp.int32, (TOKENS_PER_BLOCK, TOKENS_PER_BLOCK), 0)
        column = lax.broadcasted_iota(jnp.int32, (TOKENS_PER_BLOCK, TOKENS_PER_BLOCK), 1)
        after = jnp.where(column > row, 1.0, 0.0).astype(BF)
        w_scr[...] = halves(jnp.exp(sums_over(after, jnp.concatenate([logs, logs], axis=0))))
        total = jnp.exp(jnp.sum(logs, axis=1, keepdims=True))
        decay_scr[...] = jnp.broadcast_to(total, (H, N))
        bt_scr[...] = b_ref[...].astype(F32).T.astype(BF)

    heads = COLS // HEAD
    weight = dot(w_scr[...], spread(step * heads))
    scaled = (x_ref[...].astype(F32) * weight).astype(BF)
    state = dot(bt_scr[...], scaled)
    out_ref[:, 0:HEAD, :] = state.T.astype(BF).reshape(heads, HEAD, N)
    view = lax.axis_index("view")
    rank = jnp.int32(0)
    for k in range(1, 4):
        rank = rank + jnp.where(order_ref[0, k] == view, k, 0)
    decay = decay_scr[pl.ds(pl.multiple_of(step * heads, heads), heads), :]
    hi, mid, lo = (part[:, None, :] for part in three_terms(decay))
    place = lax.broadcasted_iota(jnp.int32, (heads, TAIL, N), 1)
    tail = jnp.where(place == 0, hi, jnp.where(place == 1, mid, jnp.where(place == 2, lo, 0.0)))
    tail = jnp.where(place == 3, rank.astype(F32), tail)
    out_ref[:, HEAD:ROWS, :] = tail.astype(BF)


def block_states(order, logs, b, x):
    steps = DI // COLS
    heads = COLS // HEAD
    return pl.pallas_call(
        state_kernel,
        grid=(steps,),
        in_specs=[
            pl.BlockSpec(memory_space=pltpu.SMEM),
            pl.BlockSpec((H, TOKENS_PER_BLOCK), lambda i: (0, 0)),
            pl.BlockSpec((TOKENS_PER_BLOCK, N), lambda i: (0, 0)),
            pl.BlockSpec((TOKENS_PER_BLOCK, COLS), lambda i: (0, i)),
        ],
        out_specs=pl.BlockSpec((heads, ROWS, N), lambda i: (i, 0, 0)),
        out_shape=jax.ShapeDtypeStruct((H, ROWS, N), BF),
        scratch_shapes=[
            pltpu.VMEM((TOKENS_PER_BLOCK, 2 * H), BF),
            pltpu.VMEM((H, N), F32),
            pltpu.VMEM((N, TOKENS_PER_BLOCK), BF),
        ],
        compiler_params=pltpu.CompilerParams(vmem_limit_bytes=16 * MIB),
        cost_estimate=pl.CostEstimate(flops=2 * 10**9, bytes_accessed=3 * MIB, transcendentals=0),
        name="block_states",
    )(order, logs, b, x)


def read_tail(ref, at):
    tail = ref[at, HEAD:ROWS, :].astype(F32)
    return tail[0:1] + tail[1:2] + tail[2:3], tail[3:4]


def scan_plane(ref, running, emit):
    views = 4
    product = jnp.ones((1, N), F32)
    for band in range(ref.shape[0] // views):
        blocks = [band * views + v for v in range(views)]
        states = [ref[k, 0:HEAD, :].astype(F32) for k in blocks]
        decays, ranks = zip(*(read_tail(ref, k) for k in blocks))
        entering = [None] * views
        for place in range(views):
            chosen, decay = states[0], decays[0]
            for v in range(views):
                here = ranks[v] == float(place)
                entering[v] = running if place == 0 else jnp.where(here, running, entering[v])
                if v:
                    chosen = jnp.where(here, states[v], chosen)
                    decay = jnp.where(here, decays[v], decay)
            running = decay * running + chosen
            product = product * decay
        if emit is not None:
            for v in range(views):
                emit(blocks[v], entering[v])
    return running, product


def total_kernel(in_ref, out_ref):
    total, product = scan_plane(in_ref, jnp.zeros((HEAD, N), F32), None)
    hi, mid, lo = three_terms(product)
    place = lax.broadcasted_iota(jnp.int32, (TAIL, N), 0)
    tail = jnp.where(place == 0, hi, jnp.where(place == 1, mid, jnp.where(place == 2, lo, 0.0)))
    for k in range(out_ref.shape[0]):
        out_ref[k, 0:HEAD, :] = total.astype(BF)
        out_ref[k, HEAD:ROWS, :] = tail.astype(BF)


def plane_totals(states, planes):
    return pl.pallas_call(
        total_kernel,
        out_shape=jax.ShapeDtypeStruct((planes, ROWS, N), BF),
        compiler_params=pltpu.CompilerParams(vmem_limit_bytes=8 * MIB),
        cost_estimate=pl.CostEstimate(flops=10**6, bytes_accessed=MIB, transcendentals=0),
        name="plane_totals",
    )(states)


def entering_kernel(in_ref, totals_ref, out_ref):
    mine = lax.axis_index("z")
    carry = jnp.zeros((HEAD, N), F32)
    for k in range(totals_ref.shape[0] - 1):
        decay, _ = read_tail(totals_ref, k)
        later = decay * carry + totals_ref[k, 0:HEAD, :].astype(F32)
        carry = jnp.where(k < mine, later, carry)

    def emit(block, value):
        out_ref[block, :, :] = value.astype(BF)

    scan_plane(in_ref, carry, emit)


def entering_states(states, totals):
    return pl.pallas_call(
        entering_kernel,
        out_shape=jax.ShapeDtypeStruct((states.shape[0], HEAD, N), BF),
        compiler_params=pltpu.CompilerParams(vmem_limit_bytes=8 * MIB),
        cost_estimate=pl.CostEstimate(flops=10**6, bytes_accessed=2 * MIB, transcendentals=0),
        name="entering_states",
    )(states, totals)


def local_kernel(
    log_ref, skip_ref, b_ref, c_ref, x_ref, gate_ref, local_ref, factor_ref,
    bt_scr, left_scr, in_scr, out_scr, enter_scr, row_scr,
):
    step = pl.program_id(0)

    @pl.when(step == 0)
    def _():
        logs = log_ref[...]
        shape = (TOKENS_PER_BLOCK, TOKENS_PER_BLOCK)
        row = lax.broadcasted_iota(jnp.int32, shape, 0)
        column = lax.broadcasted_iota(jnp.int32, shape, 1)
        upto = (column <= row) & (column // CHUNK == row // CHUNK)
        sums = sums_over(
            jnp.where(upto, 1.0, 0.0).astype(BF), jnp.concatenate([logs, logs], axis=0)
        )
        before = jnp.zeros((1, 2 * H), F32)
        row_scr[...] = jnp.zeros_like(row_scr)
        causal = upto[0:CHUNK, 0:CHUNK]
        for k in range(CHUNKS):
            rows = slice(k * CHUNK, (k + 1) * CHUNK)
            part = sums[rows]
            middle = part[CHUNK // 2 - 1 : CHUNK // 2]
            end = part[CHUNK - 1 : CHUNK]
            in_scr[rows, :] = halves(jnp.exp(middle - part))
            out_scr[rows, :] = halves(jnp.exp(part - middle))
            enter_scr[rows, :] = halves(jnp.exp(before + part))
            row_scr[k : k + 1, :] = jnp.exp(end - middle)
            row_scr[4 + k : 5 + k, :] = jnp.exp(middle)
            row_scr[8 + k : 9 + k, :] = jnp.exp(end)
            before = before + end
            b_part, c_part = b_ref[rows, :], c_ref[rows, :]
            bt_scr[k] = b_part.astype(F32).T.astype(BF)
            scores = dot(c_part, b_part, (1, 1))
            left_scr[k, :, 0:CHUNK] = jnp.where(causal, scores, 0.0).astype(BF)
            left_scr[k, :, CHUNK : CHUNK + N] = c_part

    heads = COLS // HEAD
    twice = spread(step * heads)
    once = spread(step * heads, False)
    ends = dot(halves(row_scr[...]), twice)
    skip_parts = three_terms(jnp.broadcast_to(skip_ref[...], (16, H)))
    skip = sum(dot(part.astype(BF), once) for part in skip_parts)[0:1]
    running = None
    for k in range(CHUNKS):
        rows = slice(k * CHUNK, (k + 1) * CHUNK)
        x = x_ref[rows, :].astype(F32)
        scaled = (x * dot(in_scr[rows, :], twice)).astype(BF)
        if running is None:
            inner = dot(left_scr[k, :, 0:CHUNK], scaled)
        else:
            carried = (running * ends[4 + k : 5 + k]).astype(BF)
            inner = dot(left_scr[k], jnp.concatenate([scaled, carried], axis=0))
        if k + 1 < CHUNKS:
            made = dot(bt_scr[k], scaled) * ends[k : k + 1]
            running = made if running is None else running * ends[8 + k : 9 + k] + made
        gate = gate_ref[rows, :].astype(F32)
        opened = gate / (1.0 + jnp.exp(-gate))
        mixed = inner * dot(out_scr[rows, :], twice) + skip * x
        local_ref[rows, :] = mixed * opened
        factor_ref[rows, :] = dot(enter_scr[rows, :], twice) * opened


def local_part(logs, skip, b, c, x, gate):
    whole = lambda i: (0, 0)
    columns = lambda i: (0, i)
    shape = jax.ShapeDtypeStruct((TOKENS_PER_BLOCK, DI), F32)
    return pl.pallas_call(
        local_kernel,
        grid=(DI // COLS,),
        in_specs=[
            pl.BlockSpec((H, TOKENS_PER_BLOCK), whole),
            pl.BlockSpec((1, H), whole),
            pl.BlockSpec((TOKENS_PER_BLOCK, N), whole),
            pl.BlockSpec((TOKENS_PER_BLOCK, N), whole),
            pl.BlockSpec((TOKENS_PER_BLOCK, COLS), columns),
            pl.BlockSpec((TOKENS_PER_BLOCK, COLS), columns),
        ],
        out_specs=[pl.BlockSpec((TOKENS_PER_BLOCK, COLS), columns)] * 2,
        out_shape=[shape, shape],
        scratch_shapes=[
            pltpu.VMEM((CHUNKS, N, CHUNK), BF),
            pltpu.VMEM((CHUNKS, CHUNK, CHUNK + N), BF),
            pltpu.VMEM((TOKENS_PER_BLOCK, 2 * H), BF),
            pltpu.VMEM((TOKENS_PER_BLOCK, 2 * H), BF),
            pltpu.VMEM((TOKENS_PER_BLOCK, 2 * H), BF),
            pltpu.VMEM((16, 2 * H), F32),
        ],
        compiler_params=pltpu.CompilerParams(vmem_limit_bytes=24 * MIB),
        cost_estimate=pl.CostEstimate(
            flops=8 * 10**9, bytes_accessed=12 * MIB, transcendentals=2 * 10**6
        ),
        name="local_part",
    )(logs, skip, b, c, x, gate)


def output_kernel(state_ref, c_ref, local_ref, factor_ref, gain_ref, weight_ref, out_ref, normed_scr):
    width = 256
    shape = (width, width)
    same = (
        lax.broadcasted_iota(jnp.int32, shape, 0) // HEAD
        == lax.broadcasted_iota(jnp.int32, shape, 1) // HEAD
    )
    mean_of = jnp.where(same, 1.0 / HEAD, 0.0).astype(BF)
    c = c_ref[...]
    for k in range(DI // width):
        columns = slice(k * width, (k + 1) * width)
        carried = dot(c, state_ref[columns, :], (1, 1))
        gated = local_ref[:, columns] + factor_ref[:, columns] * carried
        square = gated * gated
        hi = square.astype(BF)
        mean = dot(hi, mean_of) + dot((square - hi.astype(F32)).astype(BF), mean_of)
        normed = gated * lax.rsqrt(mean + EPS) * gain_ref[:, columns]
        normed_scr[:, columns] = normed.astype(BF)
    out_ref[...] = dot(normed_scr[...], weight_ref[...]).astype(BF)


def projected_tokens(state, c, local, factor, gain, weight):
    rows = 128
    width_out = weight.shape[1]
    whole = lambda i: (0, 0)
    block = lambda i: (i, 0)
    return pl.pallas_call(
        output_kernel,
        grid=(TOKENS_PER_BLOCK // rows,),
        in_specs=[
            pl.BlockSpec((DI, N), whole),
            pl.BlockSpec((rows, N), block),
            pl.BlockSpec((rows, DI), block),
            pl.BlockSpec((rows, DI), block),
            pl.BlockSpec((1, DI), whole),
            pl.BlockSpec((DI, width_out), whole),
        ],
        out_specs=pl.BlockSpec((rows, width_out), block),
        out_shape=jax.ShapeDtypeStruct((TOKENS_PER_BLOCK, width_out), BF),
        scratch_shapes=[pltpu.VMEM((rows, DI), BF)],
        compiler_params=pltpu.CompilerParams(vmem_limit_bytes=32 * MIB),
        cost_estimate=pl.CostEstimate(
            flops=4 * 10**9, bytes_accessed=16 * MIB, transcendentals=10**6
        ),
        name="projected_tokens",
    )(state, c, local, factor, gain, weight)


def tile_kernel(order_ref, in_ref, out_ref, sems):
    tiles = TOKENS_PER_BLOCK // TILE
    copies = [
        pltpu.make_async_copy(
            in_ref.at[pl.ds(pl.multiple_of(order_ref[0, k] * TILE, TILE), TILE), :],
            out_ref.at[pl.ds(k * TILE, TILE), :],
            sems.at[k],
        )
        for k in range(tiles)
    ]
    for copy in copies:
        copy.start()
    for copy in copies:
        copy.wait()


def chosen_tiles(order, arrived):
    return pl.pallas_call(
        tile_kernel,
        in_specs=[pl.BlockSpec(memory_space=pltpu.SMEM), pl.BlockSpec(memory_space=pl.ANY)],
        out_specs=pl.BlockSpec(memory_space=pl.ANY),
        out_shape=jax.ShapeDtypeStruct(arrived.shape, arrived.dtype),
        scratch_shapes=[pltpu.SemaphoreType.DMA((TOKENS_PER_BLOCK // TILE,))],
        compiler_params=pltpu.CompilerParams(vmem_limit_bytes=MIB),
        cost_estimate=pl.CostEstimate(flops=0, bytes_accessed=3 * MIB, transcendentals=0),
        name="chosen_tiles",
    )(order, arrived)


def swapped(x, axes):
    return lax.all_to_all(x, axes, split_axis=0, concat_axis=0, tiled=True)


def shards(
    ssd_input,
    gate_input,
    b_matrix,
    c_matrix,
    log_decay,
    d_skip,
    norm_gain,
    out_weight,
    view_order,
    tile_order,
):
    bands = lax.axis_size(SEQ)
    width_out = out_weight.shape[1]
    x, gate, b, c = (part[0, 0] for part in (ssd_input, gate_input, b_matrix, c_matrix))
    logs = log_decay[0, 0]
    states = swapped(block_states(view_order, logs, b, x), PLANE)
    local, factor = local_part(logs, d_skip.reshape(1, H), b, c, x, gate)
    totals = swapped(plane_totals(states, lax.axis_size("z")), "z")
    entering = swapped(entering_states(states, totals), PLANE).reshape(DI, N)
    projected = projected_tokens(
        entering, c, local, factor, norm_gain.reshape(1, DI), out_weight
    )
    arrived = swapped(projected.reshape(bands, TOKENS_PER_BLOCK // bands, width_out), SEQ)
    chosen = chosen_tiles(tile_order, arrived.reshape(TOKENS_PER_BLOCK, width_out))
    return chosen.reshape(1, 1, TOKENS_PER_BLOCK, width_out)


def solution(mesh):
    split = Mesh(mesh.devices.reshape(8, 4, 2, mesh.shape["view"]), (*SEQ, "view"))
    whole = P(SEQ, "view", None, None)
    in_specs = (whole,) * 5 + (P(),) * 3 + (P(SEQ, None),) * 2
    return jax.shard_map(shards, mesh=split, in_specs=in_specs, out_specs=whole, check_vma=False)
```

```python
import functools

import jax
import jax.numpy as jnp
from jax import lax
from jax.experimental import pallas as pl
from jax.experimental.pallas import tpu as pltpu
from jax.sharding import Mesh
from jax.sharding import PartitionSpec as P

H = 32
HEAD = 64
N = 128
TILE = 128
TOKENS_PER_BLOCK = 512
DI = H * HEAD
CHUNK = 128
CHUNKS = TOKENS_PER_BLOCK // CHUNK
COLS = 512
EPS = 1e-05
SEQ = ("z", "y", "core")
PLANE = ("y", "core", "view")
TAIL = 16
PIECES = 4
ROWS = HEAD + TAIL
BF = jnp.bfloat16
F32 = jnp.float32
MIB = 2**20


def dot(a, b, contract=(1, 0)):
    return lax.dot_general(
        a, b, (((contract[0],), (contract[1],)), ((), ())), preferred_element_type=F32
    )


def three_terms(x):
    hi = x.astype(BF).astype(F32)
    rest = x - hi
    mid = rest.astype(BF).astype(F32)
    return hi, mid, rest - mid


def chunk_sums(logs):
    shape = (CHUNK, CHUNK)
    row = lax.broadcasted_iota(jnp.int32, shape, 0)
    column = lax.broadcasted_iota(jnp.int32, shape, 1)
    upto = jnp.where(column <= row, 1.0, 0.0).astype(BF)
    parts = [part.astype(BF) for part in three_terms(logs)]
    return [
        sum(dot(upto, part[:, k * CHUNK : (k + 1) * CHUNK], (1, 1)) for part in parts)
        for k in range(CHUNKS)
    ]


def halves(x):
    hi = x.astype(BF).astype(F32)
    lane = lax.broadcasted_iota(jnp.int32, x.shape, x.ndim - 1)
    return jnp.where(lane < H, hi, x - hi).astype(BF)


def in_hbm(x):
    return pltpu.with_memory_space_constraint(x, pltpu.HBM)


def spread(first_head, heads_twice=True):
    shape = (2 * H if heads_twice else H, COLS)
    head = lax.broadcasted_iota(jnp.int32, shape, 0) % H
    column = lax.broadcasted_iota(jnp.int32, shape, 1) // HEAD + first_head
    return jnp.where(head == column, 1.0, 0.0).astype(BF)


def state_kernel(order_ref, log_ref, b_ref, x_ref, out_ref, w_scr, decay_scr, bt_scr):
    step = pl.program_id(0)

    @pl.when(step == 0)
    def _():
        logs = log_ref[...]
        sums = chunk_sums(jnp.concatenate([logs, logs], axis=0))
        later = jnp.zeros((1, 2 * H), F32)
        for k in reversed(range(CHUNKS)):
            end = sums[k][CHUNK - 1 : CHUNK]
            w_scr[k * CHUNK : (k + 1) * CHUNK, :] = halves(jnp.exp(end - sums[k] + later))
            later = later + end
        total = jnp.exp(jnp.sum(logs, axis=1, keepdims=True))
        decay_scr[...] = jnp.broadcast_to(total, (H, N))
        bt_scr[...] = b_ref[...].astype(F32).T.astype(BF)

    heads = COLS // HEAD
    weight = dot(w_scr[...], spread(step * heads))
    scaled = (x_ref[...].astype(F32) * weight).astype(BF)
    state = dot(bt_scr[...], scaled)
    out_ref[:, 0:HEAD, :] = state.T.astype(BF).reshape(heads, HEAD, N)
    view = lax.axis_index("view")
    rank = jnp.int32(0)
    for k in range(1, 4):
        rank = rank + jnp.where(order_ref[0, k] == view, k, 0)
    decay = decay_scr[pl.ds(pl.multiple_of(step * heads, heads), heads), :]
    hi, mid, lo = (part[:, None, :] for part in three_terms(decay))
    place = lax.broadcasted_iota(jnp.int32, (heads, TAIL, N), 1)
    tail = jnp.where(place == 0, hi, jnp.where(place == 1, mid, jnp.where(place == 2, lo, 0.0)))
    tail = jnp.where(place == 3, rank.astype(F32), tail)
    out_ref[:, HEAD:ROWS, :] = tail.astype(BF)


def block_states(order, logs, b, x):
    steps = DI // COLS
    heads = COLS // HEAD
    return pl.pallas_call(
        state_kernel,
        grid=(steps,),
        in_specs=[
            pl.BlockSpec(memory_space=pltpu.SMEM),
            pl.BlockSpec((H, TOKENS_PER_BLOCK), lambda i: (0, 0)),
            pl.BlockSpec((TOKENS_PER_BLOCK, N), lambda i: (0, 0)),
            pl.BlockSpec((TOKENS_PER_BLOCK, COLS), lambda i: (0, i)),
        ],
        out_specs=pl.BlockSpec((heads, ROWS, N), lambda i: (i, 0, 0)),
        out_shape=jax.ShapeDtypeStruct((H, ROWS, N), BF),
        scratch_shapes=[
            pltpu.VMEM((TOKENS_PER_BLOCK, 2 * H), BF),
            pltpu.VMEM((H, N), F32),
            pltpu.VMEM((N, TOKENS_PER_BLOCK), BF),
        ],
        compiler_params=pltpu.CompilerParams(vmem_limit_bytes=16 * MIB),
        cost_estimate=pl.CostEstimate(flops=2 * 10**9, bytes_accessed=3 * MIB, transcendentals=0),
        name="block_states",
    )(*(in_hbm(part) for part in (order, logs, b, x)))


def read_tail(ref, at):
    tail = ref[at, HEAD:ROWS, :].astype(F32)
    return tail[0:1] + tail[1:2] + tail[2:3], tail[3:4]


def scan_plane(ref, running, emit):
    views = 4
    product = jnp.ones((1, N), F32)
    for band in range(ref.shape[0] // views):
        blocks = [band * views + v for v in range(views)]
        states = [ref[k, 0:HEAD, :].astype(F32) for k in blocks]
        decays, ranks = zip(*(read_tail(ref, k) for k in blocks))
        entering = [None] * views
        for place in range(views):
            chosen, decay = states[0], decays[0]
            for v in range(views):
                here = ranks[v] == float(place)
                entering[v] = running if place == 0 else jnp.where(here, running, entering[v])
                if v:
                    chosen = jnp.where(here, states[v], chosen)
                    decay = jnp.where(here, decays[v], decay)
            running = decay * running + chosen
            product = product * decay
        if emit is not None:
            for v in range(views):
                emit(blocks[v], entering[v])
    return running, product


def total_kernel(in_ref, token_ref, out_ref):
    total, product = scan_plane(in_ref, jnp.zeros((HEAD, N), F32), None)
    hi, mid, lo = three_terms(product)
    place = lax.broadcasted_iota(jnp.int32, (TAIL, N), 0)
    tail = jnp.where(place == 0, hi, jnp.where(place == 1, mid, jnp.where(place == 2, lo, 0.0)))
    for k in range(out_ref.shape[0]):
        out_ref[k, 0:HEAD, :] = total.astype(BF)
        out_ref[k, HEAD:ROWS, :] = tail.astype(BF)


def plane_totals(states, token, planes):
    return pl.pallas_call(
        total_kernel,
        in_specs=[pl.BlockSpec(memory_space=pltpu.VMEM), pl.BlockSpec(memory_space=pl.ANY)],
        out_shape=jax.ShapeDtypeStruct((planes, ROWS, N), BF),
        compiler_params=pltpu.CompilerParams(vmem_limit_bytes=8 * MIB),
        cost_estimate=pl.CostEstimate(flops=10**6, bytes_accessed=MIB, transcendentals=0),
        name="plane_totals",
    )(states, token)


def entering_kernel(in_ref, totals_ref, out_ref):
    mine = lax.axis_index("z")
    carry = jnp.zeros((HEAD, N), F32)
    for k in range(totals_ref.shape[0] - 1):
        decay, _ = read_tail(totals_ref, k)
        later = decay * carry + totals_ref[k, 0:HEAD, :].astype(F32)
        carry = jnp.where(k < mine, later, carry)

    def emit(block, value):
        out_ref[block, :, :] = value.astype(BF)

    scan_plane(in_ref, carry, emit)


def entering_states(states, totals):
    return pl.pallas_call(
        entering_kernel,
        out_shape=jax.ShapeDtypeStruct((states.shape[0], HEAD, N), BF),
        compiler_params=pltpu.CompilerParams(vmem_limit_bytes=8 * MIB),
        cost_estimate=pl.CostEstimate(flops=10**6, bytes_accessed=2 * MIB, transcendentals=0),
        name="entering_states",
    )(states, totals)


def local_kernel(
    log_ref, skip_ref, b_ref, c_ref, x_ref, gate_ref, local_ref, factor_ref, token_ref,
    bt_scr, left_scr, in_scr, out_scr, enter_scr, row_scr,
):
    step = pl.program_id(0)

    @pl.when(step == 0)
    def _():
        token_ref[...] = jnp.zeros_like(token_ref)
        logs = log_ref[...]
        sums = chunk_sums(jnp.concatenate([logs, logs], axis=0))
        before = jnp.zeros((1, 2 * H), F32)
        row_scr[...] = jnp.zeros_like(row_scr)
        shape = (CHUNK, CHUNK)
        causal = lax.broadcasted_iota(jnp.int32, shape, 1) <= lax.broadcasted_iota(
            jnp.int32, shape, 0
        )
        for k in range(CHUNKS):
            rows = slice(k * CHUNK, (k + 1) * CHUNK)
            part = sums[k]
            middle = part[CHUNK // 2 - 1 : CHUNK // 2]
            end = part[CHUNK - 1 : CHUNK]
            in_scr[rows, :] = halves(jnp.exp(middle - part))
            out_scr[rows, :] = halves(jnp.exp(part - middle))
            enter_scr[rows, :] = halves(jnp.exp(before + part))
            row_scr[k : k + 1, :] = jnp.exp(end - middle)
            row_scr[4 + k : 5 + k, :] = jnp.exp(middle)
            row_scr[8 + k : 9 + k, :] = jnp.exp(end)
            before = before + end
            b_part, c_part = b_ref[rows, :], c_ref[rows, :]
            bt_scr[k] = b_part.astype(F32).T.astype(BF)
            scores = jnp.where(causal, dot(c_part, b_part, (1, 1)), 0.0)
            hi = scores.astype(BF)
            left_scr[k, :, 0:CHUNK] = hi
            left_scr[k, :, CHUNK : 2 * CHUNK] = hi
            left_scr[k, :, 2 * CHUNK : 3 * CHUNK] = (scores - hi.astype(F32)).astype(BF)
            left_scr[k, :, 3 * CHUNK : 3 * CHUNK + N] = c_part

    heads = COLS // HEAD
    twice = spread(step * heads)
    once = spread(step * heads, False)
    ends = dot(halves(row_scr[...]), twice)
    skip_parts = three_terms(jnp.broadcast_to(skip_ref[...], (16, H)))
    skip = sum(dot(part.astype(BF), once) for part in skip_parts)[0:1]
    running = None
    for k in range(CHUNKS):
        rows = slice(k * CHUNK, (k + 1) * CHUNK)
        x = x_ref[rows, :].astype(F32)
        exact = x * dot(in_scr[rows, :], twice)
        scaled = exact.astype(BF)
        right = [scaled, (exact - scaled.astype(F32)).astype(BF), scaled]
        if running is not None:
            right.append((running * ends[4 + k : 5 + k]).astype(BF))
        inner = dot(left_scr[k, :, 0 : CHUNK * len(right)], jnp.concatenate(right, axis=0))
        if k + 1 < CHUNKS:
            made = dot(bt_scr[k], scaled) * ends[k : k + 1]
            running = made if running is None else running * ends[8 + k : 9 + k] + made
        gate = gate_ref[rows, :].astype(F32)
        opened = gate / (1.0 + jnp.exp(-gate))
        mixed = inner * dot(out_scr[rows, :], twice) + skip * x
        local_ref[rows, :] = (mixed * opened).astype(BF)
        factor_ref[rows, :] = dot(enter_scr[rows, :], twice) * opened


def local_part(logs, skip, b, c, x, gate):
    whole = lambda i: (0, 0)
    columns = lambda i: (0, i)
    wide = (TOKENS_PER_BLOCK, DI)
    return pl.pallas_call(
        local_kernel,
        grid=(DI // COLS,),
        in_specs=[
            pl.BlockSpec((H, TOKENS_PER_BLOCK), whole),
            pl.BlockSpec((1, H), whole),
            pl.BlockSpec((TOKENS_PER_BLOCK, N), whole),
            pl.BlockSpec((TOKENS_PER_BLOCK, N), whole),
            pl.BlockSpec((TOKENS_PER_BLOCK, COLS), columns),
            pl.BlockSpec((TOKENS_PER_BLOCK, COLS), columns),
        ],
        out_specs=[
            pl.BlockSpec((TOKENS_PER_BLOCK, COLS), columns),
            pl.BlockSpec((TOKENS_PER_BLOCK, COLS), columns),
            pl.BlockSpec((8, N), whole),
        ],
        out_shape=[
            pltpu.HBM(wide, BF),
            pltpu.HBM(wide, F32),
            jax.ShapeDtypeStruct((8, N), F32),
        ],
        scratch_shapes=[
            pltpu.VMEM((CHUNKS, N, CHUNK), BF),
            pltpu.VMEM((CHUNKS, CHUNK, 3 * CHUNK + N), BF),
            pltpu.VMEM((TOKENS_PER_BLOCK, 2 * H), BF),
            pltpu.VMEM((TOKENS_PER_BLOCK, 2 * H), BF),
            pltpu.VMEM((TOKENS_PER_BLOCK, 2 * H), BF),
            pltpu.VMEM((16, 2 * H), F32),
        ],
        compiler_params=pltpu.CompilerParams(vmem_limit_bytes=16 * MIB),
        cost_estimate=pl.CostEstimate(
            flops=8 * 10**9, bytes_accessed=12 * MIB, transcendentals=2 * 10**6
        ),
        name="local_part",
    )(*(in_hbm(part) for part in (logs, skip, b, c, x, gate)))


def output_kernel(
    state_ref, c_ref, gain_ref, local_hbm, factor_hbm, weight_hbm, out_ref,
    local_ref, factor_ref, weight_ref, normed_scr, row_sems, weight_sems,
):
    width = 256
    shape = (width, width)
    same = (
        lax.broadcasted_iota(jnp.int32, shape, 0) // HEAD
        == lax.broadcasted_iota(jnp.int32, shape, 1) // HEAD
    )
    mean_of = jnp.where(same, 1.0 / HEAD, 0.0).astype(BF)

    def row_copies(k):
        rows = pl.ds(pl.multiple_of(k * CHUNK, CHUNK), CHUNK)
        return (
            pltpu.make_async_copy(local_hbm.at[rows, :], local_ref.at[rows, :], row_sems.at[0, k]),
            pltpu.make_async_copy(factor_hbm.at[rows, :], factor_ref.at[rows, :], row_sems.at[1, k]),
        )

    def weight_copy(j):
        columns = pl.ds(j * width, width)
        return pltpu.make_async_copy(
            weight_hbm.at[:, columns], weight_ref.at[:, columns], weight_sems.at[j]
        )

    pieces = out_ref.shape[1] // width
    for k in range(CHUNKS):
        for copy in row_copies(k):
            copy.start()

    def norm_rows(k, carry):
        for copy in row_copies(k):
            copy.wait()

        @pl.when(k == 0)
        def _():
            for j in range(pieces):
                weight_copy(j).start()

        rows = pl.ds(pl.multiple_of(k * CHUNK, CHUNK), CHUNK)
        c = c_ref[rows, :]
        for j in range(DI // width):
            columns = slice(j * width, (j + 1) * width)
            carried = dot(c, state_ref[columns, :], (1, 1))
            gated = local_ref[rows, columns].astype(F32) + factor_ref[rows, columns] * carried
            mean = dot((gated * gated).astype(BF), mean_of)
            normed = gated * (lax.rsqrt(mean + EPS) * gain_ref[:, columns])
            normed_scr[rows, columns] = normed.astype(BF)
        return carry

    lax.fori_loop(0, CHUNKS, norm_rows, 0)
    for j in range(pieces):
        weight_copy(j).wait()
        columns = slice(j * width, (j + 1) * width)
        out_ref[:, columns] = dot(normed_scr[...], weight_ref[:, columns]).astype(BF)


def projected_tokens(state, c, local, factor, gain, weight):
    width_out = weight.shape[1]
    vmem, anywhere = pl.BlockSpec(memory_space=pltpu.VMEM), pl.BlockSpec(memory_space=pl.ANY)
    return pl.pallas_call(
        output_kernel,
        in_specs=[vmem, vmem, vmem, anywhere, anywhere, anywhere],
        out_specs=vmem,
        out_shape=jax.ShapeDtypeStruct((TOKENS_PER_BLOCK, width_out), BF),
        scratch_shapes=[
            pltpu.VMEM((TOKENS_PER_BLOCK, DI), BF),
            pltpu.VMEM((TOKENS_PER_BLOCK, DI), F32),
            pltpu.VMEM(weight.shape, BF),
            pltpu.VMEM((TOKENS_PER_BLOCK, DI), BF),
            pltpu.SemaphoreType.DMA((2, CHUNKS)),
            pltpu.SemaphoreType.DMA((width_out // 256,)),
        ],
        compiler_params=pltpu.CompilerParams(vmem_limit_bytes=28 * MIB),
        cost_estimate=pl.CostEstimate(
            flops=4 * 10**9, bytes_accessed=16 * MIB, transcendentals=10**6
        ),
        name="projected_tokens",
    )(state, c, gain, in_hbm(local), in_hbm(factor), in_hbm(weight))


def tile_kernel(order_ref, in_ref, out_ref, sems):
    piece = TILE // PIECES
    copies = []
    for k in range(TOKENS_PER_BLOCK // TILE):
        first = pl.multiple_of(order_ref[0, k] * TILE, TILE)
        for i in range(PIECES):
            source = in_ref.at[pl.ds(first + i * piece, piece), :]
            target = out_ref.at[pl.ds(k * TILE + i * piece, piece), :]
            copies.append(pltpu.make_async_copy(source, target, sems.at[k * PIECES + i]))
    for copy in copies:
        copy.start()
    for copy in copies:
        copy.wait()


def chosen_tiles(order, arrived):
    return pl.pallas_call(
        tile_kernel,
        in_specs=[pl.BlockSpec(memory_space=pltpu.SMEM), pl.BlockSpec(memory_space=pl.ANY)],
        out_specs=pl.BlockSpec(memory_space=pl.ANY),
        out_shape=jax.ShapeDtypeStruct(arrived.shape, arrived.dtype),
        scratch_shapes=[pltpu.SemaphoreType.DMA((PIECES * TOKENS_PER_BLOCK // TILE,))],
        compiler_params=pltpu.CompilerParams(vmem_limit_bytes=MIB),
        cost_estimate=pl.CostEstimate(flops=0, bytes_accessed=3 * MIB, transcendentals=0),
        name="chosen_tiles",
    )(order, arrived)


def swapped(x, axes):
    return lax.all_to_all(x, axes, split_axis=0, concat_axis=0, tiled=True)


def shards(
    ssd_input,
    gate_input,
    b_matrix,
    c_matrix,
    log_decay,
    d_skip,
    norm_gain,
    out_weight,
    view_order,
    tile_order,
):
    bands = lax.axis_size(SEQ)
    width_out = out_weight.shape[1]
    x, gate, b, c = (part[0, 0] for part in (ssd_input, gate_input, b_matrix, c_matrix))
    logs = log_decay[0, 0]
    states = swapped(block_states(view_order, logs, b, x), PLANE)
    local, factor, token = local_part(logs, d_skip.reshape(1, H), b, c, x, gate)
    totals = swapped(plane_totals(states, token, lax.axis_size("z")), "z")
    entering = swapped(entering_states(states, totals), PLANE).reshape(DI, N)
    projected = projected_tokens(
        entering, c, local, factor, norm_gain.reshape(1, DI), out_weight
    )
    arrived = swapped(projected.reshape(bands, TOKENS_PER_BLOCK // bands, width_out), SEQ)
    chosen = chosen_tiles(tile_order, arrived.reshape(TOKENS_PER_BLOCK, width_out))
    return chosen.reshape(1, 1, TOKENS_PER_BLOCK, width_out)


def solution(mesh):
    split = Mesh(mesh.devices.reshape(8, 4, 2, mesh.shape["view"]), (*SEQ, "view"))
    whole = P(SEQ, "view", None, None)
    in_specs = (whole,) * 5 + (P(),) * 3 + (P(SEQ, None),) * 2
    return jax.shard_map(shards, mesh=split, in_specs=in_specs, out_specs=whole, check_vma=False)
```

```python
import functools

import jax
import jax.numpy as jnp
from jax import lax
from jax.experimental import pallas as pl
from jax.experimental.pallas import tpu as pltpu
from jax.sharding import Mesh
from jax.sharding import PartitionSpec as P

H = 32
HEAD = 64
N = 128
TILE = 128
TOKENS_PER_BLOCK = 512
DI = H * HEAD
CHUNK = 128
CHUNKS = TOKENS_PER_BLOCK // CHUNK
COLS = 512
EPS = 1e-05
SEQ = ("z", "y", "core")
PLANE = ("y", "core", "view")
TAIL = 16
PIECES = 4
HELD = 512
SHARES = 2
ROWS = HEAD + TAIL
BF = jnp.bfloat16
F32 = jnp.float32
MIB = 2**20


def dot(a, b, contract=(1, 0)):
    return lax.dot_general(
        a, b, (((contract[0],), (contract[1],)), ((), ())), preferred_element_type=F32
    )


def three_terms(x):
    hi = x.astype(BF).astype(F32)
    rest = x - hi
    mid = rest.astype(BF).astype(F32)
    return hi, mid, rest - mid


def chunk_sums(logs):
    shape = (CHUNK, CHUNK)
    row = lax.broadcasted_iota(jnp.int32, shape, 0)
    column = lax.broadcasted_iota(jnp.int32, shape, 1)
    upto = jnp.where(column <= row, 1.0, 0.0).astype(BF)
    parts = [part.astype(BF) for part in three_terms(logs)]
    return [
        sum(dot(upto, part[:, k * CHUNK : (k + 1) * CHUNK], (1, 1)) for part in parts)
        for k in range(CHUNKS)
    ]


def halves(x):
    hi = x.astype(BF).astype(F32)
    lane = lax.broadcasted_iota(jnp.int32, x.shape, x.ndim - 1)
    return jnp.where(lane < H, hi, x - hi).astype(BF)


def in_hbm(x):
    return pltpu.with_memory_space_constraint(x, pltpu.HBM)


def spread(first_head, heads_twice=True):
    shape = (2 * H if heads_twice else H, COLS)
    head = lax.broadcasted_iota(jnp.int32, shape, 0) % H
    column = lax.broadcasted_iota(jnp.int32, shape, 1) // HEAD + first_head
    return jnp.where(head == column, 1.0, 0.0).astype(BF)


def state_kernel(order_ref, log_ref, b_ref, x_ref, out_ref, w_scr, decay_scr, bt_scr):
    step = pl.program_id(0)

    @pl.when(step == 0)
    def _():
        logs = log_ref[...]
        sums = chunk_sums(jnp.concatenate([logs, logs], axis=0))
        later = jnp.zeros((1, 2 * H), F32)
        for k in reversed(range(CHUNKS)):
            end = sums[k][CHUNK - 1 : CHUNK]
            w_scr[k * CHUNK : (k + 1) * CHUNK, :] = halves(jnp.exp(end - sums[k] + later))
            later = later + end
        total = jnp.exp(jnp.sum(logs, axis=1, keepdims=True))
        decay_scr[...] = jnp.broadcast_to(total, (H, N))
        bt_scr[...] = b_ref[...].astype(F32).T.astype(BF)

    heads = COLS // HEAD
    weight = dot(w_scr[...], spread(step * heads))
    scaled = (x_ref[...].astype(F32) * weight).astype(BF)
    state = dot(bt_scr[...], scaled)
    out_ref[:, 0:HEAD, :] = state.T.astype(BF).reshape(heads, HEAD, N)
    view = lax.axis_index("view")
    rank = jnp.int32(0)
    for k in range(1, 4):
        rank = rank + jnp.where(order_ref[0, k] == view, k, 0)
    decay = decay_scr[pl.ds(pl.multiple_of(step * heads, heads), heads), :]
    hi, mid, lo = (part[:, None, :] for part in three_terms(decay))
    place = lax.broadcasted_iota(jnp.int32, (heads, TAIL, N), 1)
    tail = jnp.where(place == 0, hi, jnp.where(place == 1, mid, jnp.where(place == 2, lo, 0.0)))
    tail = jnp.where(place == 3, rank.astype(F32), tail)
    out_ref[:, HEAD:ROWS, :] = tail.astype(BF)


def block_states(order, logs, b, x):
    steps = DI // COLS
    heads = COLS // HEAD
    return pl.pallas_call(
        state_kernel,
        grid=(steps,),
        in_specs=[
            pl.BlockSpec(memory_space=pltpu.SMEM),
            pl.BlockSpec((H, TOKENS_PER_BLOCK), lambda i: (0, 0)),
            pl.BlockSpec((TOKENS_PER_BLOCK, N), lambda i: (0, 0)),
            pl.BlockSpec((TOKENS_PER_BLOCK, COLS), lambda i: (0, i)),
        ],
        out_specs=pl.BlockSpec((heads, ROWS, N), lambda i: (i, 0, 0)),
        out_shape=jax.ShapeDtypeStruct((H, ROWS, N), BF),
        scratch_shapes=[
            pltpu.VMEM((TOKENS_PER_BLOCK, 2 * H), BF),
            pltpu.VMEM((H, N), F32),
            pltpu.VMEM((N, TOKENS_PER_BLOCK), BF),
        ],
        compiler_params=pltpu.CompilerParams(vmem_limit_bytes=16 * MIB),
        cost_estimate=pl.CostEstimate(flops=2 * 10**9, bytes_accessed=3 * MIB, transcendentals=0),
        name="block_states",
    )(*(in_hbm(part) for part in (order, logs, b, x)))


def read_tail(ref, at):
    tail = ref[at, HEAD:ROWS, :].astype(F32)
    return tail[0:1] + tail[1:2] + tail[2:3], tail[3:4]


def scan_plane(ref, running, emit):
    views = 4
    product = jnp.ones((1, N), F32)
    for band in range(ref.shape[0] // views):
        blocks = [band * views + v for v in range(views)]
        states = [ref[k, 0:HEAD, :].astype(F32) for k in blocks]
        decays, ranks = zip(*(read_tail(ref, k) for k in blocks))
        entering = [None] * views
        for place in range(views):
            chosen, decay = states[0], decays[0]
            for v in range(views):
                here = ranks[v] == float(place)
                entering[v] = running if place == 0 else jnp.where(here, running, entering[v])
                if v:
                    chosen = jnp.where(here, states[v], chosen)
                    decay = jnp.where(here, decays[v], decay)
            running = decay * running + chosen
            product = product * decay
        if emit is not None:
            for v in range(views):
                emit(blocks[v], entering[v])
    return running, product


def total_kernel(in_ref, token_ref, out_ref):
    total, product = scan_plane(in_ref, jnp.zeros((HEAD, N), F32), None)
    hi, mid, lo = three_terms(product)
    place = lax.broadcasted_iota(jnp.int32, (TAIL, N), 0)
    tail = jnp.where(place == 0, hi, jnp.where(place == 1, mid, jnp.where(place == 2, lo, 0.0)))
    for k in range(out_ref.shape[0]):
        out_ref[k, 0:HEAD, :] = total.astype(BF)
        out_ref[k, HEAD:ROWS, :] = tail.astype(BF)


def plane_totals(states, token, planes):
    return pl.pallas_call(
        total_kernel,
        in_specs=[pl.BlockSpec(memory_space=pltpu.VMEM), pl.BlockSpec(memory_space=pl.ANY)],
        out_shape=jax.ShapeDtypeStruct((planes, ROWS, N), BF),
        compiler_params=pltpu.CompilerParams(vmem_limit_bytes=8 * MIB),
        cost_estimate=pl.CostEstimate(flops=10**6, bytes_accessed=MIB, transcendentals=0),
        name="plane_totals",
    )(states, in_hbm(token))


def entering_kernel(in_ref, totals_ref, out_ref):
    mine = lax.axis_index("z")
    carry = jnp.zeros((HEAD, N), F32)
    for k in range(totals_ref.shape[0] - 1):
        decay, _ = read_tail(totals_ref, k)
        later = decay * carry + totals_ref[k, 0:HEAD, :].astype(F32)
        carry = jnp.where(k < mine, later, carry)

    def emit(block, value):
        out_ref[block, :, :] = value.astype(BF)

    scan_plane(in_ref, carry, emit)


def entering_states(states, totals):
    return pl.pallas_call(
        entering_kernel,
        out_shape=jax.ShapeDtypeStruct((states.shape[0], HEAD, N), BF),
        compiler_params=pltpu.CompilerParams(vmem_limit_bytes=8 * MIB),
        cost_estimate=pl.CostEstimate(flops=10**6, bytes_accessed=2 * MIB, transcendentals=0),
        name="entering_states",
    )(states, totals)


def local_kernel(
    first_head, after_ref, log_ref, skip_ref, b_ref, c_ref, x_ref, gate_ref, weight_ref,
    local_ref, factor_ref, held_ref,
    bt_scr, left_scr, in_scr, out_scr, enter_scr, row_scr, sem,
):
    step = pl.program_id(0)
    columns = pl.ds(first_head * HEAD * HELD // DI, held_ref.shape[1])
    held = pltpu.make_async_copy(weight_ref.at[:, columns], held_ref, sem)

    @pl.when(step == 0)
    def _():
        held.start()
        logs = log_ref[...]
        sums = chunk_sums(jnp.concatenate([logs, logs], axis=0))
        before = jnp.zeros((1, 2 * H), F32)
        row_scr[...] = jnp.zeros_like(row_scr)
        shape = (CHUNK, CHUNK)
        causal = lax.broadcasted_iota(jnp.int32, shape, 1) <= lax.broadcasted_iota(
            jnp.int32, shape, 0
        )
        for k in range(CHUNKS):
            rows = slice(k * CHUNK, (k + 1) * CHUNK)
            part = sums[k]
            middle = part[CHUNK // 2 - 1 : CHUNK // 2]
            end = part[CHUNK - 1 : CHUNK]
            in_scr[rows, :] = halves(jnp.exp(middle - part))
            out_scr[rows, :] = halves(jnp.exp(part - middle))
            enter_scr[rows, :] = halves(jnp.exp(before + part))
            row_scr[k : k + 1, :] = jnp.exp(end - middle)
            row_scr[4 + k : 5 + k, :] = jnp.exp(middle)
            row_scr[8 + k : 9 + k, :] = jnp.exp(end)
            before = before + end
            b_part, c_part = b_ref[rows, :], c_ref[rows, :]
            bt_scr[k] = b_part.astype(F32).T.astype(BF)
            scores = jnp.where(causal, dot(c_part, b_part, (1, 1)), 0.0)
            hi = scores.astype(BF)
            left_scr[k, :, 0:CHUNK] = hi
            left_scr[k, :, CHUNK : 2 * CHUNK] = hi
            left_scr[k, :, 2 * CHUNK : 3 * CHUNK] = (scores - hi.astype(F32)).astype(BF)
            left_scr[k, :, 3 * CHUNK : 3 * CHUNK + N] = c_part

    head = first_head + step * (COLS // HEAD)
    twice = spread(head)
    once = spread(head, False)
    ends = dot(halves(row_scr[...]), twice)
    skip_parts = three_terms(jnp.broadcast_to(skip_ref[...], (16, H)))
    skip = sum(dot(part.astype(BF), once) for part in skip_parts)[0:1]
    running = None
    for k in range(CHUNKS):
        rows = slice(k * CHUNK, (k + 1) * CHUNK)
        x = x_ref[rows, :].astype(F32)
        exact = x * dot(in_scr[rows, :], twice)
        scaled = exact.astype(BF)
        right = [scaled, (exact - scaled.astype(F32)).astype(BF), scaled]
        if running is not None:
            right.append((running * ends[4 + k : 5 + k]).astype(BF))
        inner = dot(left_scr[k, :, 0 : CHUNK * len(right)], jnp.concatenate(right, axis=0))
        if k + 1 < CHUNKS:
            made = dot(bt_scr[k], scaled) * ends[k : k + 1]
            running = made if running is None else running * ends[8 + k : 9 + k] + made
        gate = gate_ref[rows, :].astype(F32)
        opened = gate / (1.0 + jnp.exp(-gate))
        mixed = inner * dot(out_scr[rows, :], twice) + skip * x
        local_ref[rows, :] = (mixed * opened).astype(BF)
        factor_ref[rows, :] = (dot(enter_scr[rows, :], twice) * opened).astype(BF)

    @pl.when(step == pl.num_programs(0) - 1)
    def _():
        held.wait()


def local_part(after, share, logs, skip, b, c, x, gate, weight):
    wide = (TOKENS_PER_BLOCK, DI // SHARES)
    steps = wide[1] // COLS
    whole = lambda i: (0, 0)
    mine = lambda i: (0, i)
    taken = lambda i: (0, i + share * steps)
    anywhere = pl.BlockSpec(memory_space=pl.ANY)
    return pl.pallas_call(
        functools.partial(local_kernel, share * (H // SHARES)),
        grid=(steps,),
        in_specs=[
            anywhere,
            pl.BlockSpec((H, TOKENS_PER_BLOCK), whole),
            pl.BlockSpec((1, H), whole),
            pl.BlockSpec((TOKENS_PER_BLOCK, N), whole),
            pl.BlockSpec((TOKENS_PER_BLOCK, N), whole),
            pl.BlockSpec((TOKENS_PER_BLOCK, COLS), taken),
            pl.BlockSpec((TOKENS_PER_BLOCK, COLS), taken),
            anywhere,
        ],
        out_specs=[
            pl.BlockSpec((TOKENS_PER_BLOCK, COLS), mine),
            pl.BlockSpec((TOKENS_PER_BLOCK, COLS), mine),
            pl.BlockSpec(memory_space=pltpu.VMEM),
        ],
        out_shape=[
            pltpu.HBM(wide, BF),
            pltpu.HBM(wide, BF),
            pltpu.VMEM((DI, HELD // SHARES), BF),
        ],
        scratch_shapes=[
            pltpu.VMEM((CHUNKS, N, CHUNK), BF),
            pltpu.VMEM((CHUNKS, CHUNK, 3 * CHUNK + N), BF),
            pltpu.VMEM((TOKENS_PER_BLOCK, 2 * H), BF),
            pltpu.VMEM((TOKENS_PER_BLOCK, 2 * H), BF),
            pltpu.VMEM((TOKENS_PER_BLOCK, 2 * H), BF),
            pltpu.VMEM((16, 2 * H), F32),
            pltpu.SemaphoreType.DMA,
        ],
        compiler_params=pltpu.CompilerParams(vmem_limit_bytes=16 * MIB),
        cost_estimate=pl.CostEstimate(
            flops=4 * 10**9, bytes_accessed=6 * MIB, transcendentals=10**6
        ),
        name="local_part",
    )(after, *(in_hbm(part) for part in (logs, skip, b, c, x, gate, weight)))


def output_kernel(
    state_ref, c_ref, gain_ref, held_refs, local_hbms, factor_hbms, weight_hbm, out_ref,
    local_ref, factor_ref, weight_ref, normed_scr, row_sems, weight_sem,
):
    width = 256
    half_rows = TOKENS_PER_BLOCK // 2
    shape = (width, width)
    copies = []
    for k in range(2):
        rows = pl.ds(k * half_rows, half_rows)
        group = []
        for part in range(SHARES):
            columns = pl.ds(part * (DI // SHARES), DI // SHARES)
            for i, (source, target) in enumerate(
                ((local_hbms[part], local_ref), (factor_hbms[part], factor_ref))
            ):
                group.append(
                    pltpu.make_async_copy(
                        source.at[rows, :],
                        target.at[rows, columns],
                        row_sems.at[k, part * 2 + i],
                    )
                )
        for copy in group:
            copy.start()
        copies.append(group)
    rest = out_ref.shape[1] - HELD
    weight_copy = pltpu.make_async_copy(
        weight_hbm.at[:, pl.ds(HELD, rest)], weight_ref, weight_sem
    )
    weight_copy.start()
    same = (
        lax.broadcasted_iota(jnp.int32, shape, 0) // HEAD
        == lax.broadcasted_iota(jnp.int32, shape, 1) // HEAD
    )
    mean_of = jnp.where(same, 1.0 / HEAD, 0.0).astype(BF)
    for k in range(2):
        for copy in copies[k]:
            copy.wait()
        rows = slice(k * half_rows, (k + 1) * half_rows)
        c = c_ref[rows, :]
        for j in range(DI // width):
            columns = slice(j * width, (j + 1) * width)
            carried = dot(c, state_ref[columns, :], (1, 1))
            gated = local_ref[rows, columns].astype(F32) + factor_ref[rows, columns] * carried
            mean = dot((gated * gated).astype(BF), mean_of)
            normed = gated * (lax.rsqrt(mean + EPS) * gain_ref[:, columns])
            normed_scr[rows, columns] = normed.astype(BF)
    each = HELD // SHARES
    for part in range(SHARES):
        columns = slice(part * each, (part + 1) * each)
        out_ref[:, columns] = dot(normed_scr[...], held_refs[part][...]).astype(BF)
    weight_copy.wait()
    for j in range(rest // width):
        columns = slice(j * width, (j + 1) * width)
        made = dot(normed_scr[...], weight_ref[:, columns])
        out_ref[:, HELD + j * width : HELD + (j + 1) * width] = made.astype(BF)


def projected_tokens(state, c, gain, weight, local, factor, held):
    width_out = weight.shape[1]
    vmem, anywhere = pl.BlockSpec(memory_space=pltpu.VMEM), pl.BlockSpec(memory_space=pl.ANY)
    held_vmem = [pltpu.with_memory_space_constraint(part, pltpu.VMEM) for part in held]
    return pl.pallas_call(
        output_kernel,
        in_specs=[vmem, vmem, vmem, [vmem] * SHARES, [anywhere] * SHARES, [anywhere] * SHARES, anywhere],
        out_specs=vmem,
        out_shape=jax.ShapeDtypeStruct((TOKENS_PER_BLOCK, width_out), BF),
        scratch_shapes=[
            pltpu.VMEM((TOKENS_PER_BLOCK, DI), BF),
            pltpu.VMEM((TOKENS_PER_BLOCK, DI), BF),
            pltpu.VMEM((DI, width_out - HELD), BF),
            pltpu.VMEM((TOKENS_PER_BLOCK, DI), BF),
            pltpu.SemaphoreType.DMA((2, 2 * SHARES)),
            pltpu.SemaphoreType.DMA,
        ],
        compiler_params=pltpu.CompilerParams(vmem_limit_bytes=28 * MIB),
        cost_estimate=pl.CostEstimate(
            flops=4 * 10**9, bytes_accessed=12 * MIB, transcendentals=10**6
        ),
        name="projected_tokens",
    )(state, c, gain, held_vmem, [in_hbm(p) for p in local], [in_hbm(p) for p in factor], in_hbm(weight))


def tile_kernel(order_ref, in_ref, out_ref, sems):
    piece = TILE // PIECES
    copies = []
    for k in range(TOKENS_PER_BLOCK // TILE):
        first = pl.multiple_of(order_ref[0, k] * TILE, TILE)
        for i in range(PIECES):
            source = in_ref.at[pl.ds(first + i * piece, piece), :]
            target = out_ref.at[pl.ds(k * TILE + i * piece, piece), :]
            copies.append(pltpu.make_async_copy(source, target, sems.at[k * PIECES + i]))
    for copy in copies:
        copy.start()
    for copy in copies:
        copy.wait()


def chosen_tiles(order, arrived):
    return pl.pallas_call(
        tile_kernel,
        in_specs=[pl.BlockSpec(memory_space=pltpu.SMEM), pl.BlockSpec(memory_space=pl.ANY)],
        out_specs=pl.BlockSpec(memory_space=pl.ANY),
        out_shape=jax.ShapeDtypeStruct(arrived.shape, arrived.dtype),
        scratch_shapes=[pltpu.SemaphoreType.DMA((PIECES * TOKENS_PER_BLOCK // TILE,))],
        compiler_params=pltpu.CompilerParams(vmem_limit_bytes=MIB),
        cost_estimate=pl.CostEstimate(flops=0, bytes_accessed=3 * MIB, transcendentals=0),
        name="chosen_tiles",
    )(order, arrived)


def swapped(x, axes):
    return lax.all_to_all(x, axes, split_axis=0, concat_axis=0, tiled=True)


def shards(
    ssd_input,
    gate_input,
    b_matrix,
    c_matrix,
    log_decay,
    d_skip,
    norm_gain,
    out_weight,
    view_order,
    tile_order,
):
    bands = lax.axis_size(SEQ)
    width_out = out_weight.shape[1]
    x, gate, b, c = (part[0, 0] for part in (ssd_input, gate_input, b_matrix, c_matrix))
    logs = log_decay[0, 0]
    own = (logs, d_skip.reshape(1, H), b, c, x, gate, out_weight)
    states = swapped(block_states(view_order, logs, b, x), PLANE)
    first = local_part(in_hbm(view_order), 0, *own)
    totals = plane_totals(states, first[0], lax.axis_size("z"))
    second = local_part(totals, 1, *own)
    entering = swapped(entering_states(states, swapped(totals, "z")), PLANE).reshape(DI, N)
    projected = projected_tokens(
        entering, c, norm_gain.reshape(1, DI), out_weight, *zip(first, second)
    )
    arrived = swapped(projected.reshape(bands, TOKENS_PER_BLOCK // bands, width_out), SEQ)
    chosen = chosen_tiles(tile_order, arrived.reshape(TOKENS_PER_BLOCK, width_out))
    return chosen.reshape(1, 1, TOKENS_PER_BLOCK, width_out)


def solution(mesh):
    split = Mesh(mesh.devices.reshape(8, 4, 2, mesh.shape["view"]), (*SEQ, "view"))
    whole = P(SEQ, "view", None, None)
    in_specs = (whole,) * 5 + (P(),) * 3 + (P(SEQ, None),) * 2
    return jax.shard_map(shards, mesh=split, in_specs=in_specs, out_specs=whole, check_vma=False)
```

```python
import functools

import jax
import jax.numpy as jnp
from jax import lax
from jax.experimental import pallas as pl
from jax.experimental.pallas import tpu as pltpu
from jax.sharding import Mesh
from jax.sharding import PartitionSpec as P

H = 32
HEAD = 64
N = 128
TILE = 128
TOKENS_PER_BLOCK = 512
DI = H * HEAD
CHUNK = 128
CHUNKS = TOKENS_PER_BLOCK // CHUNK
COLS = 1024
EPS = 1e-05
SEQ = ("z", "y", "core")
PLANE = ("y", "core", "view")
TAIL = 16
PIECES = 4
HELD = 512
ROWS = HEAD + TAIL
BF = jnp.bfloat16
F32 = jnp.float32
MIB = 2**20


def dot(a, b, contract=(1, 0)):
    return lax.dot_general(
        a, b, (((contract[0],), (contract[1],)), ((), ())), preferred_element_type=F32
    )


def three_terms(x):
    hi = x.astype(BF).astype(F32)
    rest = x - hi
    mid = rest.astype(BF).astype(F32)
    return hi, mid, rest - mid


def chunk_sums(logs):
    shape = (CHUNK, CHUNK)
    row = lax.broadcasted_iota(jnp.int32, shape, 0)
    column = lax.broadcasted_iota(jnp.int32, shape, 1)
    upto = jnp.where(column <= row, 1.0, 0.0).astype(BF)
    parts = [part.astype(BF) for part in three_terms(logs)]
    return [
        sum(dot(upto, part[:, k * CHUNK : (k + 1) * CHUNK], (1, 1)) for part in parts)
        for k in range(CHUNKS)
    ]


def halves(x):
    hi = x.astype(BF).astype(F32)
    lane = lax.broadcasted_iota(jnp.int32, x.shape, x.ndim - 1)
    return jnp.where(lane < H, hi, x - hi).astype(BF)


def in_hbm(x):
    return pltpu.with_memory_space_constraint(x, pltpu.HBM)


def spread(first_head, columns, copies=2):
    shape = (copies * H, columns)
    head = lax.broadcasted_iota(jnp.int32, shape, 0) % H
    column = lax.broadcasted_iota(jnp.int32, shape, 1) // HEAD + first_head
    return jnp.where(head == column, 1.0, 0.0).astype(BF)


def column_copies(source, target, sems):
    return [
        pltpu.make_async_copy(
            source.at[:, pl.ds(k * COLS, COLS)], target.at[:, pl.ds(k * COLS, COLS)], sems.at[k]
        )
        for k in range(DI // COLS)
    ]


def state_kernel(order_ref, log_hbm, b_hbm, x_hbm, out_ref, logs_scr, b_scr, x_scr, sems, x_sems):
    log_copy = pltpu.make_async_copy(log_hbm, logs_scr, sems.at[0])
    b_copy = pltpu.make_async_copy(b_hbm, b_scr, sems.at[1])
    x_copies = column_copies(x_hbm, x_scr, x_sems)
    for copy in (log_copy, b_copy, *x_copies):
        copy.start()
    log_copy.wait()
    logs = logs_scr[...]
    sums = chunk_sums(jnp.concatenate([logs, logs], axis=0))
    later = jnp.zeros((1, 2 * H), F32)
    weights = []
    for k in reversed(range(CHUNKS)):
        end = sums[k][CHUNK - 1 : CHUNK]
        weights.insert(0, halves(jnp.exp(end - sums[k] + later)))
        later = later + end
    weights = jnp.concatenate(weights, axis=0)

    view = lax.axis_index("view")
    rank = jnp.int32(0)
    for k in range(1, 4):
        rank = rank + jnp.where(order_ref[0, k] == view, k, 0)
    decay = jnp.broadcast_to(jnp.exp(jnp.sum(logs, axis=1, keepdims=True)), (H, N))
    hi, mid, lo = (part[:, None, :] for part in three_terms(decay))
    place = lax.broadcasted_iota(jnp.int32, (H, TAIL, N), 1)
    tail = jnp.where(place == 0, hi, jnp.where(place == 1, mid, jnp.where(place == 2, lo, 0.0)))
    tail = jnp.where(place == 3, rank.astype(F32), tail)
    out_ref[:, HEAD:ROWS, :] = tail.astype(BF)

    b_copy.wait()
    b_rows = b_scr[...].astype(F32).T.astype(BF)
    heads = COLS // HEAD
    for k, copy in enumerate(x_copies):
        copy.wait()
        x = x_scr[:, k * COLS : (k + 1) * COLS].astype(F32)
        scaled = (x * dot(weights, spread(k * heads, COLS))).astype(BF)
        state = dot(b_rows, scaled).T.astype(BF)
        out_ref[k * heads : (k + 1) * heads, 0:HEAD, :] = state.reshape(heads, HEAD, N)


def block_states(order, logs, b, x):
    anywhere = pl.BlockSpec(memory_space=pl.ANY)
    return pl.pallas_call(
        state_kernel,
        in_specs=[pl.BlockSpec(memory_space=pltpu.SMEM), anywhere, anywhere, anywhere],
        out_shape=jax.ShapeDtypeStruct((H, ROWS, N), BF),
        scratch_shapes=[
            pltpu.VMEM(logs.shape, F32),
            pltpu.VMEM(b.shape, BF),
            pltpu.VMEM(x.shape, BF),
            pltpu.SemaphoreType.DMA((2,)),
            pltpu.SemaphoreType.DMA((DI // COLS,)),
        ],
        compiler_params=pltpu.CompilerParams(vmem_limit_bytes=16 * MIB),
        cost_estimate=pl.CostEstimate(flops=2 * 10**9, bytes_accessed=3 * MIB, transcendentals=0),
        name="block_states",
    )(*(in_hbm(part) for part in (order, logs, b, x)))


def read_tail(ref, at):
    tail = ref[at, HEAD:ROWS, :].astype(F32)
    return tail[0:1] + tail[1:2] + tail[2:3], tail[3:4]


def scan_plane(ref, running, emit):
    views = 4
    product = jnp.ones((1, N), F32)
    for band in range(ref.shape[0] // views):
        blocks = [band * views + v for v in range(views)]
        states = [ref[k, 0:HEAD, :].astype(F32) for k in blocks]
        decays, ranks = zip(*(read_tail(ref, k) for k in blocks))
        entering = [None] * views
        for place in range(views):
            chosen, decay = states[0], decays[0]
            for v in range(views):
                here = ranks[v] == float(place)
                entering[v] = running if place == 0 else jnp.where(here, running, entering[v])
                if v:
                    chosen = jnp.where(here, states[v], chosen)
                    decay = jnp.where(here, decays[v], decay)
            running = decay * running + chosen
            product = product * decay
        if emit is not None:
            for v in range(views):
                emit(blocks[v], entering[v])
    return running, product


def total_kernel(in_ref, token_ref, out_ref):
    total, product = scan_plane(in_ref, jnp.zeros((HEAD, N), F32), None)
    hi, mid, lo = three_terms(product)
    place = lax.broadcasted_iota(jnp.int32, (TAIL, N), 0)
    tail = jnp.where(place == 0, hi, jnp.where(place == 1, mid, jnp.where(place == 2, lo, 0.0)))
    for k in range(out_ref.shape[0]):
        out_ref[k, 0:HEAD, :] = total.astype(BF)
        out_ref[k, HEAD:ROWS, :] = tail.astype(BF)


def plane_totals(states, token, planes):
    return pl.pallas_call(
        total_kernel,
        in_specs=[pl.BlockSpec(memory_space=pltpu.VMEM), pl.BlockSpec(memory_space=pl.ANY)],
        out_shape=jax.ShapeDtypeStruct((planes, ROWS, N), BF),
        compiler_params=pltpu.CompilerParams(vmem_limit_bytes=8 * MIB),
        cost_estimate=pl.CostEstimate(flops=10**6, bytes_accessed=MIB, transcendentals=0),
        name="plane_totals",
    )(states, in_hbm(token))


def entering_kernel(in_ref, totals_ref, out_ref):
    mine = lax.axis_index("z")
    carry = jnp.zeros((HEAD, N), F32)
    for k in range(totals_ref.shape[0] - 1):
        decay, _ = read_tail(totals_ref, k)
        later = decay * carry + totals_ref[k, 0:HEAD, :].astype(F32)
        carry = jnp.where(k < mine, later, carry)

    def emit(block, value):
        out_ref[block, :, :] = value.astype(BF)

    scan_plane(in_ref, carry, emit)


def entering_states(states, totals):
    return pl.pallas_call(
        entering_kernel,
        out_shape=jax.ShapeDtypeStruct((states.shape[0], HEAD, N), BF),
        compiler_params=pltpu.CompilerParams(vmem_limit_bytes=8 * MIB),
        cost_estimate=pl.CostEstimate(flops=10**6, bytes_accessed=2 * MIB, transcendentals=0),
        name="entering_states",
    )(states, totals)


def local_kernel(
    skip_ref, log_hbm, b_hbm, c_hbm, x_hbm, gate_hbm, weight_hbm,
    local_hbm, factor_hbm, held_ref,
    log_scr, b_scr, c_scr, x_scr, gate_scr, local_scr, factor_scr, row_scr,
    sems, x_sems, gate_sems, local_sems, factor_sems,
):
    log_copy = pltpu.make_async_copy(log_hbm, log_scr, sems.at[0])
    b_copy = pltpu.make_async_copy(b_hbm, b_scr, sems.at[1])
    c_copy = pltpu.make_async_copy(c_hbm, c_scr, sems.at[2])
    held_copy = pltpu.make_async_copy(weight_hbm.at[:, pl.ds(0, HELD)], held_ref, sems.at[3])
    x_copies = column_copies(x_hbm, x_scr, x_sems)
    gate_copies = column_copies(gate_hbm, gate_scr, gate_sems)
    local_copies = column_copies(local_scr, local_hbm, local_sems)
    factor_copies = column_copies(factor_scr, factor_hbm, factor_sems)
    for copy in (log_copy, b_copy, c_copy):
        copy.start()
    for pair in zip(x_copies, gate_copies):
        for copy in pair:
            copy.start()
    held_copy.start()

    log_copy.wait()
    logs = log_scr[...]
    sums = chunk_sums(jnp.concatenate([logs, logs], axis=0))
    before = jnp.zeros((1, 2 * H), F32)
    row_scr[...] = jnp.zeros_like(row_scr)
    inward, outward, entered = [], [], []
    for k in range(CHUNKS):
        part = sums[k]
        middle = part[CHUNK // 2 - 1 : CHUNK // 2]
        end = part[CHUNK - 1 : CHUNK]
        inward.append(halves(jnp.exp(middle - part)))
        outward.append(halves(jnp.exp(part - middle)))
        entered.append(halves(jnp.exp(before + part)))
        row_scr[k : k + 1, :] = jnp.exp(end - middle)
        row_scr[4 + k : 5 + k, :] = jnp.exp(middle)
        row_scr[8 + k : 9 + k, :] = jnp.exp(end)
        before = before + end
    ends_once = halves(row_scr[...])
    skips = [part.astype(BF) for part in three_terms(jnp.broadcast_to(skip_ref[...], (16, H)))]

    b_copy.wait()
    c_copy.wait()
    shape = (CHUNK, CHUNK)
    causal = lax.broadcasted_iota(jnp.int32, shape, 1) <= lax.broadcasted_iota(
        jnp.int32, shape, 0
    )
    b_rows, left = [], []
    for k in range(CHUNKS):
        rows = slice(k * CHUNK, (k + 1) * CHUNK)
        b_part, c_part = b_scr[rows, :], c_scr[rows, :]
        b_rows.append(b_part.astype(F32).T.astype(BF))
        scores = jnp.where(causal, dot(c_part, b_part, (1, 1)), 0.0)
        hi = scores.astype(BF)
        lo = (scores - hi.astype(F32)).astype(BF)
        left.append(jnp.concatenate([hi, hi, lo, c_part], axis=1))

    for block in range(DI // COLS):
        columns = slice(block * COLS, (block + 1) * COLS)
        head = block * (COLS // HEAD)
        twice = spread(head, COLS)
        once = spread(head, COLS, 1)
        ends = dot(ends_once, twice)
        skip = sum(dot(part, once) for part in skips)[0:1]
        running = None
        x_copies[block].wait()
        gate_copies[block].wait()
        for k in range(CHUNKS):
            rows = slice(k * CHUNK, (k + 1) * CHUNK)
            x = x_scr[rows, columns].astype(F32)
            exact = x * dot(inward[k], twice)
            scaled = exact.astype(BF)
            right = [scaled, (exact - scaled.astype(F32)).astype(BF), scaled]
            if running is not None:
                right.append((running * ends[4 + k : 5 + k]).astype(BF))
            inner = dot(left[k][:, 0 : CHUNK * len(right)], jnp.concatenate(right, axis=0))
            if k + 1 < CHUNKS:
                made = dot(b_rows[k], scaled) * ends[k : k + 1]
                running = made if running is None else running * ends[8 + k : 9 + k] + made
            half = 0.5 * gate_scr[rows, columns].astype(F32)
            opened = half + half * jnp.tanh(half)
            mixed = inner * dot(outward[k], twice) + skip * x
            local_scr[rows, columns] = (mixed * opened).astype(BF)
            factor_scr[rows, columns] = (dot(entered[k], twice) * opened).astype(BF)
        local_copies[block].start()
        factor_copies[block].start()
    for copy in (held_copy, *local_copies, *factor_copies):
        copy.wait()


def local_part(logs, skip, b, c, x, gate, weight):
    blocks = DI // COLS
    anywhere = pl.BlockSpec(memory_space=pl.ANY)
    return pl.pallas_call(
        local_kernel,
        in_specs=[pl.BlockSpec(memory_space=pltpu.VMEM)] + [anywhere] * 6,
        out_specs=[anywhere, anywhere, pl.BlockSpec(memory_space=pltpu.VMEM)],
        out_shape=[pltpu.HBM(x.shape, BF), pltpu.HBM(x.shape, BF), pltpu.VMEM((DI, HELD), BF)],
        scratch_shapes=[
            pltpu.VMEM(logs.shape, F32),
            pltpu.VMEM(b.shape, BF),
            pltpu.VMEM(c.shape, BF),
            pltpu.VMEM(x.shape, BF),
            pltpu.VMEM(x.shape, BF),
            pltpu.VMEM(x.shape, BF),
            pltpu.VMEM(x.shape, BF),
            pltpu.VMEM((16, 2 * H), F32),
            pltpu.SemaphoreType.DMA((4,)),
            *[pltpu.SemaphoreType.DMA((blocks,))] * 4,
        ],
        compiler_params=pltpu.CompilerParams(vmem_limit_bytes=32 * MIB),
        cost_estimate=pl.CostEstimate(
            flops=8 * 10**9, bytes_accessed=12 * MIB, transcendentals=10**6
        ),
        name="local_part",
    )(skip, *(in_hbm(part) for part in (logs, b, c, x, gate, weight)))


def output_kernel(
    state_ref, c_ref, gain_ref, held_ref, local_hbm, factor_hbm, weight_hbm, out_ref,
    local_ref, factor_ref, weight_ref, normed_scr, row_sems, weight_sem,
):
    width = 256
    half_rows = TOKENS_PER_BLOCK // 2
    shape = (width, width)
    copies = []
    for k in range(2):
        rows = pl.ds(k * half_rows, half_rows)
        group = [
            pltpu.make_async_copy(source.at[rows, :], target.at[rows, :], row_sems.at[k, i])
            for i, (source, target) in enumerate(
                ((local_hbm, local_ref), (factor_hbm, factor_ref))
            )
        ]
        for copy in group:
            copy.start()
        copies.append(group)
    rest = out_ref.shape[1] - HELD
    weight_copy = pltpu.make_async_copy(
        weight_hbm.at[:, pl.ds(HELD, rest)], weight_ref, weight_sem
    )
    weight_copy.start()
    same = (
        lax.broadcasted_iota(jnp.int32, shape, 0) // HEAD
        == lax.broadcasted_iota(jnp.int32, shape, 1) // HEAD
    )
    mean_of = jnp.where(same, 1.0 / HEAD, 0.0).astype(BF)
    for k in range(2):
        for copy in copies[k]:
            copy.wait()
        rows = slice(k * half_rows, (k + 1) * half_rows)
        c = c_ref[rows, :]
        for j in range(DI // width):
            columns = slice(j * width, (j + 1) * width)
            carried = dot(c, state_ref[columns, :], (1, 1))
            gated = local_ref[rows, columns].astype(F32) + factor_ref[rows, columns] * carried
            mean = dot((gated * gated).astype(BF), mean_of)
            normed = gated * (lax.rsqrt(mean + EPS) * gain_ref[:, columns])
            normed_scr[rows, columns] = normed.astype(BF)
    for j in range(HELD // width):
        columns = slice(j * width, (j + 1) * width)
        out_ref[:, columns] = dot(normed_scr[...], held_ref[:, columns]).astype(BF)
    weight_copy.wait()
    for j in range(rest // width):
        columns = slice(j * width, (j + 1) * width)
        made = dot(normed_scr[...], weight_ref[:, columns])
        out_ref[:, HELD + j * width : HELD + (j + 1) * width] = made.astype(BF)


def projected_tokens(state, c, gain, weight, local, factor, held):
    width_out = weight.shape[1]
    vmem, anywhere = pl.BlockSpec(memory_space=pltpu.VMEM), pl.BlockSpec(memory_space=pl.ANY)
    held = pltpu.with_memory_space_constraint(held, pltpu.VMEM)
    return pl.pallas_call(
        output_kernel,
        in_specs=[vmem] * 4 + [anywhere] * 3,
        out_specs=vmem,
        out_shape=jax.ShapeDtypeStruct((TOKENS_PER_BLOCK, width_out), BF),
        scratch_shapes=[
            pltpu.VMEM((TOKENS_PER_BLOCK, DI), BF),
            pltpu.VMEM((TOKENS_PER_BLOCK, DI), BF),
            pltpu.VMEM((DI, width_out - HELD), BF),
            pltpu.VMEM((TOKENS_PER_BLOCK, DI), BF),
            pltpu.SemaphoreType.DMA((2, 2)),
            pltpu.SemaphoreType.DMA,
        ],
        compiler_params=pltpu.CompilerParams(vmem_limit_bytes=28 * MIB),
        cost_estimate=pl.CostEstimate(
            flops=4 * 10**9, bytes_accessed=12 * MIB, transcendentals=10**6
        ),
        name="projected_tokens",
    )(state, c, gain, held, in_hbm(local), in_hbm(factor), in_hbm(weight))


def tile_kernel(order_ref, in_ref, out_ref, sems):
    piece = TILE // PIECES
    copies = []
    for k in range(TOKENS_PER_BLOCK // TILE):
        first = pl.multiple_of(order_ref[0, k] * TILE, TILE)
        for i in range(PIECES):
            source = in_ref.at[pl.ds(first + i * piece, piece), :]
            target = out_ref.at[pl.ds(k * TILE + i * piece, piece), :]
            copies.append(pltpu.make_async_copy(source, target, sems.at[k * PIECES + i]))
    for copy in copies:
        copy.start()
    for copy in copies:
        copy.wait()


def chosen_tiles(order, arrived):
    return pl.pallas_call(
        tile_kernel,
        in_specs=[pl.BlockSpec(memory_space=pltpu.SMEM), pl.BlockSpec(memory_space=pl.ANY)],
        out_specs=pl.BlockSpec(memory_space=pl.ANY),
        out_shape=jax.ShapeDtypeStruct(arrived.shape, arrived.dtype),
        scratch_shapes=[pltpu.SemaphoreType.DMA((PIECES * TOKENS_PER_BLOCK // TILE,))],
        compiler_params=pltpu.CompilerParams(vmem_limit_bytes=MIB),
        cost_estimate=pl.CostEstimate(flops=0, bytes_accessed=3 * MIB, transcendentals=0),
        name="chosen_tiles",
    )(order, arrived)


def swapped(x, axes):
    return lax.all_to_all(x, axes, split_axis=0, concat_axis=0, tiled=True)


def shards(
    ssd_input,
    gate_input,
    b_matrix,
    c_matrix,
    log_decay,
    d_skip,
    norm_gain,
    out_weight,
    view_order,
    tile_order,
):
    bands = lax.axis_size(SEQ)
    width_out = out_weight.shape[1]
    x, gate, b, c = (part[0, 0] for part in (ssd_input, gate_input, b_matrix, c_matrix))
    logs = log_decay[0, 0]
    states = swapped(block_states(view_order, logs, b, x), PLANE)
    local, factor, held = local_part(logs, d_skip.reshape(1, H), b, c, x, gate, out_weight)
    totals = swapped(plane_totals(states, local, lax.axis_size("z")), "z")
    entering = swapped(entering_states(states, totals), PLANE).reshape(DI, N)
    projected = projected_tokens(
        entering, c, norm_gain.reshape(1, DI), out_weight, local, factor, held
    )
    arrived = swapped(projected.reshape(bands, TOKENS_PER_BLOCK // bands, width_out), SEQ)
    chosen = chosen_tiles(tile_order, arrived.reshape(TOKENS_PER_BLOCK, width_out))
    return chosen.reshape(1, 1, TOKENS_PER_BLOCK, width_out)


def solution(mesh):
    split = Mesh(mesh.devices.reshape(8, 4, 2, mesh.shape["view"]), (*SEQ, "view"))
    whole = P(SEQ, "view", None, None)
    in_specs = (whole,) * 5 + (P(),) * 3 + (P(SEQ, None),) * 2
    return jax.shard_map(shards, mesh=split, in_specs=in_specs, out_specs=whole, check_vma=False)
```

```python
import functools

import jax
import jax.numpy as jnp
from jax import lax
from jax.experimental import pallas as pl
from jax.experimental.pallas import tpu as pltpu
from jax.sharding import Mesh
from jax.sharding import PartitionSpec as P

H = 32
HEAD = 64
N = 128
TILE = 128
TOKENS_PER_BLOCK = 512
DI = H * HEAD
CHUNK = 128
CHUNKS = TOKENS_PER_BLOCK // CHUNK
COLS = 1024
EPS = 1e-05
SEQ = ("z", "y", "core")
PLANE = ("y", "core", "view")
SUB = 8
PARTS = HEAD // SUB
MESSAGE = (PARTS + 1, SUB, N)
HELD = 512
BF = jnp.bfloat16
F32 = jnp.float32
MIB = 2**20


def dot(a, b, contract=(1, 0)):
    return lax.dot_general(
        a, b, (((contract[0],), (contract[1],)), ((), ())), preferred_element_type=F32
    )


def three_terms(x):
    hi = x.astype(BF).astype(F32)
    rest = x - hi
    mid = rest.astype(BF).astype(F32)
    return hi, mid, rest - mid


def chunk_sums(logs):
    shape = (CHUNK, CHUNK)
    row = lax.broadcasted_iota(jnp.int32, shape, 0)
    column = lax.broadcasted_iota(jnp.int32, shape, 1)
    upto = jnp.where(column <= row, 1.0, 0.0).astype(BF)
    parts = [part.astype(BF) for part in three_terms(logs)]
    return [
        sum(dot(upto, part[:, k * CHUNK : (k + 1) * CHUNK], (1, 1)) for part in parts)
        for k in range(CHUNKS)
    ]


def halves(x):
    hi = x.astype(BF).astype(F32)
    lane = lax.broadcasted_iota(jnp.int32, x.shape, x.ndim - 1)
    return jnp.where(lane < H, hi, x - hi).astype(BF)


def in_hbm(x):
    return pltpu.with_memory_space_constraint(x, pltpu.HBM)


def spread(first_head, columns, copies=2):
    shape = (copies * H, columns)
    head = lax.broadcasted_iota(jnp.int32, shape, 0) % H
    column = lax.broadcasted_iota(jnp.int32, shape, 1) // HEAD + first_head
    return jnp.where(head == column, 1.0, 0.0).astype(BF)


def column_copies(source, target, sems):
    return [
        pltpu.make_async_copy(
            source.at[:, pl.ds(k * COLS, COLS)], target.at[:, pl.ds(k * COLS, COLS)], sems.at[k]
        )
        for k in range(DI // COLS)
    ]


def state_kernel(order_ref, log_hbm, b_hbm, x_hbm, out_ref, logs_scr, b_scr, x_scr, sems, x_sems):
    log_copy = pltpu.make_async_copy(log_hbm, logs_scr, sems.at[0])
    b_copy = pltpu.make_async_copy(b_hbm, b_scr, sems.at[1])
    x_copies = column_copies(x_hbm, x_scr, x_sems)
    for copy in (log_copy, b_copy, *x_copies):
        copy.start()
    log_copy.wait()
    logs = logs_scr[...]
    sums = chunk_sums(jnp.concatenate([logs, logs], axis=0))
    later = jnp.zeros((1, 2 * H), F32)
    weights = []
    for k in reversed(range(CHUNKS)):
        end = sums[k][CHUNK - 1 : CHUNK]
        weights.insert(0, halves(jnp.exp(end - sums[k] + later)))
        later = later + end
    weights = jnp.concatenate(weights, axis=0)

    view = lax.axis_index("view")
    rank = jnp.int32(0)
    for k in range(1, 4):
        rank = rank + jnp.where(order_ref[0, k] == view, k, 0)
    decay = jnp.broadcast_to(jnp.exp(jnp.sum(logs, axis=1, keepdims=True)), (H, N))
    hi, mid, lo = (part[:, None, :] for part in three_terms(decay))
    place = lax.broadcasted_iota(jnp.int32, (H, SUB, N), 1)
    tail = jnp.where(place == 0, hi, jnp.where(place == 1, mid, jnp.where(place == 2, lo, 0.0)))
    tail = jnp.where(place == 3, rank.astype(F32), tail)
    out_ref[:, PARTS] = tail.astype(BF)

    b_copy.wait()
    b_rows = b_scr[...].astype(F32).T.astype(BF)
    heads = COLS // HEAD
    for k, copy in enumerate(x_copies):
        copy.wait()
        x = x_scr[:, k * COLS : (k + 1) * COLS].astype(F32)
        scaled = (x * dot(weights, spread(k * heads, COLS))).astype(BF)
        state = dot(b_rows, scaled).T.reshape(heads, PARTS, SUB, N)
        out_ref[k * heads : (k + 1) * heads, 0:PARTS] = state.astype(BF)


def block_states(order, logs, b, x):
    anywhere = pl.BlockSpec(memory_space=pl.ANY)
    return pl.pallas_call(
        state_kernel,
        in_specs=[pl.BlockSpec(memory_space=pltpu.SMEM), anywhere, anywhere, anywhere],
        out_shape=jax.ShapeDtypeStruct((H, *MESSAGE), BF),
        scratch_shapes=[
            pltpu.VMEM(logs.shape, F32),
            pltpu.VMEM(b.shape, BF),
            pltpu.VMEM(x.shape, BF),
            pltpu.SemaphoreType.DMA((2,)),
            pltpu.SemaphoreType.DMA((DI // COLS,)),
        ],
        compiler_params=pltpu.CompilerParams(vmem_limit_bytes=16 * MIB),
        cost_estimate=pl.CostEstimate(flops=2 * 10**9, bytes_accessed=3 * MIB, transcendentals=0),
        name="block_states",
    )(*(in_hbm(part) for part in (order, logs, b, x)))


def read_tail(ref, at):
    tail = ref[at, PARTS].astype(F32)
    return tail[0:1] + tail[1:2] + tail[2:3], tail[3:4]


def read_state(ref, at):
    return ref[at, 0:PARTS].astype(F32).reshape(HEAD, N)


def scan_plane(ref, running, emit):
    views = 4
    product = jnp.ones((1, N), F32)
    for band in range(ref.shape[0] // views):
        blocks = [band * views + v for v in range(views)]
        states = [read_state(ref, k) for k in blocks]
        decays, ranks = zip(*(read_tail(ref, k) for k in blocks))
        entering = [None] * views
        for place in range(views):
            chosen, decay = states[0], decays[0]
            for v in range(views):
                here = ranks[v] == float(place)
                entering[v] = running if place == 0 else jnp.where(here, running, entering[v])
                if v:
                    chosen = jnp.where(here, states[v], chosen)
                    decay = jnp.where(here, decays[v], decay)
            running = decay * running + chosen
            product = product * decay
        if emit is not None:
            for v in range(views):
                emit(blocks[v], entering[v])
    return running, product


def total_kernel(in_ref, token_ref, out_ref):
    total, product = scan_plane(in_ref, jnp.zeros((HEAD, N), F32), None)
    hi, mid, lo = three_terms(product)
    place = lax.broadcasted_iota(jnp.int32, (SUB, N), 0)
    tail = jnp.where(place == 0, hi, jnp.where(place == 1, mid, jnp.where(place == 2, lo, 0.0)))
    for k in range(out_ref.shape[0]):
        out_ref[k, 0:PARTS] = total.reshape(PARTS, SUB, N).astype(BF)
        out_ref[k, PARTS] = tail.astype(BF)


def plane_totals(states, token, planes):
    return pl.pallas_call(
        total_kernel,
        in_specs=[pl.BlockSpec(memory_space=pltpu.VMEM), pl.BlockSpec(memory_space=pl.ANY)],
        out_shape=jax.ShapeDtypeStruct((planes, *MESSAGE), BF),
        compiler_params=pltpu.CompilerParams(vmem_limit_bytes=8 * MIB),
        cost_estimate=pl.CostEstimate(flops=10**6, bytes_accessed=MIB, transcendentals=0),
        name="plane_totals",
    )(states, in_hbm(token))


def entering_kernel(in_ref, totals_ref, out_ref):
    mine = lax.axis_index("z")
    carry = jnp.zeros((HEAD, N), F32)
    for k in range(totals_ref.shape[0] - 1):
        decay, _ = read_tail(totals_ref, k)
        later = decay * carry + read_state(totals_ref, k)
        carry = jnp.where(k < mine, later, carry)

    def emit(block, value):
        out_ref[block, :, :] = value.astype(BF)

    scan_plane(in_ref, carry, emit)


def entering_states(states, totals):
    return pl.pallas_call(
        entering_kernel,
        out_shape=jax.ShapeDtypeStruct((states.shape[0], HEAD, N), BF),
        compiler_params=pltpu.CompilerParams(vmem_limit_bytes=8 * MIB),
        cost_estimate=pl.CostEstimate(flops=10**6, bytes_accessed=2 * MIB, transcendentals=0),
        name="entering_states",
    )(states, totals)


def local_kernel(
    skip_ref, log_hbm, b_hbm, c_hbm, x_hbm, gate_hbm, weight_hbm,
    local_hbm, factor_hbm, held_ref,
    log_scr, b_scr, c_scr, x_scr, gate_scr, local_scr, factor_scr, row_scr,
    sems, x_sems, gate_sems, local_sems, factor_sems,
):
    log_copy = pltpu.make_async_copy(log_hbm, log_scr, sems.at[0])
    b_copy = pltpu.make_async_copy(b_hbm, b_scr, sems.at[1])
    c_copy = pltpu.make_async_copy(c_hbm, c_scr, sems.at[2])
    held_copy = pltpu.make_async_copy(weight_hbm.at[:, pl.ds(0, HELD)], held_ref, sems.at[3])
    x_copies = column_copies(x_hbm, x_scr, x_sems)
    gate_copies = column_copies(gate_hbm, gate_scr, gate_sems)
    local_copies = column_copies(local_scr, local_hbm, local_sems)
    factor_copies = column_copies(factor_scr, factor_hbm, factor_sems)
    for copy in (log_copy, b_copy, c_copy):
        copy.start()
    for pair in zip(x_copies, gate_copies):
        for copy in pair:
            copy.start()
    held_copy.start()

    log_copy.wait()
    logs = log_scr[...]
    sums = chunk_sums(jnp.concatenate([logs, logs], axis=0))
    before = jnp.zeros((1, 2 * H), F32)
    row_scr[...] = jnp.zeros_like(row_scr)
    inward, outward, entered = [], [], []
    for k in range(CHUNKS):
        part = sums[k]
        middle = part[CHUNK // 2 - 1 : CHUNK // 2]
        end = part[CHUNK - 1 : CHUNK]
        inward.append(halves(jnp.exp(middle - part)))
        outward.append(halves(jnp.exp(part - middle)))
        entered.append(halves(jnp.exp(before + part)))
        row_scr[k : k + 1, :] = jnp.exp(end - middle)
        row_scr[4 + k : 5 + k, :] = jnp.exp(middle)
        row_scr[8 + k : 9 + k, :] = jnp.exp(end)
        before = before + end
    ends_once = halves(row_scr[...])
    skips = [part.astype(BF) for part in three_terms(jnp.broadcast_to(skip_ref[...], (16, H)))]

    b_copy.wait()
    c_copy.wait()
    shape = (CHUNK, CHUNK)
    causal = lax.broadcasted_iota(jnp.int32, shape, 1) <= lax.broadcasted_iota(
        jnp.int32, shape, 0
    )
    b_rows, left = [], []
    for k in range(CHUNKS):
        rows = slice(k * CHUNK, (k + 1) * CHUNK)
        b_part, c_part = b_scr[rows, :], c_scr[rows, :]
        b_rows.append(b_part.astype(F32).T.astype(BF))
        scores = jnp.where(causal, dot(c_part, b_part, (1, 1)), 0.0)
        hi = scores.astype(BF)
        lo = (scores - hi.astype(F32)).astype(BF)
        left.append(jnp.concatenate([hi, hi, lo, c_part], axis=1))

    for block in range(DI // COLS):
        columns = slice(block * COLS, (block + 1) * COLS)
        head = block * (COLS // HEAD)
        twice = spread(head, COLS)
        once = spread(head, COLS, 1)
        ends = dot(ends_once, twice)
        skip = sum(dot(part, once) for part in skips)[0:1]
        running = None
        x_copies[block].wait()
        gate_copies[block].wait()
        for k in range(CHUNKS):
            rows = slice(k * CHUNK, (k + 1) * CHUNK)
            x = x_scr[rows, columns].astype(F32)
            exact = x * dot(inward[k], twice)
            scaled = exact.astype(BF)
            right = [scaled, (exact - scaled.astype(F32)).astype(BF), scaled]
            if running is not None:
                right.append((running * ends[4 + k : 5 + k]).astype(BF))
            inner = dot(left[k][:, 0 : CHUNK * len(right)], jnp.concatenate(right, axis=0))
            if k + 1 < CHUNKS:
                made = dot(b_rows[k], scaled) * ends[k : k + 1]
                running = made if running is None else running * ends[8 + k : 9 + k] + made
            half = 0.5 * gate_scr[rows, columns].astype(F32)
            opened = half + half * jnp.tanh(half)
            mixed = inner * dot(outward[k], twice) + skip * x
            local_scr[rows, columns] = (mixed * opened).astype(BF)
            factor_scr[rows, columns] = (dot(entered[k], twice) * opened).astype(BF)
        local_copies[block].start()
        factor_copies[block].start()
    for copy in (held_copy, *local_copies, *factor_copies):
        copy.wait()


def local_part(logs, skip, b, c, x, gate, weight):
    blocks = DI // COLS
    anywhere = pl.BlockSpec(memory_space=pl.ANY)
    return pl.pallas_call(
        local_kernel,
        in_specs=[pl.BlockSpec(memory_space=pltpu.VMEM)] + [anywhere] * 6,
        out_specs=[anywhere, anywhere, pl.BlockSpec(memory_space=pltpu.VMEM)],
        out_shape=[pltpu.HBM(x.shape, BF), pltpu.HBM(x.shape, BF), pltpu.VMEM((DI, HELD), BF)],
        scratch_shapes=[
            pltpu.VMEM(logs.shape, F32),
            pltpu.VMEM(b.shape, BF),
            pltpu.VMEM(c.shape, BF),
            pltpu.VMEM(x.shape, BF),
            pltpu.VMEM(x.shape, BF),
            pltpu.VMEM(x.shape, BF),
            pltpu.VMEM(x.shape, BF),
            pltpu.VMEM((16, 2 * H), F32),
            pltpu.SemaphoreType.DMA((4,)),
            *[pltpu.SemaphoreType.DMA((blocks,))] * 4,
        ],
        compiler_params=pltpu.CompilerParams(vmem_limit_bytes=32 * MIB),
        cost_estimate=pl.CostEstimate(
            flops=8 * 10**9, bytes_accessed=12 * MIB, transcendentals=10**6
        ),
        name="local_part",
    )(skip, *(in_hbm(part) for part in (logs, b, c, x, gate, weight)))


def output_kernel(
    state_ref, c_ref, gain_ref, held_ref, local_hbm, factor_hbm, weight_hbm, out_ref,
    local_ref, factor_ref, weight_ref, normed_scr, row_sems, weight_sem,
):
    width = 256
    half_rows = TOKENS_PER_BLOCK // 2
    shape = (width, width)
    copies = []
    for k in range(2):
        rows = pl.ds(k * half_rows, half_rows)
        group = [
            pltpu.make_async_copy(source.at[rows, :], target.at[rows, :], row_sems.at[k, i])
            for i, (source, target) in enumerate(
                ((local_hbm, local_ref), (factor_hbm, factor_ref))
            )
        ]
        for copy in group:
            copy.start()
        copies.append(group)
    rest = out_ref.shape[1] - HELD
    weight_copy = pltpu.make_async_copy(
        weight_hbm.at[:, pl.ds(HELD, rest)], weight_ref, weight_sem
    )
    weight_copy.start()
    same = (
        lax.broadcasted_iota(jnp.int32, shape, 0) // HEAD
        == lax.broadcasted_iota(jnp.int32, shape, 1) // HEAD
    )
    mean_of = jnp.where(same, 1.0 / HEAD, 0.0).astype(BF)
    for k in range(2):
        for copy in copies[k]:
            copy.wait()
        rows = slice(k * half_rows, (k + 1) * half_rows)
        c = c_ref[rows, :]
        for j in range(DI // width):
            columns = slice(j * width, (j + 1) * width)
            carried = dot(c, state_ref[columns, :], (1, 1))
            gated = local_ref[rows, columns].astype(F32) + factor_ref[rows, columns] * carried
            mean = dot((gated * gated).astype(BF), mean_of)
            normed = gated * (lax.rsqrt(mean + EPS) * gain_ref[:, columns])
            normed_scr[rows, columns] = normed.astype(BF)
    for j in range(HELD // width):
        columns = slice(j * width, (j + 1) * width)
        out_ref[:, columns] = dot(normed_scr[...], held_ref[:, columns]).astype(BF)
    weight_copy.wait()
    for j in range(rest // width):
        columns = slice(j * width, (j + 1) * width)
        made = dot(normed_scr[...], weight_ref[:, columns])
        out_ref[:, HELD + j * width : HELD + (j + 1) * width] = made.astype(BF)


def projected_tokens(state, c, gain, weight, local, factor, held):
    width_out = weight.shape[1]
    vmem, anywhere = pl.BlockSpec(memory_space=pltpu.VMEM), pl.BlockSpec(memory_space=pl.ANY)
    held = pltpu.with_memory_space_constraint(held, pltpu.VMEM)
    return pl.pallas_call(
        output_kernel,
        in_specs=[vmem] * 4 + [anywhere] * 3,
        out_specs=vmem,
        out_shape=jax.ShapeDtypeStruct((TOKENS_PER_BLOCK, width_out), BF),
        scratch_shapes=[
            pltpu.VMEM((TOKENS_PER_BLOCK, DI), BF),
            pltpu.VMEM((TOKENS_PER_BLOCK, DI), BF),
            pltpu.VMEM((DI, width_out - HELD), BF),
            pltpu.VMEM((TOKENS_PER_BLOCK, DI), BF),
            pltpu.SemaphoreType.DMA((2, 2)),
            pltpu.SemaphoreType.DMA,
        ],
        compiler_params=pltpu.CompilerParams(vmem_limit_bytes=28 * MIB),
        cost_estimate=pl.CostEstimate(
            flops=4 * 10**9, bytes_accessed=12 * MIB, transcendentals=10**6
        ),
        name="projected_tokens",
    )(state, c, gain, held, in_hbm(local), in_hbm(factor), in_hbm(weight))


def tile_kernel(order_ref, in_ref, out_ref, sems):
    copies = []
    for k in range(TOKENS_PER_BLOCK // TILE):
        source = in_ref.at[pl.ds(pl.multiple_of(order_ref[0, k] * TILE, TILE), TILE), :]
        target = out_ref.at[pl.ds(k * TILE, TILE), :]
        copies.append(pltpu.make_async_copy(source, target, sems.at[k]))
    for copy in copies:
        copy.start()
    for copy in copies:
        copy.wait()


def chosen_tiles(order, arrived):
    return pl.pallas_call(
        tile_kernel,
        in_specs=[pl.BlockSpec(memory_space=pltpu.SMEM), pl.BlockSpec(memory_space=pl.ANY)],
        out_specs=pl.BlockSpec(memory_space=pl.ANY),
        out_shape=jax.ShapeDtypeStruct(arrived.shape, arrived.dtype),
        scratch_shapes=[pltpu.SemaphoreType.DMA((TOKENS_PER_BLOCK // TILE,))],
        compiler_params=pltpu.CompilerParams(vmem_limit_bytes=MIB),
        cost_estimate=pl.CostEstimate(flops=0, bytes_accessed=3 * MIB, transcendentals=0),
        name="chosen_tiles",
    )(order, arrived)


def swapped(x, axes):
    return lax.all_to_all(x, axes, split_axis=0, concat_axis=0, tiled=True)


def shards(
    ssd_input,
    gate_input,
    b_matrix,
    c_matrix,
    log_decay,
    d_skip,
    norm_gain,
    out_weight,
    view_order,
    tile_order,
):
    bands = lax.axis_size(SEQ)
    width_out = out_weight.shape[1]
    x, gate, b, c = (part[0, 0] for part in (ssd_input, gate_input, b_matrix, c_matrix))
    logs = log_decay[0, 0]
    states = swapped(block_states(view_order, logs, b, x), PLANE)
    local, factor, held = local_part(logs, d_skip.reshape(1, H), b, c, x, gate, out_weight)
    totals = swapped(plane_totals(states, local, lax.axis_size("z")), "z")
    entering = swapped(entering_states(states, totals), PLANE).reshape(DI, N)
    projected = projected_tokens(
        entering, c, norm_gain.reshape(1, DI), out_weight, local, factor, held
    )
    arrived = swapped(projected.reshape(bands, TOKENS_PER_BLOCK // bands, width_out), SEQ)
    chosen = chosen_tiles(tile_order, arrived.reshape(TOKENS_PER_BLOCK, width_out))
    return chosen.reshape(1, 1, TOKENS_PER_BLOCK, width_out)


def solution(mesh):
    split = Mesh(mesh.devices.reshape(8, 4, 2, mesh.shape["view"]), (*SEQ, "view"))
    whole = P(SEQ, "view", None, None)
    in_specs = (whole,) * 5 + (P(),) * 3 + (P(SEQ, None),) * 2
    return jax.shard_map(shards, mesh=split, in_specs=in_specs, out_specs=whole, check_vma=False)
```

```python
import functools

import jax
import jax.numpy as jnp
from jax import lax
from jax.experimental import pallas as pl
from jax.experimental.pallas import tpu as pltpu
from jax.sharding import Mesh
from jax.sharding import PartitionSpec as P

H = 32
HEAD = 64
N = 128
TILE = 128
TOKENS_PER_BLOCK = 512
DI = H * HEAD
CHUNK = 128
CHUNKS = TOKENS_PER_BLOCK // CHUNK
COLS = 1024
EPS = 1e-05
SEQ = ("z", "y", "core")
PLANE = ("y", "core", "view")
SUB = 8
PARTS = HEAD // SUB
MESSAGE = (PARTS + 1, SUB, N)
HELD = 512
BF = jnp.bfloat16
F32 = jnp.float32
MIB = 2**20


def dot(a, b, contract=(1, 0)):
    return lax.dot_general(
        a, b, (((contract[0],), (contract[1],)), ((), ())), preferred_element_type=F32
    )


def three_terms(x):
    hi = x.astype(BF).astype(F32)
    rest = x - hi
    mid = rest.astype(BF).astype(F32)
    return hi, mid, rest - mid


def chunk_sums(logs):
    shape = (CHUNK, CHUNK)
    row = lax.broadcasted_iota(jnp.int32, shape, 0)
    column = lax.broadcasted_iota(jnp.int32, shape, 1)
    upto = jnp.where(column <= row, 1.0, 0.0).astype(BF)
    parts = [part.astype(BF) for part in three_terms(logs)]
    return [
        sum(dot(upto, part[:, k * CHUNK : (k + 1) * CHUNK], (1, 1)) for part in parts)
        for k in range(CHUNKS)
    ]


def halves(x):
    hi = x.astype(BF).astype(F32)
    lane = lax.broadcasted_iota(jnp.int32, x.shape, x.ndim - 1)
    return jnp.where(lane < H, hi, x - hi).astype(BF)


def in_hbm(x):
    return pltpu.with_memory_space_constraint(x, pltpu.HBM)


def spread(first_head, columns, copies=2):
    shape = (copies * H, columns)
    head = lax.broadcasted_iota(jnp.int32, shape, 0) % H
    column = lax.broadcasted_iota(jnp.int32, shape, 1) // HEAD + first_head
    return jnp.where(head == column, 1.0, 0.0).astype(BF)


def column_copies(source, target, sems):
    return [
        pltpu.make_async_copy(
            source.at[:, pl.ds(k * COLS, COLS)], target.at[:, pl.ds(k * COLS, COLS)], sems.at[k]
        )
        for k in range(DI // COLS)
    ]


def state_kernel(
    order_hbm, log_hbm, b_hbm, x_hbm, out_ref, order_scr, logs_scr, b_scr, x_scr, sems, x_sems
):
    order_copy = pltpu.make_async_copy(order_hbm, order_scr, sems.at[2])
    log_copy = pltpu.make_async_copy(log_hbm, logs_scr, sems.at[0])
    b_copy = pltpu.make_async_copy(b_hbm, b_scr, sems.at[1])
    x_copies = column_copies(x_hbm, x_scr, x_sems)
    for copy in (log_copy, order_copy, b_copy, *x_copies):
        copy.start()
    log_copy.wait()
    logs = logs_scr[...]
    sums = chunk_sums(jnp.concatenate([logs, logs], axis=0))
    later = jnp.zeros((1, 2 * H), F32)
    weights = []
    for k in reversed(range(CHUNKS)):
        end = sums[k][CHUNK - 1 : CHUNK]
        weights.insert(0, halves(jnp.exp(end - sums[k] + later)))
        later = later + end
    weights = jnp.concatenate(weights, axis=0)

    order_copy.wait()
    order = order_scr[...]
    turn = lax.broadcasted_iota(jnp.int32, order.shape, 1)
    found = jnp.where(order == lax.axis_index("view"), turn, 0)
    rank = jnp.sum(found.astype(F32), axis=1, keepdims=True)[None]
    decay = jnp.broadcast_to(jnp.exp(jnp.sum(logs, axis=1, keepdims=True)), (H, N))
    hi, mid, lo = (part[:, None, :] for part in three_terms(decay))
    place = lax.broadcasted_iota(jnp.int32, (H, SUB, N), 1)
    tail = jnp.where(place == 0, hi, jnp.where(place == 1, mid, jnp.where(place == 2, lo, 0.0)))
    tail = jnp.where(place == 3, rank, tail)
    out_ref[:, PARTS] = tail.astype(BF)

    b_copy.wait()
    b_rows = b_scr[...].astype(F32).T.astype(BF)
    heads = COLS // HEAD
    for k, copy in enumerate(x_copies):
        copy.wait()
        x = x_scr[:, k * COLS : (k + 1) * COLS].astype(F32)
        scaled = (x * dot(weights, spread(k * heads, COLS))).astype(BF)
        state = dot(b_rows, scaled).T.reshape(heads, PARTS, SUB, N)
        out_ref[k * heads : (k + 1) * heads, 0:PARTS] = state.astype(BF)


def block_states(order, logs, b, x):
    anywhere = pl.BlockSpec(memory_space=pl.ANY)
    return pl.pallas_call(
        state_kernel,
        in_specs=[anywhere] * 4,
        out_shape=jax.ShapeDtypeStruct((H, *MESSAGE), BF),
        scratch_shapes=[
            pltpu.VMEM(order.shape, order.dtype),
            pltpu.VMEM(logs.shape, F32),
            pltpu.VMEM(b.shape, BF),
            pltpu.VMEM(x.shape, BF),
            pltpu.SemaphoreType.DMA((3,)),
            pltpu.SemaphoreType.DMA((DI // COLS,)),
        ],
        compiler_params=pltpu.CompilerParams(vmem_limit_bytes=16 * MIB),
        cost_estimate=pl.CostEstimate(flops=2 * 10**9, bytes_accessed=3 * MIB, transcendentals=0),
        name="block_states",
    )(*(in_hbm(part) for part in (order, logs, b, x)))


def read_tail(ref, at):
    tail = ref[at, PARTS].astype(F32)
    return tail[0:1] + tail[1:2] + tail[2:3], tail[3:4]


def read_state(ref, at):
    return ref[at, 0:PARTS].astype(F32).reshape(HEAD, N)


def scan_plane(ref, running, emit):
    views = 4
    product = jnp.ones((1, N), F32)
    for band in range(ref.shape[0] // views):
        blocks = [band * views + v for v in range(views)]
        states = [read_state(ref, k) for k in blocks]
        decays, ranks = zip(*(read_tail(ref, k) for k in blocks))
        entering = [None] * views
        for place in range(views):
            chosen, decay = states[0], decays[0]
            for v in range(views):
                here = ranks[v] == float(place)
                entering[v] = running if place == 0 else jnp.where(here, running, entering[v])
                if v:
                    chosen = jnp.where(here, states[v], chosen)
                    decay = jnp.where(here, decays[v], decay)
            running = decay * running + chosen
            product = product * decay
        if emit is not None:
            for v in range(views):
                emit(blocks[v], entering[v])
    return running, product


def total_kernel(in_ref, token_ref, out_ref):
    total, product = scan_plane(in_ref, jnp.zeros((HEAD, N), F32), None)
    hi, mid, lo = three_terms(product)
    place = lax.broadcasted_iota(jnp.int32, (SUB, N), 0)
    tail = jnp.where(place == 0, hi, jnp.where(place == 1, mid, jnp.where(place == 2, lo, 0.0)))
    for k in range(out_ref.shape[0]):
        out_ref[k, 0:PARTS] = total.reshape(PARTS, SUB, N).astype(BF)
        out_ref[k, PARTS] = tail.astype(BF)


def plane_totals(states, token, planes):
    return pl.pallas_call(
        total_kernel,
        in_specs=[pl.BlockSpec(memory_space=pltpu.VMEM), pl.BlockSpec(memory_space=pl.ANY)],
        out_shape=jax.ShapeDtypeStruct((planes, *MESSAGE), BF),
        compiler_params=pltpu.CompilerParams(vmem_limit_bytes=8 * MIB),
        cost_estimate=pl.CostEstimate(flops=10**6, bytes_accessed=MIB, transcendentals=0),
        name="plane_totals",
    )(states, in_hbm(token))


def entering_kernel(in_ref, totals_ref, out_ref):
    mine = lax.axis_index("z")
    carry = jnp.zeros((HEAD, N), F32)
    for k in range(totals_ref.shape[0] - 1):
        decay, _ = read_tail(totals_ref, k)
        later = decay * carry + read_state(totals_ref, k)
        carry = jnp.where(k < mine, later, carry)

    def emit(block, value):
        out_ref[block, :, :] = value.astype(BF)

    scan_plane(in_ref, carry, emit)


def entering_states(states, totals):
    return pl.pallas_call(
        entering_kernel,
        out_shape=jax.ShapeDtypeStruct((states.shape[0], HEAD, N), BF),
        compiler_params=pltpu.CompilerParams(vmem_limit_bytes=8 * MIB),
        cost_estimate=pl.CostEstimate(flops=10**6, bytes_accessed=2 * MIB, transcendentals=0),
        name="entering_states",
    )(states, totals)


def local_kernel(
    skip_ref, log_hbm, b_hbm, c_hbm, x_hbm, gate_hbm, weight_hbm,
    local_hbm, factor_hbm, held_ref,
    log_scr, b_scr, c_scr, x_scr, gate_scr, local_scr, factor_scr, row_scr,
    sems, x_sems, gate_sems, local_sems, factor_sems,
):
    log_copy = pltpu.make_async_copy(log_hbm, log_scr, sems.at[0])
    b_copy = pltpu.make_async_copy(b_hbm, b_scr, sems.at[1])
    c_copy = pltpu.make_async_copy(c_hbm, c_scr, sems.at[2])
    held_copy = pltpu.make_async_copy(weight_hbm.at[:, pl.ds(0, HELD)], held_ref, sems.at[3])
    x_copies = column_copies(x_hbm, x_scr, x_sems)
    gate_copies = column_copies(gate_hbm, gate_scr, gate_sems)
    local_copies = column_copies(local_scr, local_hbm, local_sems)
    factor_copies = column_copies(factor_scr, factor_hbm, factor_sems)
    for copy in (log_copy, b_copy, c_copy):
        copy.start()
    for pair in zip(x_copies, gate_copies):
        for copy in pair:
            copy.start()
    held_copy.start()

    log_copy.wait()
    logs = log_scr[...]
    sums = chunk_sums(jnp.concatenate([logs, logs], axis=0))
    before = jnp.zeros((1, 2 * H), F32)
    row_scr[...] = jnp.zeros_like(row_scr)
    inward, outward, entered = [], [], []
    for k in range(CHUNKS):
        part = sums[k]
        middle = part[CHUNK // 2 - 1 : CHUNK // 2]
        end = part[CHUNK - 1 : CHUNK]
        inward.append(halves(jnp.exp(middle - part)))
        outward.append(halves(jnp.exp(part - middle)))
        entered.append(halves(jnp.exp(before + part)))
        row_scr[k : k + 1, :] = jnp.exp(end - middle)
        row_scr[4 + k : 5 + k, :] = jnp.exp(middle)
        row_scr[8 + k : 9 + k, :] = jnp.exp(end)
        before = before + end
    ends_once = halves(row_scr[...])
    skips = [part.astype(BF) for part in three_terms(jnp.broadcast_to(skip_ref[...], (16, H)))]

    b_copy.wait()
    c_copy.wait()
    shape = (CHUNK, CHUNK)
    causal = lax.broadcasted_iota(jnp.int32, shape, 1) <= lax.broadcasted_iota(
        jnp.int32, shape, 0
    )
    b_rows, left = [], []
    for k in range(CHUNKS):
        rows = slice(k * CHUNK, (k + 1) * CHUNK)
        b_part, c_part = b_scr[rows, :], c_scr[rows, :]
        b_rows.append(b_part.astype(F32).T.astype(BF))
        scores = jnp.where(causal, dot(c_part, b_part, (1, 1)), 0.0)
        hi = scores.astype(BF)
        lo = (scores - hi.astype(F32)).astype(BF)
        left.append(jnp.concatenate([hi, hi, lo, c_part], axis=1))

    for block in range(DI // COLS):
        columns = slice(block * COLS, (block + 1) * COLS)
        head = block * (COLS // HEAD)
        twice = spread(head, COLS)
        once = spread(head, COLS, 1)
        ends = dot(ends_once, twice)
        skip = sum(dot(part, once) for part in skips)[0:1]
        running = None
        x_copies[block].wait()
        gate_copies[block].wait()
        for k in range(CHUNKS):
            rows = slice(k * CHUNK, (k + 1) * CHUNK)
            x = x_scr[rows, columns].astype(F32)
            exact = x * dot(inward[k], twice)
            scaled = exact.astype(BF)
            right = [scaled, (exact - scaled.astype(F32)).astype(BF), scaled]
            if running is not None:
                right.append((running * ends[4 + k : 5 + k]).astype(BF))
            inner = dot(left[k][:, 0 : CHUNK * len(right)], jnp.concatenate(right, axis=0))
            if k + 1 < CHUNKS:
                made = dot(b_rows[k], scaled) * ends[k : k + 1]
                running = made if running is None else running * ends[8 + k : 9 + k] + made
            half = 0.5 * gate_scr[rows, columns].astype(F32)
            opened = half + half * jnp.tanh(half)
            mixed = inner * dot(outward[k], twice) + skip * x
            local_scr[rows, columns] = (mixed * opened).astype(BF)
            factor_scr[rows, columns] = (dot(entered[k], twice) * opened).astype(BF)
        local_copies[block].start()
        factor_copies[block].start()
    for copy in (held_copy, *local_copies, *factor_copies):
        copy.wait()


def local_part(logs, skip, b, c, x, gate, weight):
    blocks = DI // COLS
    anywhere = pl.BlockSpec(memory_space=pl.ANY)
    return pl.pallas_call(
        local_kernel,
        in_specs=[pl.BlockSpec(memory_space=pltpu.VMEM)] + [anywhere] * 6,
        out_specs=[anywhere, anywhere, pl.BlockSpec(memory_space=pltpu.VMEM)],
        out_shape=[pltpu.HBM(x.shape, BF), pltpu.HBM(x.shape, BF), pltpu.VMEM((DI, HELD), BF)],
        scratch_shapes=[
            pltpu.VMEM(logs.shape, F32),
            pltpu.VMEM(b.shape, BF),
            pltpu.VMEM(c.shape, BF),
            pltpu.VMEM(x.shape, BF),
            pltpu.VMEM(x.shape, BF),
            pltpu.VMEM(x.shape, BF),
            pltpu.VMEM(x.shape, BF),
            pltpu.VMEM((16, 2 * H), F32),
            pltpu.SemaphoreType.DMA((4,)),
            *[pltpu.SemaphoreType.DMA((blocks,))] * 4,
        ],
        compiler_params=pltpu.CompilerParams(vmem_limit_bytes=32 * MIB),
        cost_estimate=pl.CostEstimate(
            flops=8 * 10**9, bytes_accessed=12 * MIB, transcendentals=10**6
        ),
        name="local_part",
    )(skip, *(in_hbm(part) for part in (logs, b, c, x, gate, weight)))


def output_kernel(
    state_ref, c_ref, gain_ref, held_ref, local_hbm, factor_hbm, weight_hbm, out_ref,
    local_ref, factor_ref, weight_ref, normed_scr, row_sems, weight_sem,
):
    width = 256
    half_rows = TOKENS_PER_BLOCK // 2
    shape = (width, width)
    copies = []
    for k in range(2):
        rows = pl.ds(k * half_rows, half_rows)
        group = [
            pltpu.make_async_copy(source.at[rows, :], target.at[rows, :], row_sems.at[k, i])
            for i, (source, target) in enumerate(
                ((local_hbm, local_ref), (factor_hbm, factor_ref))
            )
        ]
        for copy in group:
            copy.start()
        copies.append(group)
    rest = out_ref.shape[1] - HELD
    weight_copy = pltpu.make_async_copy(
        weight_hbm.at[:, pl.ds(HELD, rest)], weight_ref, weight_sem
    )
    weight_copy.start()
    same = (
        lax.broadcasted_iota(jnp.int32, shape, 0) // HEAD
        == lax.broadcasted_iota(jnp.int32, shape, 1) // HEAD
    )
    mean_of = jnp.where(same, 1.0 / HEAD, 0.0).astype(BF)
    for k in range(2):
        for copy in copies[k]:
            copy.wait()
        rows = slice(k * half_rows, (k + 1) * half_rows)
        c = c_ref[rows, :]
        for j in range(DI // width):
            columns = slice(j * width, (j + 1) * width)
            carried = dot(c, state_ref[columns, :], (1, 1))
            gated = local_ref[rows, columns].astype(F32) + factor_ref[rows, columns] * carried
            mean = dot((gated * gated).astype(BF), mean_of)
            normed = gated * (lax.rsqrt(mean + EPS) * gain_ref[:, columns])
            normed_scr[rows, columns] = normed.astype(BF)
    for j in range(HELD // width):
        columns = slice(j * width, (j + 1) * width)
        out_ref[:, columns] = dot(normed_scr[...], held_ref[:, columns]).astype(BF)
    weight_copy.wait()
    for j in range(rest // width):
        columns = slice(j * width, (j + 1) * width)
        made = dot(normed_scr[...], weight_ref[:, columns])
        out_ref[:, HELD + j * width : HELD + (j + 1) * width] = made.astype(BF)


def projected_tokens(state, c, gain, weight, local, factor, held):
    width_out = weight.shape[1]
    vmem, anywhere = pl.BlockSpec(memory_space=pltpu.VMEM), pl.BlockSpec(memory_space=pl.ANY)
    held = pltpu.with_memory_space_constraint(held, pltpu.VMEM)
    return pl.pallas_call(
        output_kernel,
        in_specs=[vmem] * 4 + [anywhere] * 3,
        out_specs=vmem,
        out_shape=jax.ShapeDtypeStruct((TOKENS_PER_BLOCK, width_out), BF),
        scratch_shapes=[
            pltpu.VMEM((TOKENS_PER_BLOCK, DI), BF),
            pltpu.VMEM((TOKENS_PER_BLOCK, DI), BF),
            pltpu.VMEM((DI, width_out - HELD), BF),
            pltpu.VMEM((TOKENS_PER_BLOCK, DI), BF),
            pltpu.SemaphoreType.DMA((2, 2)),
            pltpu.SemaphoreType.DMA,
        ],
        compiler_params=pltpu.CompilerParams(vmem_limit_bytes=28 * MIB),
        cost_estimate=pl.CostEstimate(
            flops=4 * 10**9, bytes_accessed=12 * MIB, transcendentals=10**6
        ),
        name="projected_tokens",
    )(state, c, gain, held, in_hbm(local), in_hbm(factor), in_hbm(weight))


def tile_kernel(order_ref, in_ref, out_ref, sems):
    order = order_ref[...]
    copies = []
    for k in range(TOKENS_PER_BLOCK // TILE):
        source = in_ref.at[pl.ds(pl.multiple_of(order[0, k] * TILE, TILE), TILE), :]
        target = out_ref.at[pl.ds(k * TILE, TILE), :]
        copies.append(pltpu.make_async_copy(source, target, sems.at[k]))
    for copy in copies:
        copy.start()
    for copy in copies:
        copy.wait()


def chosen_tiles(order, arrived):
    return pl.pallas_call(
        tile_kernel,
        in_specs=[pl.BlockSpec(memory_space=pltpu.VMEM), pl.BlockSpec(memory_space=pl.ANY)],
        out_specs=pl.BlockSpec(memory_space=pl.ANY),
        out_shape=jax.ShapeDtypeStruct(arrived.shape, arrived.dtype),
        scratch_shapes=[pltpu.SemaphoreType.DMA((TOKENS_PER_BLOCK // TILE,))],
        compiler_params=pltpu.CompilerParams(vmem_limit_bytes=MIB),
        cost_estimate=pl.CostEstimate(flops=0, bytes_accessed=3 * MIB, transcendentals=0),
        name="chosen_tiles",
    )(order, arrived)


def swapped(x, axes):
    return lax.all_to_all(x, axes, split_axis=0, concat_axis=0, tiled=True)


def shards(
    ssd_input,
    gate_input,
    b_matrix,
    c_matrix,
    log_decay,
    d_skip,
    norm_gain,
    out_weight,
    view_order,
    tile_order,
):
    bands = lax.axis_size(SEQ)
    width_out = out_weight.shape[1]
    x, gate, b, c = (part[0, 0] for part in (ssd_input, gate_input, b_matrix, c_matrix))
    logs = log_decay[0, 0]
    states = swapped(block_states(view_order, logs, b, x), PLANE)
    local, factor, held = local_part(logs, d_skip.reshape(1, H), b, c, x, gate, out_weight)
    totals = swapped(plane_totals(states, local, lax.axis_size("z")), "z")
    entering = swapped(entering_states(states, totals), PLANE).reshape(DI, N)
    projected = projected_tokens(
        entering, c, norm_gain.reshape(1, DI), out_weight, local, factor, held
    )
    arrived = swapped(projected.reshape(bands, TOKENS_PER_BLOCK // bands, width_out), SEQ)
    chosen = chosen_tiles(tile_order, arrived.reshape(TOKENS_PER_BLOCK, width_out))
    return chosen.reshape(1, 1, TOKENS_PER_BLOCK, width_out)


def solution(mesh):
    split = Mesh(mesh.devices.reshape(8, 4, 2, mesh.shape["view"]), (*SEQ, "view"))
    whole = P(SEQ, "view", None, None)
    in_specs = (whole,) * 5 + (P(),) * 3 + (P(SEQ, None),) * 2
    return jax.shard_map(shards, mesh=split, in_specs=in_specs, out_specs=whole, check_vma=False)
```

```python
import functools

import jax
import jax.numpy as jnp
from jax import lax
from jax.experimental import pallas as pl
from jax.experimental.pallas import tpu as pltpu
from jax.sharding import Mesh
from jax.sharding import PartitionSpec as P

H = 32
HEAD = 64
N = 128
TILE = 128
TOKENS_PER_BLOCK = 512
DI = H * HEAD
CHUNK = 128
CHUNKS = TOKENS_PER_BLOCK // CHUNK
COLS = 1024
EPS = 1e-05
SEQ = ("z", "y", "core")
PLANE = ("y", "core", "view")
SUB = 8
PARTS = HEAD // SUB
MESSAGE = (PARTS + 1, SUB, N)
HELD = 512
BF = jnp.bfloat16
F32 = jnp.float32
MIB = 2**20


def dot(a, b, contract=(1, 0)):
    return lax.dot_general(
        a, b, (((contract[0],), (contract[1],)), ((), ())), preferred_element_type=F32
    )


def three_terms(x):
    hi = x.astype(BF).astype(F32)
    rest = x - hi
    mid = rest.astype(BF).astype(F32)
    return hi, mid, rest - mid


def chunk_sums(logs):
    shape = (CHUNK, CHUNK)
    row = lax.broadcasted_iota(jnp.int32, shape, 0)
    column = lax.broadcasted_iota(jnp.int32, shape, 1)
    upto = jnp.where(column <= row, 1.0, 0.0).astype(BF)
    parts = [part.astype(BF) for part in three_terms(logs)]
    return [
        sum(dot(upto, part[:, k * CHUNK : (k + 1) * CHUNK], (1, 1)) for part in parts)
        for k in range(CHUNKS)
    ]


def halves(x):
    hi = x.astype(BF).astype(F32)
    lane = lax.broadcasted_iota(jnp.int32, x.shape, x.ndim - 1)
    return jnp.where(lane < H, hi, x - hi).astype(BF)


def in_hbm(x):
    return pltpu.with_memory_space_constraint(x, pltpu.HBM)


def spread(first_head, columns, copies=2):
    shape = (copies * H, columns)
    head = lax.broadcasted_iota(jnp.int32, shape, 0) % H
    column = lax.broadcasted_iota(jnp.int32, shape, 1) // HEAD + first_head
    return jnp.where(head == column, 1.0, 0.0).astype(BF)


def column_copies(source, target, sems):
    return [
        pltpu.make_async_copy(
            source.at[:, pl.ds(k * COLS, COLS)], target.at[:, pl.ds(k * COLS, COLS)], sems.at[k]
        )
        for k in range(DI // COLS)
    ]


def state_kernel(
    order_hbm, log_hbm, b_hbm, x_hbm, out_ref, sums_ref,
    order_scr, logs_scr, b_scr, x_scr, sems, x_sems,
):
    order_copy = pltpu.make_async_copy(order_hbm, order_scr, sems.at[2])
    log_copy = pltpu.make_async_copy(log_hbm, logs_scr, sems.at[0])
    b_copy = pltpu.make_async_copy(b_hbm, b_scr, sems.at[1])
    x_copies = column_copies(x_hbm, x_scr, x_sems)
    for copy in (log_copy, order_copy, b_copy, *x_copies):
        copy.start()
    log_copy.wait()
    logs = logs_scr[...]
    sums = chunk_sums(jnp.concatenate([logs, logs], axis=0))
    later = jnp.zeros((1, 2 * H), F32)
    weights = []
    for k in reversed(range(CHUNKS)):
        sums_ref[k * CHUNK : (k + 1) * CHUNK, :] = sums[k]
        end = sums[k][CHUNK - 1 : CHUNK]
        weights.insert(0, halves(jnp.exp(end - sums[k] + later)))
        later = later + end
    weights = jnp.concatenate(weights, axis=0)

    order_copy.wait()
    order = order_scr[...]
    turn = lax.broadcasted_iota(jnp.int32, order.shape, 1)
    found = jnp.where(order == lax.axis_index("view"), turn, 0)
    rank = jnp.sum(found.astype(F32), axis=1, keepdims=True)[None]
    decay = jnp.broadcast_to(jnp.exp(jnp.sum(logs, axis=1, keepdims=True)), (H, N))
    hi, mid, lo = (part[:, None, :] for part in three_terms(decay))
    place = lax.broadcasted_iota(jnp.int32, (H, SUB, N), 1)
    tail = jnp.where(place == 0, hi, jnp.where(place == 1, mid, jnp.where(place == 2, lo, 0.0)))
    tail = jnp.where(place == 3, rank, tail)
    out_ref[:, PARTS] = tail.astype(BF)

    b_copy.wait()
    b_rows = b_scr[...].astype(F32).T.astype(BF)
    heads = COLS // HEAD
    for k, copy in enumerate(x_copies):
        copy.wait()
        x = x_scr[:, k * COLS : (k + 1) * COLS].astype(F32)
        scaled = (x * dot(weights, spread(k * heads, COLS))).astype(BF)
        state = dot(b_rows, scaled).T.reshape(heads, PARTS, SUB, N)
        out_ref[k * heads : (k + 1) * heads, 0:PARTS] = state.astype(BF)


def block_states(order, logs, b, x):
    anywhere = pl.BlockSpec(memory_space=pl.ANY)
    return pl.pallas_call(
        state_kernel,
        in_specs=[anywhere] * 4,
        out_specs=[pl.BlockSpec(), pl.BlockSpec(memory_space=pltpu.VMEM)],
        out_shape=[
            jax.ShapeDtypeStruct((H, *MESSAGE), BF),
            pltpu.VMEM((TOKENS_PER_BLOCK, 2 * H), F32),
        ],
        scratch_shapes=[
            pltpu.VMEM(order.shape, order.dtype),
            pltpu.VMEM(logs.shape, F32),
            pltpu.VMEM(b.shape, BF),
            pltpu.VMEM(x.shape, BF),
            pltpu.SemaphoreType.DMA((3,)),
            pltpu.SemaphoreType.DMA((DI // COLS,)),
        ],
        compiler_params=pltpu.CompilerParams(vmem_limit_bytes=16 * MIB),
        cost_estimate=pl.CostEstimate(flops=2 * 10**9, bytes_accessed=3 * MIB, transcendentals=0),
        name="block_states",
    )(*(in_hbm(part) for part in (order, logs, b, x)))


def read_tail(ref, at):
    tail = ref[at, PARTS].astype(F32)
    return tail[0:1] + tail[1:2] + tail[2:3], tail[3:4]


def read_state(ref, at):
    return ref[at, 0:PARTS].astype(F32).reshape(HEAD, N)


def scan_plane(ref, running, emit):
    views = 4
    product = jnp.ones((1, N), F32)
    for band in range(ref.shape[0] // views):
        blocks = [band * views + v for v in range(views)]
        states = [read_state(ref, k) for k in blocks]
        decays, ranks = zip(*(read_tail(ref, k) for k in blocks))
        entering = [None] * views
        for place in range(views):
            chosen, decay = states[0], decays[0]
            for v in range(views):
                here = ranks[v] == float(place)
                entering[v] = running if place == 0 else jnp.where(here, running, entering[v])
                if v:
                    chosen = jnp.where(here, states[v], chosen)
                    decay = jnp.where(here, decays[v], decay)
            running = decay * running + chosen
            product = product * decay
        if emit is not None:
            for v in range(views):
                emit(blocks[v], entering[v])
    return running, product


def total_kernel(in_ref, token_ref, out_ref):
    total, product = scan_plane(in_ref, jnp.zeros((HEAD, N), F32), None)
    hi, mid, lo = three_terms(product)
    place = lax.broadcasted_iota(jnp.int32, (SUB, N), 0)
    tail = jnp.where(place == 0, hi, jnp.where(place == 1, mid, jnp.where(place == 2, lo, 0.0)))
    for k in range(out_ref.shape[0]):
        out_ref[k, 0:PARTS] = total.reshape(PARTS, SUB, N).astype(BF)
        out_ref[k, PARTS] = tail.astype(BF)


def plane_totals(states, token, planes):
    return pl.pallas_call(
        total_kernel,
        in_specs=[pl.BlockSpec(memory_space=pltpu.VMEM), pl.BlockSpec(memory_space=pl.ANY)],
        out_shape=jax.ShapeDtypeStruct((planes, *MESSAGE), BF),
        compiler_params=pltpu.CompilerParams(vmem_limit_bytes=8 * MIB),
        cost_estimate=pl.CostEstimate(flops=10**6, bytes_accessed=MIB, transcendentals=0),
        name="plane_totals",
    )(states, in_hbm(token))


def entering_kernel(in_ref, totals_ref, out_ref):
    mine = lax.axis_index("z")
    carry = jnp.zeros((HEAD, N), F32)
    for k in range(totals_ref.shape[0] - 1):
        decay, _ = read_tail(totals_ref, k)
        later = decay * carry + read_state(totals_ref, k)
        carry = jnp.where(k < mine, later, carry)

    def emit(block, value):
        out_ref[block, :, :] = value.astype(BF)

    scan_plane(in_ref, carry, emit)


def entering_states(states, totals):
    return pl.pallas_call(
        entering_kernel,
        out_shape=jax.ShapeDtypeStruct((states.shape[0], HEAD, N), BF),
        compiler_params=pltpu.CompilerParams(vmem_limit_bytes=8 * MIB),
        cost_estimate=pl.CostEstimate(flops=10**6, bytes_accessed=2 * MIB, transcendentals=0),
        name="entering_states",
    )(states, totals)


def local_kernel(
    skip_ref, sums_ref, b_hbm, c_hbm, x_hbm, gate_hbm, weight_hbm,
    local_hbm, factor_hbm, held_ref,
    b_scr, c_scr, x_scr, gate_scr, local_scr, factor_scr, row_scr,
    sems, x_sems, gate_sems, local_sems, factor_sems,
):
    b_copy = pltpu.make_async_copy(b_hbm, b_scr, sems.at[1])
    c_copy = pltpu.make_async_copy(c_hbm, c_scr, sems.at[2])
    held_copy = pltpu.make_async_copy(weight_hbm.at[:, pl.ds(0, HELD)], held_ref, sems.at[3])
    x_copies = column_copies(x_hbm, x_scr, x_sems)
    gate_copies = column_copies(gate_hbm, gate_scr, gate_sems)
    local_copies = column_copies(local_scr, local_hbm, local_sems)
    factor_copies = column_copies(factor_scr, factor_hbm, factor_sems)
    for copy in (b_copy, c_copy):
        copy.start()
    for pair in zip(x_copies, gate_copies):
        for copy in pair:
            copy.start()
    held_copy.start()

    before = jnp.zeros((1, 2 * H), F32)
    row_scr[...] = jnp.zeros_like(row_scr)
    inward, outward, entered = [], [], []
    for k in range(CHUNKS):
        part = sums_ref[k * CHUNK : (k + 1) * CHUNK, :]
        middle = part[CHUNK // 2 - 1 : CHUNK // 2]
        end = part[CHUNK - 1 : CHUNK]
        inward.append(halves(jnp.exp(middle - part)))
        outward.append(halves(jnp.exp(part - middle)))
        entered.append(halves(jnp.exp(before + part)))
        row_scr[k : k + 1, :] = jnp.exp(end - middle)
        row_scr[4 + k : 5 + k, :] = jnp.exp(middle)
        row_scr[8 + k : 9 + k, :] = jnp.exp(end)
        before = before + end
    ends_once = halves(row_scr[...])
    skips = [part.astype(BF) for part in three_terms(jnp.broadcast_to(skip_ref[...], (16, H)))]

    b_copy.wait()
    c_copy.wait()
    shape = (CHUNK, CHUNK)
    causal = lax.broadcasted_iota(jnp.int32, shape, 1) <= lax.broadcasted_iota(
        jnp.int32, shape, 0
    )
    b_rows, left = [], []
    for k in range(CHUNKS):
        rows = slice(k * CHUNK, (k + 1) * CHUNK)
        b_part, c_part = b_scr[rows, :], c_scr[rows, :]
        b_rows.append(b_part.astype(F32).T.astype(BF))
        scores = jnp.where(causal, dot(c_part, b_part, (1, 1)), 0.0)
        left.append(jnp.concatenate([scores.astype(BF), c_part], axis=1))

    for block in range(DI // COLS):
        columns = slice(block * COLS, (block + 1) * COLS)
        head = block * (COLS // HEAD)
        twice = spread(head, COLS)
        once = spread(head, COLS, 1)
        ends = dot(ends_once, twice)
        skip = sum(dot(part, once) for part in skips)[0:1]
        running = None
        x_copies[block].wait()
        gate_copies[block].wait()
        for k in range(CHUNKS):
            rows = slice(k * CHUNK, (k + 1) * CHUNK)
            x = x_scr[rows, columns].astype(F32)
            scaled = (x * dot(inward[k], twice)).astype(BF)
            right = [scaled]
            if running is not None:
                right.append((running * ends[4 + k : 5 + k]).astype(BF))
            inner = dot(left[k][:, 0 : CHUNK * len(right)], jnp.concatenate(right, axis=0))
            if k + 1 < CHUNKS:
                made = dot(b_rows[k], scaled) * ends[k : k + 1]
                running = made if running is None else running * ends[8 + k : 9 + k] + made
            half = 0.5 * gate_scr[rows, columns].astype(F32)
            opened = half + half * jnp.tanh(half)
            mixed = inner * dot(outward[k], twice) + skip * x
            local_scr[rows, columns] = (mixed * opened).astype(BF)
            factor_scr[rows, columns] = (dot(entered[k], twice) * opened).astype(BF)
        local_copies[block].start()
        factor_copies[block].start()
    for copy in (held_copy, *local_copies, *factor_copies):
        copy.wait()


def local_part(skip, sums, b, c, x, gate, weight):
    blocks = DI // COLS
    anywhere = pl.BlockSpec(memory_space=pl.ANY)
    return pl.pallas_call(
        local_kernel,
        in_specs=[pl.BlockSpec(memory_space=pltpu.VMEM)] * 2 + [anywhere] * 5,
        out_specs=[anywhere, anywhere, pl.BlockSpec(memory_space=pltpu.VMEM)],
        out_shape=[pltpu.HBM(x.shape, BF), pltpu.HBM(x.shape, BF), pltpu.VMEM((DI, HELD), BF)],
        scratch_shapes=[
            pltpu.VMEM(b.shape, BF),
            pltpu.VMEM(c.shape, BF),
            pltpu.VMEM(x.shape, BF),
            pltpu.VMEM(x.shape, BF),
            pltpu.VMEM(x.shape, BF),
            pltpu.VMEM(x.shape, BF),
            pltpu.VMEM((16, 2 * H), F32),
            pltpu.SemaphoreType.DMA((4,)),
            *[pltpu.SemaphoreType.DMA((blocks,))] * 4,
        ],
        compiler_params=pltpu.CompilerParams(vmem_limit_bytes=32 * MIB),
        cost_estimate=pl.CostEstimate(
            flops=8 * 10**9, bytes_accessed=12 * MIB, transcendentals=10**6
        ),
        name="local_part",
    )(
        skip,
        pltpu.with_memory_space_constraint(sums, pltpu.VMEM),
        *(in_hbm(part) for part in (b, c, x, gate, weight)),
    )


def output_kernel(
    state_ref, c_ref, gain_ref, held_ref, local_hbm, factor_hbm, weight_hbm, out_ref,
    local_ref, factor_ref, weight_ref, normed_scr, row_sems, weight_sem,
):
    width = 256
    half_rows = TOKENS_PER_BLOCK // 2
    shape = (width, width)
    copies = []
    for k in range(2):
        rows = pl.ds(k * half_rows, half_rows)
        group = [
            pltpu.make_async_copy(source.at[rows, :], target.at[rows, :], row_sems.at[k, i])
            for i, (source, target) in enumerate(
                ((local_hbm, local_ref), (factor_hbm, factor_ref))
            )
        ]
        for copy in group:
            copy.start()
        copies.append(group)
    rest = out_ref.shape[1] - HELD
    weight_copy = pltpu.make_async_copy(
        weight_hbm.at[:, pl.ds(HELD, rest)], weight_ref, weight_sem
    )
    weight_copy.start()
    same = (
        lax.broadcasted_iota(jnp.int32, shape, 0) // HEAD
        == lax.broadcasted_iota(jnp.int32, shape, 1) // HEAD
    )
    mean_of = jnp.where(same, 1.0 / HEAD, 0.0).astype(BF)
    for k in range(2):
        for copy in copies[k]:
            copy.wait()
        rows = slice(k * half_rows, (k + 1) * half_rows)
        c = c_ref[rows, :]
        for j in range(DI // width):
            columns = slice(j * width, (j + 1) * width)
            carried = dot(c, state_ref[columns, :], (1, 1))
            gated = local_ref[rows, columns].astype(F32) + factor_ref[rows, columns] * carried
            mean = dot((gated * gated).astype(BF), mean_of)
            normed = gated * (lax.rsqrt(mean + EPS) * gain_ref[:, columns])
            normed_scr[rows, columns] = normed.astype(BF)
    for j in range(HELD // width):
        columns = slice(j * width, (j + 1) * width)
        out_ref[:, columns] = dot(normed_scr[...], held_ref[:, columns]).astype(BF)
    weight_copy.wait()
    for j in range(rest // width):
        columns = slice(j * width, (j + 1) * width)
        made = dot(normed_scr[...], weight_ref[:, columns])
        out_ref[:, HELD + j * width : HELD + (j + 1) * width] = made.astype(BF)


def projected_tokens(state, c, gain, weight, local, factor, held):
    width_out = weight.shape[1]
    vmem, anywhere = pl.BlockSpec(memory_space=pltpu.VMEM), pl.BlockSpec(memory_space=pl.ANY)
    held = pltpu.with_memory_space_constraint(held, pltpu.VMEM)
    return pl.pallas_call(
        output_kernel,
        in_specs=[vmem] * 4 + [anywhere] * 3,
        out_specs=vmem,
        out_shape=jax.ShapeDtypeStruct((TOKENS_PER_BLOCK, width_out), BF),
        scratch_shapes=[
            pltpu.VMEM((TOKENS_PER_BLOCK, DI), BF),
            pltpu.VMEM((TOKENS_PER_BLOCK, DI), BF),
            pltpu.VMEM((DI, width_out - HELD), BF),
            pltpu.VMEM((TOKENS_PER_BLOCK, DI), BF),
            pltpu.SemaphoreType.DMA((2, 2)),
            pltpu.SemaphoreType.DMA,
        ],
        compiler_params=pltpu.CompilerParams(vmem_limit_bytes=28 * MIB),
        cost_estimate=pl.CostEstimate(
            flops=4 * 10**9, bytes_accessed=12 * MIB, transcendentals=10**6
        ),
        name="projected_tokens",
    )(state, c, gain, held, in_hbm(local), in_hbm(factor), in_hbm(weight))


def tile_kernel(order_ref, in_ref, out_ref, sems):
    order = order_ref[...]
    copies = []
    for k in range(TOKENS_PER_BLOCK // TILE):
        source = in_ref.at[pl.ds(pl.multiple_of(order[0, k] * TILE, TILE), TILE), :]
        target = out_ref.at[pl.ds(k * TILE, TILE), :]
        copies.append(pltpu.make_async_copy(source, target, sems.at[k]))
    for copy in copies:
        copy.start()
    for copy in copies:
        copy.wait()


def chosen_tiles(order, arrived):
    return pl.pallas_call(
        tile_kernel,
        in_specs=[pl.BlockSpec(memory_space=pltpu.VMEM), pl.BlockSpec(memory_space=pl.ANY)],
        out_specs=pl.BlockSpec(memory_space=pl.ANY),
        out_shape=jax.ShapeDtypeStruct(arrived.shape, arrived.dtype),
        scratch_shapes=[pltpu.SemaphoreType.DMA((TOKENS_PER_BLOCK // TILE,))],
        compiler_params=pltpu.CompilerParams(vmem_limit_bytes=MIB),
        cost_estimate=pl.CostEstimate(flops=0, bytes_accessed=3 * MIB, transcendentals=0),
        name="chosen_tiles",
    )(order, arrived)


def swapped(x, axes):
    return lax.all_to_all(x, axes, split_axis=0, concat_axis=0, tiled=True)


def shards(
    ssd_input,
    gate_input,
    b_matrix,
    c_matrix,
    log_decay,
    d_skip,
    norm_gain,
    out_weight,
    view_order,
    tile_order,
):
    bands = lax.axis_size(SEQ)
    width_out = out_weight.shape[1]
    x, gate, b, c = (part[0, 0] for part in (ssd_input, gate_input, b_matrix, c_matrix))
    logs = log_decay[0, 0]
    states, sums = block_states(view_order, logs, b, x)
    states = swapped(states, PLANE)
    local, factor, held = local_part(d_skip.reshape(1, H), sums, b, c, x, gate, out_weight)
    totals = swapped(plane_totals(states, local, lax.axis_size("z")), "z")
    entering = swapped(entering_states(states, totals), PLANE).reshape(DI, N)
    projected = projected_tokens(
        entering, c, norm_gain.reshape(1, DI), out_weight, local, factor, held
    )
    arrived = swapped(projected.reshape(bands, TOKENS_PER_BLOCK // bands, width_out), SEQ)
    chosen = chosen_tiles(tile_order, arrived.reshape(TOKENS_PER_BLOCK, width_out))
    return chosen.reshape(1, 1, TOKENS_PER_BLOCK, width_out)


def solution(mesh):
    split = Mesh(mesh.devices.reshape(8, 4, 2, mesh.shape["view"]), (*SEQ, "view"))
    whole = P(SEQ, "view", None, None)
    in_specs = (whole,) * 5 + (P(),) * 3 + (P(SEQ, None),) * 2
    return jax.shard_map(shards, mesh=split, in_specs=in_specs, out_specs=whole, check_vma=False)
```

```python
import functools

import jax
import jax.numpy as jnp
from jax import lax
from jax.experimental import pallas as pl
from jax.experimental.pallas import tpu as pltpu
from jax.sharding import Mesh
from jax.sharding import PartitionSpec as P

H = 32
HEAD = 64
N = 128
TILE = 128
TOKENS_PER_BLOCK = 512
RETURN_PARTS = 4
DI = H * HEAD
CHUNK = 128
CHUNKS = TOKENS_PER_BLOCK // CHUNK
COLS = 1024
EPS = 1e-05
SEQ = ("z", "y", "core")
PLANE = ("y", "core", "view")
SUB = 8
PARTS = HEAD // SUB
MESSAGE = (PARTS + 1, SUB, N)
HELD = 512
BF = jnp.bfloat16
F32 = jnp.float32
MIB = 2**20


def dot(a, b, contract=(1, 0)):
    return lax.dot_general(
        a, b, (((contract[0],), (contract[1],)), ((), ())), preferred_element_type=F32
    )


def three_terms(x):
    hi = x.astype(BF).astype(F32)
    rest = x - hi
    mid = rest.astype(BF).astype(F32)
    return hi, mid, rest - mid


def chunk_sums(logs):
    shape = (CHUNK, CHUNK)
    row = lax.broadcasted_iota(jnp.int32, shape, 0)
    column = lax.broadcasted_iota(jnp.int32, shape, 1)
    upto = jnp.where(column <= row, 1.0, 0.0).astype(BF)
    parts = [part.astype(BF) for part in three_terms(logs)]
    return [
        sum(dot(upto, part[:, k * CHUNK : (k + 1) * CHUNK], (1, 1)) for part in parts)
        for k in range(CHUNKS)
    ]


def halves(x):
    hi = x.astype(BF).astype(F32)
    lane = lax.broadcasted_iota(jnp.int32, x.shape, x.ndim - 1)
    return jnp.where(lane < H, hi, x - hi).astype(BF)


def in_hbm(x):
    return pltpu.with_memory_space_constraint(x, pltpu.HBM)


def spread(first_head, columns, copies=2):
    shape = (copies * H, columns)
    head = lax.broadcasted_iota(jnp.int32, shape, 0) % H
    column = lax.broadcasted_iota(jnp.int32, shape, 1) // HEAD + first_head
    return jnp.where(head == column, 1.0, 0.0).astype(BF)


def column_copies(source, target, sems):
    return [
        pltpu.make_async_copy(
            source.at[:, pl.ds(k * COLS, COLS)], target.at[:, pl.ds(k * COLS, COLS)], sems.at[k]
        )
        for k in range(DI // COLS)
    ]


def state_kernel(
    order_hbm, log_hbm, b_hbm, x_hbm, out_ref, sums_ref,
    order_scr, logs_scr, b_scr, x_scr, sems, x_sems,
):
    order_copy = pltpu.make_async_copy(order_hbm, order_scr, sems.at[2])
    log_copy = pltpu.make_async_copy(log_hbm, logs_scr, sems.at[0])
    b_copy = pltpu.make_async_copy(b_hbm, b_scr, sems.at[1])
    x_copies = column_copies(x_hbm, x_scr, x_sems)
    for copy in (log_copy, order_copy, b_copy, *x_copies):
        copy.start()
    log_copy.wait()
    logs = logs_scr[...]
    sums = chunk_sums(jnp.concatenate([logs, logs], axis=0))
    later = jnp.zeros((1, 2 * H), F32)
    weights = []
    for k in reversed(range(CHUNKS)):
        sums_ref[k * CHUNK : (k + 1) * CHUNK, :] = sums[k]
        end = sums[k][CHUNK - 1 : CHUNK]
        weights.insert(0, halves(jnp.exp(end - sums[k] + later)))
        later = later + end
    weights = jnp.concatenate(weights, axis=0)

    order_copy.wait()
    order = order_scr[...]
    turn = lax.broadcasted_iota(jnp.int32, order.shape, 1)
    found = jnp.where(order == lax.axis_index("view"), turn, 0)
    rank = jnp.sum(found.astype(F32), axis=1, keepdims=True)[None]
    decay = jnp.broadcast_to(jnp.exp(jnp.sum(logs, axis=1, keepdims=True)), (H, N))
    hi, mid, lo = (part[:, None, :] for part in three_terms(decay))
    place = lax.broadcasted_iota(jnp.int32, (H, SUB, N), 1)
    tail = jnp.where(place == 0, hi, jnp.where(place == 1, mid, jnp.where(place == 2, lo, 0.0)))
    tail = jnp.where(place == 3, rank, tail)
    out_ref[:, PARTS] = tail.astype(BF)

    b_copy.wait()
    b_rows = b_scr[...].astype(F32).T.astype(BF)
    heads = COLS // HEAD
    for k, copy in enumerate(x_copies):
        copy.wait()
        x = x_scr[:, k * COLS : (k + 1) * COLS].astype(F32)
        scaled = (x * dot(weights, spread(k * heads, COLS))).astype(BF)
        state = dot(b_rows, scaled).T.reshape(heads, PARTS, SUB, N)
        out_ref[k * heads : (k + 1) * heads, 0:PARTS] = state.astype(BF)


def block_states(order, logs, b, x):
    anywhere = pl.BlockSpec(memory_space=pl.ANY)
    return pl.pallas_call(
        state_kernel,
        in_specs=[anywhere] * 4,
        out_specs=[pl.BlockSpec(), pl.BlockSpec(memory_space=pltpu.VMEM)],
        out_shape=[
            jax.ShapeDtypeStruct((H, *MESSAGE), BF),
            pltpu.VMEM((TOKENS_PER_BLOCK, 2 * H), F32),
        ],
        scratch_shapes=[
            pltpu.VMEM(order.shape, order.dtype),
            pltpu.VMEM(logs.shape, F32),
            pltpu.VMEM(b.shape, BF),
            pltpu.VMEM(x.shape, BF),
            pltpu.SemaphoreType.DMA((3,)),
            pltpu.SemaphoreType.DMA((DI // COLS,)),
        ],
        compiler_params=pltpu.CompilerParams(vmem_limit_bytes=16 * MIB),
        cost_estimate=pl.CostEstimate(flops=2 * 10**9, bytes_accessed=3 * MIB, transcendentals=0),
        name="block_states",
    )(*(in_hbm(part) for part in (order, logs, b, x)))


def read_tail(ref, at):
    tail = ref[at, PARTS].astype(F32)
    return tail[0:1] + tail[1:2] + tail[2:3], tail[3:4]


def read_state(ref, at):
    return ref[at, 0:PARTS].astype(F32).reshape(HEAD, N)


def scan_plane(ref, running, emit):
    views = 4
    product = jnp.ones((1, N), F32)
    for band in range(ref.shape[0] // views):
        blocks = [band * views + v for v in range(views)]
        states = [read_state(ref, k) for k in blocks]
        decays, ranks = zip(*(read_tail(ref, k) for k in blocks))
        entering = [None] * views
        for place in range(views):
            chosen, decay = states[0], decays[0]
            for v in range(views):
                here = ranks[v] == float(place)
                entering[v] = running if place == 0 else jnp.where(here, running, entering[v])
                if v:
                    chosen = jnp.where(here, states[v], chosen)
                    decay = jnp.where(here, decays[v], decay)
            running = decay * running + chosen
            product = product * decay
        if emit is not None:
            for v in range(views):
                emit(blocks[v], entering[v])
    return running, product


def total_kernel(in_ref, out_ref):
    total, product = scan_plane(in_ref, jnp.zeros((HEAD, N), F32), None)
    hi, mid, lo = three_terms(product)
    place = lax.broadcasted_iota(jnp.int32, (SUB, N), 0)
    tail = jnp.where(place == 0, hi, jnp.where(place == 1, mid, jnp.where(place == 2, lo, 0.0)))
    for k in range(out_ref.shape[0]):
        out_ref[k, 0:PARTS] = total.reshape(PARTS, SUB, N).astype(BF)
        out_ref[k, PARTS] = tail.astype(BF)


def plane_totals(states, planes):
    return pl.pallas_call(
        total_kernel,
        out_shape=jax.ShapeDtypeStruct((planes, *MESSAGE), BF),
        compiler_params=pltpu.CompilerParams(vmem_limit_bytes=8 * MIB),
        cost_estimate=pl.CostEstimate(flops=10**6, bytes_accessed=MIB, transcendentals=0),
        name="plane_totals",
    )(states)


def entering_kernel(in_ref, totals_ref, out_hbm, out_ref, sems):
    mine = lax.axis_index("z")
    carry = jnp.zeros((HEAD, N), F32)
    for k in range(totals_ref.shape[0] - 1):
        decay, _ = read_tail(totals_ref, k)
        later = decay * carry + read_state(totals_ref, k)
        carry = jnp.where(k < mine, later, carry)

    group = in_ref.shape[0] // RETURN_PARTS
    copies = []
    for k in range(RETURN_PARTS):
        blocks = pl.ds(k * group, group)
        copies.append(pltpu.make_async_copy(out_ref.at[blocks], out_hbm.at[blocks], sems.at[k]))

    def emit(block, value):
        out_ref[block, :, :] = value.astype(BF)
        if block % group == group - 1:
            copies[block // group].start()

    scan_plane(in_ref, carry, emit)
    for copy in copies:
        copy.wait()


def entering_states(states, totals):
    return pl.pallas_call(
        entering_kernel,
        out_specs=pl.BlockSpec(memory_space=pl.ANY),
        out_shape=pltpu.HBM((states.shape[0], HEAD, N), BF),
        scratch_shapes=[
            pltpu.VMEM((states.shape[0], HEAD, N), BF),
            pltpu.SemaphoreType.DMA((RETURN_PARTS,)),
        ],
        compiler_params=pltpu.CompilerParams(vmem_limit_bytes=8 * MIB),
        cost_estimate=pl.CostEstimate(flops=10**6, bytes_accessed=2 * MIB, transcendentals=0),
        name="entering_states",
    )(states, totals)


def local_kernel(
    after_ref, skip_ref, sums_ref, b_hbm, c_hbm, x_hbm, gate_hbm, weight_hbm,
    local_hbm, factor_hbm, held_ref,
    b_scr, c_scr, x_scr, gate_scr, local_scr, factor_scr, row_scr,
    sems, x_sems, gate_sems, local_sems, factor_sems,
):
    b_copy = pltpu.make_async_copy(b_hbm, b_scr, sems.at[1])
    c_copy = pltpu.make_async_copy(c_hbm, c_scr, sems.at[2])
    held_copy = pltpu.make_async_copy(weight_hbm.at[:, pl.ds(0, HELD)], held_ref, sems.at[3])
    x_copies = column_copies(x_hbm, x_scr, x_sems)
    gate_copies = column_copies(gate_hbm, gate_scr, gate_sems)
    local_copies = column_copies(local_scr, local_hbm, local_sems)
    factor_copies = column_copies(factor_scr, factor_hbm, factor_sems)
    for copy in (b_copy, c_copy):
        copy.start()
    for pair in zip(x_copies, gate_copies):
        for copy in pair:
            copy.start()
    held_copy.start()

    before = jnp.zeros((1, 2 * H), F32)
    row_scr[...] = jnp.zeros_like(row_scr)
    inward, outward, entered = [], [], []
    for k in range(CHUNKS):
        part = sums_ref[k * CHUNK : (k + 1) * CHUNK, :]
        middle = part[CHUNK // 2 - 1 : CHUNK // 2]
        end = part[CHUNK - 1 : CHUNK]
        inward.append(halves(jnp.exp(middle - part)))
        outward.append(halves(jnp.exp(part - middle)))
        entered.append(halves(jnp.exp(before + part)))
        row_scr[k : k + 1, :] = jnp.exp(end - middle)
        row_scr[4 + k : 5 + k, :] = jnp.exp(middle)
        row_scr[8 + k : 9 + k, :] = jnp.exp(end)
        before = before + end
    ends_once = halves(row_scr[...])
    skips = [part.astype(BF) for part in three_terms(jnp.broadcast_to(skip_ref[...], (16, H)))]

    b_copy.wait()
    c_copy.wait()
    shape = (CHUNK, CHUNK)
    causal = lax.broadcasted_iota(jnp.int32, shape, 1) <= lax.broadcasted_iota(
        jnp.int32, shape, 0
    )
    b_rows, left = [], []
    for k in range(CHUNKS):
        rows = slice(k * CHUNK, (k + 1) * CHUNK)
        b_part, c_part = b_scr[rows, :], c_scr[rows, :]
        b_rows.append(b_part.astype(F32).T.astype(BF))
        scores = jnp.where(causal, dot(c_part, b_part, (1, 1)), 0.0)
        left.append(jnp.concatenate([scores.astype(BF), c_part], axis=1))

    for block in range(DI // COLS):
        columns = slice(block * COLS, (block + 1) * COLS)
        head = block * (COLS // HEAD)
        twice = spread(head, COLS)
        once = spread(head, COLS, 1)
        ends = dot(ends_once, twice)
        skip = sum(dot(part, once) for part in skips)[0:1]
        running = None
        x_copies[block].wait()
        gate_copies[block].wait()
        for k in range(CHUNKS):
            rows = slice(k * CHUNK, (k + 1) * CHUNK)
            x = x_scr[rows, columns].astype(F32)
            scaled = (x * dot(inward[k], twice)).astype(BF)
            right = [scaled]
            if running is not None:
                right.append((running * ends[4 + k : 5 + k]).astype(BF))
            inner = dot(left[k][:, 0 : CHUNK * len(right)], jnp.concatenate(right, axis=0))
            if k + 1 < CHUNKS:
                made = dot(b_rows[k], scaled) * ends[k : k + 1]
                running = made if running is None else running * ends[8 + k : 9 + k] + made
            half = 0.5 * gate_scr[rows, columns].astype(F32)
            opened = half + half * jnp.tanh(half)
            mixed = inner * dot(outward[k], twice) + skip * x
            local_scr[rows, columns] = (mixed * opened).astype(BF)
            factor_scr[rows, columns] = (dot(entered[k], twice) * opened).astype(BF)
        local_copies[block].start()
        factor_copies[block].start()
    for copy in (held_copy, *local_copies, *factor_copies):
        copy.wait()


def local_part(after, skip, sums, b, c, x, gate, weight):
    blocks = DI // COLS
    anywhere = pl.BlockSpec(memory_space=pl.ANY)
    return pl.pallas_call(
        local_kernel,
        in_specs=[anywhere] + [pl.BlockSpec(memory_space=pltpu.VMEM)] * 2 + [anywhere] * 5,
        out_specs=[anywhere, anywhere, pl.BlockSpec(memory_space=pltpu.VMEM)],
        out_shape=[pltpu.HBM(x.shape, BF), pltpu.HBM(x.shape, BF), pltpu.VMEM((DI, HELD), BF)],
        scratch_shapes=[
            pltpu.VMEM(b.shape, BF),
            pltpu.VMEM(c.shape, BF),
            pltpu.VMEM(x.shape, BF),
            pltpu.VMEM(x.shape, BF),
            pltpu.VMEM(x.shape, BF),
            pltpu.VMEM(x.shape, BF),
            pltpu.VMEM((16, 2 * H), F32),
            pltpu.SemaphoreType.DMA((4,)),
            *[pltpu.SemaphoreType.DMA((blocks,))] * 4,
        ],
        compiler_params=pltpu.CompilerParams(vmem_limit_bytes=32 * MIB),
        cost_estimate=pl.CostEstimate(
            flops=8 * 10**9, bytes_accessed=12 * MIB, transcendentals=10**6
        ),
        name="local_part",
    )(
        after,
        skip,
        pltpu.with_memory_space_constraint(sums, pltpu.VMEM),
        *(in_hbm(part) for part in (b, c, x, gate, weight)),
    )


def output_kernel(
    state_ref, c_ref, gain_ref, held_ref, local_hbm, factor_hbm, weight_hbm, out_ref,
    local_ref, factor_ref, weight_ref, normed_scr, row_sems, weight_sem,
):
    width = 256
    half_rows = TOKENS_PER_BLOCK // 2
    shape = (width, width)
    copies = []
    for k in range(2):
        rows = pl.ds(k * half_rows, half_rows)
        group = [
            pltpu.make_async_copy(source.at[rows, :], target.at[rows, :], row_sems.at[k, i])
            for i, (source, target) in enumerate(
                ((local_hbm, local_ref), (factor_hbm, factor_ref))
            )
        ]
        for copy in group:
            copy.start()
        copies.append(group)
    rest = out_ref.shape[1] - HELD
    weight_copy = pltpu.make_async_copy(
        weight_hbm.at[:, pl.ds(HELD, rest)], weight_ref, weight_sem
    )
    weight_copy.start()
    same = (
        lax.broadcasted_iota(jnp.int32, shape, 0) // HEAD
        == lax.broadcasted_iota(jnp.int32, shape, 1) // HEAD
    )
    mean_of = jnp.where(same, 1.0 / HEAD, 0.0).astype(BF)
    for k in range(2):
        for copy in copies[k]:
            copy.wait()
        rows = slice(k * half_rows, (k + 1) * half_rows)
        c = c_ref[rows, :]
        for j in range(DI // width):
            columns = slice(j * width, (j + 1) * width)
            carried = dot(c, state_ref[columns, :], (1, 1))
            gated = local_ref[rows, columns].astype(F32) + factor_ref[rows, columns] * carried
            mean = dot((gated * gated).astype(BF), mean_of)
            normed = gated * (lax.rsqrt(mean + EPS) * gain_ref[:, columns])
            normed_scr[rows, columns] = normed.astype(BF)
    for j in range(HELD // width):
        columns = slice(j * width, (j + 1) * width)
        out_ref[:, columns] = dot(normed_scr[...], held_ref[:, columns]).astype(BF)
    weight_copy.wait()
    for j in range(rest // width):
        columns = slice(j * width, (j + 1) * width)
        made = dot(normed_scr[...], weight_ref[:, columns])
        out_ref[:, HELD + j * width : HELD + (j + 1) * width] = made.astype(BF)


def projected_tokens(state, c, gain, weight, local, factor, held):
    width_out = weight.shape[1]
    vmem, anywhere = pl.BlockSpec(memory_space=pltpu.VMEM), pl.BlockSpec(memory_space=pl.ANY)
    held = pltpu.with_memory_space_constraint(held, pltpu.VMEM)
    return pl.pallas_call(
        output_kernel,
        in_specs=[vmem] * 4 + [anywhere] * 3,
        out_specs=vmem,
        out_shape=jax.ShapeDtypeStruct((TOKENS_PER_BLOCK, width_out), BF),
        scratch_shapes=[
            pltpu.VMEM((TOKENS_PER_BLOCK, DI), BF),
            pltpu.VMEM((TOKENS_PER_BLOCK, DI), BF),
            pltpu.VMEM((DI, width_out - HELD), BF),
            pltpu.VMEM((TOKENS_PER_BLOCK, DI), BF),
            pltpu.SemaphoreType.DMA((2, 2)),
            pltpu.SemaphoreType.DMA,
        ],
        compiler_params=pltpu.CompilerParams(vmem_limit_bytes=28 * MIB),
        cost_estimate=pl.CostEstimate(
            flops=4 * 10**9, bytes_accessed=12 * MIB, transcendentals=10**6
        ),
        name="projected_tokens",
    )(state, c, gain, held, in_hbm(local), in_hbm(factor), in_hbm(weight))


def tile_kernel(order_ref, in_ref, out_ref, sems):
    order = order_ref[...]
    copies = []
    for k in range(TOKENS_PER_BLOCK // TILE):
        source = in_ref.at[pl.ds(pl.multiple_of(order[0, k] * TILE, TILE), TILE), :]
        target = out_ref.at[pl.ds(k * TILE, TILE), :]
        copies.append(pltpu.make_async_copy(source, target, sems.at[k]))
    for copy in copies:
        copy.start()
    for copy in copies:
        copy.wait()


def chosen_tiles(order, arrived):
    return pl.pallas_call(
        tile_kernel,
        in_specs=[pl.BlockSpec(memory_space=pltpu.VMEM), pl.BlockSpec(memory_space=pl.ANY)],
        out_specs=pl.BlockSpec(memory_space=pl.ANY),
        out_shape=jax.ShapeDtypeStruct(arrived.shape, arrived.dtype),
        scratch_shapes=[pltpu.SemaphoreType.DMA((TOKENS_PER_BLOCK // TILE,))],
        compiler_params=pltpu.CompilerParams(vmem_limit_bytes=MIB),
        cost_estimate=pl.CostEstimate(flops=0, bytes_accessed=3 * MIB, transcendentals=0),
        name="chosen_tiles",
    )(order, arrived)


def swapped(x, axes):
    return lax.all_to_all(x, axes, split_axis=0, concat_axis=0, tiled=True)


def shards(
    ssd_input,
    gate_input,
    b_matrix,
    c_matrix,
    log_decay,
    d_skip,
    norm_gain,
    out_weight,
    view_order,
    tile_order,
):
    bands = lax.axis_size(SEQ)
    width_out = out_weight.shape[1]
    x, gate, b, c = (part[0, 0] for part in (ssd_input, gate_input, b_matrix, c_matrix))
    logs = log_decay[0, 0]
    states, sums = block_states(view_order, logs, b, x)
    states = swapped(states, PLANE)
    totals = swapped(plane_totals(states, lax.axis_size("z")), "z")
    entering = swapped(entering_states(states, totals), PLANE).reshape(DI, N)
    local, factor, held = local_part(
        totals, d_skip.reshape(1, H), sums, b, c, x, gate, out_weight
    )
    projected = projected_tokens(
        entering, c, norm_gain.reshape(1, DI), out_weight, local, factor, held
    )
    arrived = swapped(projected.reshape(bands, TOKENS_PER_BLOCK // bands, width_out), SEQ)
    chosen = chosen_tiles(tile_order, arrived.reshape(TOKENS_PER_BLOCK, width_out))
    return chosen.reshape(1, 1, TOKENS_PER_BLOCK, width_out)


def solution(mesh):
    split = Mesh(mesh.devices.reshape(8, 4, 2, mesh.shape["view"]), (*SEQ, "view"))
    whole = P(SEQ, "view", None, None)
    in_specs = (whole,) * 5 + (P(),) * 3 + (P(SEQ, None),) * 2
    return jax.shard_map(shards, mesh=split, in_specs=in_specs, out_specs=whole, check_vma=False)
```

```python
import functools

import jax
import jax.numpy as jnp
from jax import lax
from jax.experimental import pallas as pl
from jax.experimental.pallas import tpu as pltpu
from jax.sharding import Mesh
from jax.sharding import PartitionSpec as P

H = 32
HEAD = 64
N = 128
TILE = 128
TOKENS_PER_BLOCK = 512
DI = H * HEAD
CHUNK = 128
CHUNKS = TOKENS_PER_BLOCK // CHUNK
COLS = 1024
EPS = 1e-05
SEQ = ("z", "y", "core")
PLANE = ("y", "core", "view")
SUB = 8
PARTS = HEAD // SUB
MESSAGE = (PARTS + 1, SUB, N)
HELD = 512
BF = jnp.bfloat16
F32 = jnp.float32
MIB = 2**20


def dot(a, b, contract=(1, 0)):
    return lax.dot_general(
        a, b, (((contract[0],), (contract[1],)), ((), ())), preferred_element_type=F32
    )


def three_terms(x):
    hi = x.astype(BF).astype(F32)
    rest = x - hi
    mid = rest.astype(BF).astype(F32)
    return hi, mid, rest - mid


def chunk_sums(logs):
    shape = (CHUNK, CHUNK)
    row = lax.broadcasted_iota(jnp.int32, shape, 0)
    column = lax.broadcasted_iota(jnp.int32, shape, 1)
    upto = jnp.where(column <= row, 1.0, 0.0).astype(BF)
    parts = [part.astype(BF) for part in three_terms(logs)]
    return [
        sum(dot(upto, part[:, k * CHUNK : (k + 1) * CHUNK], (1, 1)) for part in parts)
        for k in range(CHUNKS)
    ]


def halves(x):
    hi = x.astype(BF).astype(F32)
    lane = lax.broadcasted_iota(jnp.int32, x.shape, x.ndim - 1)
    return jnp.where(lane < H, hi, x - hi).astype(BF)


def in_hbm(x):
    return pltpu.with_memory_space_constraint(x, pltpu.HBM)


def spread(first_head, columns, copies=2):
    shape = (copies * H, columns)
    head = lax.broadcasted_iota(jnp.int32, shape, 0) % H
    column = lax.broadcasted_iota(jnp.int32, shape, 1) // HEAD + first_head
    return jnp.where(head == column, 1.0, 0.0).astype(BF)


def column_copies(source, target, sems):
    return [
        pltpu.make_async_copy(
            source.at[:, pl.ds(k * COLS, COLS)], target.at[:, pl.ds(k * COLS, COLS)], sems.at[k]
        )
        for k in range(DI // COLS)
    ]


def state_kernel(
    order_hbm, log_hbm, b_hbm, x_hbm, out_ref, sums_ref,
    order_scr, logs_scr, b_scr, x_scr, sems, x_sems,
):
    order_copy = pltpu.make_async_copy(order_hbm, order_scr, sems.at[2])
    log_copy = pltpu.make_async_copy(log_hbm, logs_scr, sems.at[0])
    b_copy = pltpu.make_async_copy(b_hbm, b_scr, sems.at[1])
    x_copies = column_copies(x_hbm, x_scr, x_sems)
    for copy in (log_copy, order_copy, b_copy, *x_copies):
        copy.start()
    log_copy.wait()
    logs = logs_scr[...]
    sums = chunk_sums(jnp.concatenate([logs, logs], axis=0))
    later = jnp.zeros((1, 2 * H), F32)
    weights = []
    for k in reversed(range(CHUNKS)):
        sums_ref[k * CHUNK : (k + 1) * CHUNK, :] = sums[k]
        end = sums[k][CHUNK - 1 : CHUNK]
        weights.insert(0, halves(jnp.exp(end - sums[k] + later)))
        later = later + end
    weights = jnp.concatenate(weights, axis=0)

    order_copy.wait()
    order = order_scr[...]
    turn = lax.broadcasted_iota(jnp.int32, order.shape, 1)
    found = jnp.where(order == lax.axis_index("view"), turn, 0)
    rank = jnp.sum(found.astype(F32), axis=1, keepdims=True)[None]
    decay = jnp.broadcast_to(jnp.exp(jnp.sum(logs, axis=1, keepdims=True)), (H, N))
    hi, mid, lo = (part[:, None, :] for part in three_terms(decay))
    place = lax.broadcasted_iota(jnp.int32, (H, SUB, N), 1)
    tail = jnp.where(place == 0, hi, jnp.where(place == 1, mid, jnp.where(place == 2, lo, 0.0)))
    tail = jnp.where(place == 3, rank, tail)
    out_ref[:, PARTS] = tail.astype(BF)

    b_copy.wait()
    b_rows = b_scr[...].astype(F32).T.astype(BF)
    heads = COLS // HEAD
    for k, copy in enumerate(x_copies):
        copy.wait()
        x = x_scr[:, k * COLS : (k + 1) * COLS].astype(F32)
        scaled = (x * dot(weights, spread(k * heads, COLS))).astype(BF)
        state = dot(b_rows, scaled).T.reshape(heads, PARTS, SUB, N)
        out_ref[k * heads : (k + 1) * heads, 0:PARTS] = state.astype(BF)


def block_states(order, logs, b, x):
    anywhere = pl.BlockSpec(memory_space=pl.ANY)
    return pl.pallas_call(
        state_kernel,
        in_specs=[anywhere] * 4,
        out_specs=[pl.BlockSpec(), pl.BlockSpec(memory_space=pltpu.VMEM)],
        out_shape=[
            jax.ShapeDtypeStruct((H, *MESSAGE), BF),
            pltpu.VMEM((TOKENS_PER_BLOCK, 2 * H), F32),
        ],
        scratch_shapes=[
            pltpu.VMEM(order.shape, order.dtype),
            pltpu.VMEM(logs.shape, F32),
            pltpu.VMEM(b.shape, BF),
            pltpu.VMEM(x.shape, BF),
            pltpu.SemaphoreType.DMA((3,)),
            pltpu.SemaphoreType.DMA((DI // COLS,)),
        ],
        compiler_params=pltpu.CompilerParams(vmem_limit_bytes=16 * MIB),
        cost_estimate=pl.CostEstimate(flops=2 * 10**9, bytes_accessed=3 * MIB, transcendentals=0),
        name="block_states",
    )(*(in_hbm(part) for part in (order, logs, b, x)))


def read_tail(ref, at):
    tail = ref[at, PARTS].astype(F32)
    return tail[0:1] + tail[1:2] + tail[2:3], tail[3:4]


def read_state(ref, at):
    return ref[at, 0:PARTS].astype(F32).reshape(HEAD, N)


def scan_plane(ref, running, emit):
    views = 4
    product = jnp.ones((1, N), F32)
    for band in range(ref.shape[0] // views):
        blocks = [band * views + v for v in range(views)]
        states = [read_state(ref, k) for k in blocks]
        decays, ranks = zip(*(read_tail(ref, k) for k in blocks))
        entering = [None] * views
        for place in range(views):
            chosen, decay = states[0], decays[0]
            for v in range(views):
                here = ranks[v] == float(place)
                entering[v] = running if place == 0 else jnp.where(here, running, entering[v])
                if v:
                    chosen = jnp.where(here, states[v], chosen)
                    decay = jnp.where(here, decays[v], decay)
            running = decay * running + chosen
            product = product * decay
        if emit is not None:
            for v in range(views):
                emit(blocks[v], entering[v])
    return running, product


def total_kernel(in_ref, token_ref, out_ref):
    total, product = scan_plane(in_ref, jnp.zeros((HEAD, N), F32), None)
    hi, mid, lo = three_terms(product)
    place = lax.broadcasted_iota(jnp.int32, (SUB, N), 0)
    tail = jnp.where(place == 0, hi, jnp.where(place == 1, mid, jnp.where(place == 2, lo, 0.0)))
    for k in range(out_ref.shape[0]):
        out_ref[k, 0:PARTS] = total.reshape(PARTS, SUB, N).astype(BF)
        out_ref[k, PARTS] = tail.astype(BF)


def plane_totals(states, token, planes):
    return pl.pallas_call(
        total_kernel,
        in_specs=[pl.BlockSpec(memory_space=pltpu.VMEM), pl.BlockSpec(memory_space=pl.ANY)],
        out_shape=jax.ShapeDtypeStruct((planes, *MESSAGE), BF),
        compiler_params=pltpu.CompilerParams(vmem_limit_bytes=8 * MIB),
        cost_estimate=pl.CostEstimate(flops=10**6, bytes_accessed=MIB, transcendentals=0),
        name="plane_totals",
    )(states, in_hbm(token))


def entering_kernel(in_ref, totals_ref, out_ref):
    mine = lax.axis_index("z")
    carry = jnp.zeros((HEAD, N), F32)
    for k in range(totals_ref.shape[0] - 1):
        decay, _ = read_tail(totals_ref, k)
        later = decay * carry + read_state(totals_ref, k)
        carry = jnp.where(k < mine, later, carry)

    def emit(block, value):
        out_ref[block, :, :] = value.astype(BF)

    scan_plane(in_ref, carry, emit)


def entering_states(states, totals):
    return pl.pallas_call(
        entering_kernel,
        out_shape=jax.ShapeDtypeStruct((states.shape[0], HEAD, N), BF),
        compiler_params=pltpu.CompilerParams(vmem_limit_bytes=8 * MIB),
        cost_estimate=pl.CostEstimate(flops=10**6, bytes_accessed=2 * MIB, transcendentals=0),
        name="entering_states",
    )(states, totals)


def local_kernel(
    skip_ref, sums_ref, b_hbm, c_hbm, x_hbm, gate_hbm, weight_hbm,
    local_hbm, factor_hbm, held_ref,
    b_scr, c_scr, x_scr, gate_scr, local_scr, factor_scr, row_scr,
    sems, x_sems, gate_sems, local_sems, factor_sems,
):
    b_copy = pltpu.make_async_copy(b_hbm, b_scr, sems.at[1])
    c_copy = pltpu.make_async_copy(c_hbm, c_scr, sems.at[2])
    held_copy = pltpu.make_async_copy(weight_hbm.at[:, pl.ds(0, HELD)], held_ref, sems.at[3])
    x_copies = column_copies(x_hbm, x_scr, x_sems)
    gate_copies = column_copies(gate_hbm, gate_scr, gate_sems)
    local_copies = column_copies(local_scr, local_hbm, local_sems)
    factor_copies = column_copies(factor_scr, factor_hbm, factor_sems)
    for copy in (b_copy, c_copy):
        copy.start()
    for pair in zip(x_copies, gate_copies):
        for copy in pair:
            copy.start()
    held_copy.start()

    before = jnp.zeros((1, 2 * H), F32)
    row_scr[...] = jnp.zeros_like(row_scr)
    inward, outward, entered = [], [], []
    for k in range(CHUNKS):
        part = sums_ref[k * CHUNK : (k + 1) * CHUNK, :]
        middle = part[CHUNK // 2 - 1 : CHUNK // 2]
        end = part[CHUNK - 1 : CHUNK]
        inward.append(halves(jnp.exp(middle - part)))
        outward.append(halves(jnp.exp(part - middle)))
        entered.append(halves(jnp.exp(before + part)))
        row_scr[k : k + 1, :] = jnp.exp(end - middle)
        row_scr[4 + k : 5 + k, :] = jnp.exp(middle)
        row_scr[8 + k : 9 + k, :] = jnp.exp(end)
        before = before + end
    ends_once = halves(row_scr[...])
    skips = [part.astype(BF) for part in three_terms(jnp.broadcast_to(skip_ref[...], (16, H)))]

    b_copy.wait()
    c_copy.wait()
    shape = (CHUNK, CHUNK)
    causal = lax.broadcasted_iota(jnp.int32, shape, 1) <= lax.broadcasted_iota(
        jnp.int32, shape, 0
    )
    b_rows, left = [], []
    for k in range(CHUNKS):
        rows = slice(k * CHUNK, (k + 1) * CHUNK)
        b_part, c_part = b_scr[rows, :], c_scr[rows, :]
        b_rows.append(b_part.astype(F32).T.astype(BF))
        scores = jnp.where(causal, dot(c_part, b_part, (1, 1)), 0.0)
        hi = scores.astype(BF)
        lo = (scores - hi.astype(F32)).astype(BF)
        left.append(jnp.concatenate([hi, hi, lo, c_part], axis=1))

    for block in range(DI // COLS):
        columns = slice(block * COLS, (block + 1) * COLS)
        head = block * (COLS // HEAD)
        twice = spread(head, COLS)
        once = spread(head, COLS, 1)
        ends = dot(ends_once, twice)
        skip = sum(dot(part, once) for part in skips)[0:1]
        running = None
        x_copies[block].wait()
        gate_copies[block].wait()
        for k in range(CHUNKS):
            rows = slice(k * CHUNK, (k + 1) * CHUNK)
            x = x_scr[rows, columns].astype(F32)
            exact = x * dot(inward[k], twice)
            scaled = exact.astype(BF)
            right = [scaled, (exact - scaled.astype(F32)).astype(BF), scaled]
            if running is not None:
                right.append((running * ends[4 + k : 5 + k]).astype(BF))
            inner = dot(left[k][:, 0 : CHUNK * len(right)], jnp.concatenate(right, axis=0))
            if k + 1 < CHUNKS:
                made = dot(b_rows[k], scaled) * ends[k : k + 1]
                running = made if running is None else running * ends[8 + k : 9 + k] + made
            half = 0.5 * gate_scr[rows, columns].astype(F32)
            opened = half + half * jnp.tanh(half)
            mixed = inner * dot(outward[k], twice) + skip * x
            local_scr[rows, columns] = (mixed * opened).astype(BF)
            factor_scr[rows, columns] = (dot(entered[k], twice) * opened).astype(BF)
        local_copies[block].start()
        factor_copies[block].start()
    for copy in (held_copy, *local_copies, *factor_copies):
        copy.wait()


def local_part(skip, sums, b, c, x, gate, weight):
    blocks = DI // COLS
    anywhere = pl.BlockSpec(memory_space=pl.ANY)
    return pl.pallas_call(
        local_kernel,
        in_specs=[pl.BlockSpec(memory_space=pltpu.VMEM)] * 2 + [anywhere] * 5,
        out_specs=[anywhere, anywhere, pl.BlockSpec(memory_space=pltpu.VMEM)],
        out_shape=[pltpu.HBM(x.shape, BF), pltpu.HBM(x.shape, BF), pltpu.VMEM((DI, HELD), BF)],
        scratch_shapes=[
            pltpu.VMEM(b.shape, BF),
            pltpu.VMEM(c.shape, BF),
            pltpu.VMEM(x.shape, BF),
            pltpu.VMEM(x.shape, BF),
            pltpu.VMEM(x.shape, BF),
            pltpu.VMEM(x.shape, BF),
            pltpu.VMEM((16, 2 * H), F32),
            pltpu.SemaphoreType.DMA((4,)),
            *[pltpu.SemaphoreType.DMA((blocks,))] * 4,
        ],
        compiler_params=pltpu.CompilerParams(vmem_limit_bytes=32 * MIB),
        cost_estimate=pl.CostEstimate(
            flops=8 * 10**9, bytes_accessed=12 * MIB, transcendentals=10**6
        ),
        name="local_part",
    )(
        skip,
        pltpu.with_memory_space_constraint(sums, pltpu.VMEM),
        *(in_hbm(part) for part in (b, c, x, gate, weight)),
    )


def output_kernel(
    state_ref, c_ref, gain_ref, held_ref, local_hbm, factor_hbm, weight_hbm, out_ref,
    local_ref, factor_ref, weight_ref, normed_scr, row_sems, weight_sem,
):
    width = 256
    half_rows = TOKENS_PER_BLOCK // 2
    shape = (width, width)
    copies = []
    for k in range(2):
        rows = pl.ds(k * half_rows, half_rows)
        group = [
            pltpu.make_async_copy(source.at[rows, :], target.at[rows, :], row_sems.at[k, i])
            for i, (source, target) in enumerate(
                ((local_hbm, local_ref), (factor_hbm, factor_ref))
            )
        ]
        for copy in group:
            copy.start()
        copies.append(group)
    rest = out_ref.shape[1] - HELD
    weight_copy = pltpu.make_async_copy(
        weight_hbm.at[:, pl.ds(HELD, rest)], weight_ref, weight_sem
    )
    weight_copy.start()
    same = (
        lax.broadcasted_iota(jnp.int32, shape, 0) // HEAD
        == lax.broadcasted_iota(jnp.int32, shape, 1) // HEAD
    )
    mean_of = jnp.where(same, 1.0 / HEAD, 0.0).astype(BF)
    for k in range(2):
        for copy in copies[k]:
            copy.wait()
        rows = slice(k * half_rows, (k + 1) * half_rows)
        c = c_ref[rows, :]
        for j in range(DI // width):
            columns = slice(j * width, (j + 1) * width)
            carried = dot(c, state_ref[columns, :], (1, 1))
            gated = local_ref[rows, columns].astype(F32) + factor_ref[rows, columns] * carried
            mean = dot((gated * gated).astype(BF), mean_of)
            normed = gated * (lax.rsqrt(mean + EPS) * gain_ref[:, columns])
            normed_scr[rows, columns] = normed.astype(BF)
    for j in range(HELD // width):
        columns = slice(j * width, (j + 1) * width)
        out_ref[:, columns] = dot(normed_scr[...], held_ref[:, columns]).astype(BF)
    weight_copy.wait()
    for j in range(rest // width):
        columns = slice(j * width, (j + 1) * width)
        made = dot(normed_scr[...], weight_ref[:, columns])
        out_ref[:, HELD + j * width : HELD + (j + 1) * width] = made.astype(BF)


def projected_tokens(state, c, gain, weight, local, factor, held):
    width_out = weight.shape[1]
    vmem, anywhere = pl.BlockSpec(memory_space=pltpu.VMEM), pl.BlockSpec(memory_space=pl.ANY)
    held = pltpu.with_memory_space_constraint(held, pltpu.VMEM)
    return pl.pallas_call(
        output_kernel,
        in_specs=[vmem] * 4 + [anywhere] * 3,
        out_specs=vmem,
        out_shape=jax.ShapeDtypeStruct((TOKENS_PER_BLOCK, width_out), BF),
        scratch_shapes=[
            pltpu.VMEM((TOKENS_PER_BLOCK, DI), BF),
            pltpu.VMEM((TOKENS_PER_BLOCK, DI), BF),
            pltpu.VMEM((DI, width_out - HELD), BF),
            pltpu.VMEM((TOKENS_PER_BLOCK, DI), BF),
            pltpu.SemaphoreType.DMA((2, 2)),
            pltpu.SemaphoreType.DMA,
        ],
        compiler_params=pltpu.CompilerParams(vmem_limit_bytes=28 * MIB),
        cost_estimate=pl.CostEstimate(
            flops=4 * 10**9, bytes_accessed=12 * MIB, transcendentals=10**6
        ),
        name="projected_tokens",
    )(state, c, gain, held, in_hbm(local), in_hbm(factor), in_hbm(weight))


def tile_kernel(order_ref, in_ref, out_ref, sems):
    order = order_ref[...]
    copies = []
    for k in range(TOKENS_PER_BLOCK // TILE):
        source = in_ref.at[pl.ds(pl.multiple_of(order[0, k] * TILE, TILE), TILE), :]
        target = out_ref.at[pl.ds(k * TILE, TILE), :]
        copies.append(pltpu.make_async_copy(source, target, sems.at[k]))
    for copy in copies:
        copy.start()
    for copy in copies:
        copy.wait()


def chosen_tiles(order, arrived):
    return pl.pallas_call(
        tile_kernel,
        in_specs=[pl.BlockSpec(memory_space=pltpu.VMEM), pl.BlockSpec(memory_space=pl.ANY)],
        out_specs=pl.BlockSpec(memory_space=pl.ANY),
        out_shape=jax.ShapeDtypeStruct(arrived.shape, arrived.dtype),
        scratch_shapes=[pltpu.SemaphoreType.DMA((TOKENS_PER_BLOCK // TILE,))],
        compiler_params=pltpu.CompilerParams(vmem_limit_bytes=MIB),
        cost_estimate=pl.CostEstimate(flops=0, bytes_accessed=3 * MIB, transcendentals=0),
        name="chosen_tiles",
    )(order, arrived)


def swapped(x, axes):
    return lax.all_to_all(x, axes, split_axis=0, concat_axis=0, tiled=True)


def shards(
    ssd_input,
    gate_input,
    b_matrix,
    c_matrix,
    log_decay,
    d_skip,
    norm_gain,
    out_weight,
    view_order,
    tile_order,
):
    bands = lax.axis_size(SEQ)
    width_out = out_weight.shape[1]
    x, gate, b, c = (part[0, 0] for part in (ssd_input, gate_input, b_matrix, c_matrix))
    logs = log_decay[0, 0]
    states, sums = block_states(view_order, logs, b, x)
    states = swapped(states, PLANE)
    local, factor, held = local_part(d_skip.reshape(1, H), sums, b, c, x, gate, out_weight)
    totals = swapped(plane_totals(states, local, lax.axis_size("z")), "z")
    entering = swapped(entering_states(states, totals), PLANE).reshape(DI, N)
    projected = projected_tokens(
        entering, c, norm_gain.reshape(1, DI), out_weight, local, factor, held
    )
    arrived = swapped(projected.reshape(bands, TOKENS_PER_BLOCK // bands, width_out), SEQ)
    chosen = chosen_tiles(tile_order, arrived.reshape(TOKENS_PER_BLOCK, width_out))
    return chosen.reshape(1, 1, TOKENS_PER_BLOCK, width_out)


def solution(mesh):
    split = Mesh(mesh.devices.reshape(8, 4, 2, mesh.shape["view"]), (*SEQ, "view"))
    whole = P(SEQ, "view", None, None)
    in_specs = (whole,) * 5 + (P(),) * 3 + (P(SEQ, None),) * 2
    return jax.shard_map(shards, mesh=split, in_specs=in_specs, out_specs=whole, check_vma=False)
```
